128 devices in a mesh: dp: 4 (over y_hi, core), tok: 32 (over y_lo, z, x).
Axes of the slice: x: 4, y: 4 (y_hi: 2, y_lo: 2; y = y_hi * 2 + y_lo), z: 4, core: 2. Of those that a mesh axis runs over, the one named last changes fastest.
Arguments:
- attn_float: bfloat16 [8192, 8192], P(('dp', 'tok')), may hold values from -6 to 6
- attn_quant: bfloat16 [8192, 8192], P(('dp', 'tok')), may hold values from -6 to 6
- proj_weight: bfloat16 [8192, 4096], P('tok'), may hold values from -0.0625 to 0.0625
- weight_codes: int32 [8192, 4096], P('tok'), may hold values from 0 to 15
- group_scales: float32 [64, 4096], P('tok'), may hold values from 0.0012 to 0.005
Outputs:
- float_out: bfloat16 [8192, 4096], P(('dp', 'tok'))
- quant_out: bfloat16 [8192, 4096], P(('dp', 'tok'))
- hessian_cols: float32 [8192, 128], P('tok')
- cross_cols: float32 [8192, 128], P('tok')
The draws below stay inside these ranges and needn't reach their ends.
All inputs are finite; a program needn't handle non-finite values.
Results may differ from the reference program's by a relative error of at most 0.0049.
Values may be sent and summed in bfloat16 or wider, within the bound.
No kernel may reach another device: no remote copies, remote signals or barrier semaphores. Data moves between devices by JAX's collectives and lax.ppermute only.
A program may use at most 320 MiB of HBM per device.

```python
import math
import jax
import jax.numpy as jnp

D_IN = 8192
D_OUT = 4096
GROUP = 128
BLOCK = 128
TOKENS = 8192


def touch_ends(drawn, own_key, low, high):
    index_at = [jax.random.randint(jax.random.fold_in(own_key, axis), (), 0, length) for axis, length in enumerate(drawn.shape)]
    main_axis = drawn.shape.index(max(drawn.shape))
    beside = index_at[:main_axis] + [(index_at[main_axis] + 1) % drawn.shape[main_axis]] + index_at[main_axis + 1:]
    return drawn.at[tuple(index_at)].set(low).at[tuple(beside)].set(high)


def block_levels(stream_key, extent, cuts, low, largest):
    level, own = 1.0, jax.random.fold_in(stream_key, 6)
    for dim, parts in cuts:
        steps = jnp.exp(jax.random.uniform(jax.random.fold_in(own, dim), (parts,), jnp.float32, low / len(cuts), largest / len(cuts)))
        level = level * jnp.repeat(steps, extent[dim] // parts).reshape([-1 if axis == dim else 1 for axis in range(len(extent))])
    return level


def normal_values(own_key, extent, scale, limit, shards=(), dtype=jnp.bfloat16):
    level = block_levels(own_key, extent, shards, -0.22, 0.18) if shards else 1.0
    entries = jax.random.normal(own_key, extent, jnp.float32) * scale * level
    return jnp.minimum(jnp.maximum(entries, -limit), limit).astype(dtype)


def setup_inputs(seed: int = 0) -> dict:
    streams_of = jax.random.split(jax.random.key(seed), 6)
    return {
        "attn_float": normal_values(streams_of[0], (TOKENS, D_IN), 1.0, 6.0, ((0, 128),)),
        "attn_quant": normal_values(streams_of[1], (TOKENS, D_IN), 1.0, 6.0, ((0, 128),)),
        "proj_weight": normal_values(streams_of[2], (D_IN, D_OUT), D_IN ** -0.5, 0.0625, ((0, 32),)),
        "weight_codes": touch_ends(jax.random.randint(streams_of[3], (D_IN, D_OUT), 0, 16), jax.random.fold_in(streams_of[3], 1), 0, 15).astype(jnp.int32),
        "group_scales": jnp.clip(jnp.exp(math.log(0.005) - 1.4271163 * jax.random.uniform(streams_of[4], (D_IN // GROUP, D_OUT), jnp.float32) ** block_levels(streams_of[4], (D_IN // GROUP, D_OUT), ((0, 32),), -0.2, 0.2)), 0.0012, 0.005),
    }


def dequantize(weight_codes, group_scales):
    groups = group_scales.shape[0]
    values = (weight_codes - 8).astype(jnp.float32).reshape(groups, GROUP, D_OUT)
    return (values * group_scales[:, None, :]).reshape(D_IN, D_OUT).astype(jnp.bfloat16)


def reference(attn_float, attn_quant, proj_weight, weight_codes, group_scales):
    quant_weight = dequantize(weight_codes, group_scales)
    shift = (attn_float.astype(jnp.float32) - attn_quant.astype(jnp.float32)).astype(jnp.bfloat16)
    hessian_cols = jnp.dot(attn_quant.T, attn_quant[:, :BLOCK], preferred_element_type=jnp.float32) / TOKENS
    cross_cols = jnp.dot(attn_quant.T, shift[:, :BLOCK], preferred_element_type=jnp.float32) / TOKENS
    float_out = jnp.dot(attn_float, proj_weight, preferred_element_type=jnp.float32).astype(jnp.bfloat16)
    quant_out = jnp.dot(attn_quant, quant_weight, preferred_element_type=jnp.float32).astype(jnp.bfloat16)
    return float_out, quant_out, hessian_cols, cross_cols
```

```python
import jax
import jax.numpy as jnp
from jax import lax
from jax.experimental import pallas as pl
from jax.experimental.pallas import tpu as pltpu
from jax.sharding import Mesh
from jax.sharding import PartitionSpec as P

BLOCK = 128
FINE = ("yh", "core", "yl", "z", "x")
PLANE = ("yh", "yl", "x")
F32 = jnp.float32
BF16 = jnp.bfloat16


def params():
    return pltpu.CompilerParams(vmem_limit_bytes=40 << 20)


def pack_kernel(z_ref, float_ref, quant_ref, out_ref, block_ref):
    width = out_ref.shape[2] // 8
    z = z_ref[0]
    for kind, ref in enumerate((float_ref, quant_ref)):
        for j in range(4):
            zj = lax.rem(z + j, 4)
            for yl in range(2):
                for x in range(4):
                    start = pl.multiple_of(((yl * 4 + zj) * 4 + x) * width, width)
                    block = ref[:, pl.ds(start, width)]
                    for half in range(2):
                        at = (j * 2 + (yl ^ half)) * width
                        out_ref[kind * 8 + half * 4 + x, :, at : at + width] = block
    quant = quant_ref[:, :BLOCK]
    shift = (float_ref[:, :BLOCK].astype(F32) - quant.astype(F32)).astype(BF16)
    for d in range(16):
        block_ref[d, :, :BLOCK] = quant
        block_ref[d, :, BLOCK:] = shift


def pack(z, attn_float, attn_quant):
    tokens, d_in = attn_float.shape
    whole = pl.BlockSpec(memory_space=pltpu.VMEM)
    return pl.pallas_call(
        pack_kernel,
        out_shape=(
            jax.ShapeDtypeStruct((16, tokens, d_in // 4), BF16),
            jax.ShapeDtypeStruct((16, tokens, 2 * BLOCK), BF16),
        ),
        in_specs=[pl.BlockSpec(memory_space=pltpu.SMEM), whole, whole],
        out_specs=(whole, whole),
        compiler_params=params(),
        name="pack",
    )(z.reshape(1), attn_float, attn_quant)


def finish_kernel(core_ref, first_ref, second_ref, float_ref, quant_ref):
    core = core_ref[0]
    width = first_ref.shape[2]
    for n, ref in enumerate((first_ref, second_ref)):
        quarter = core if n == 0 else 1 - core
        for kind, out in enumerate((float_ref, quant_ref)):
            for half in range(2):
                at = kind * 8 + half * 4
                total = ref[at].astype(F32)
                for x in range(1, 4):
                    total += ref[at + x].astype(F32)
                start = pl.multiple_of((half * 2 + quarter) * width, width)
                out[:, pl.ds(start, width)] = total.astype(BF16)


def finish(core, first, second):
    _, tokens, width = first.shape
    whole = pl.BlockSpec(memory_space=pltpu.VMEM)
    return pl.pallas_call(
        finish_kernel,
        out_shape=(jax.ShapeDtypeStruct((tokens, 4 * width), BF16),) * 2,
        in_specs=[pl.BlockSpec(memory_space=pltpu.SMEM), whole, whole],
        out_specs=(whole, whole),
        compiler_params=params(),
        name="finish",
    )(core.reshape(1), first, second)


def swap(a, axis):
    return lax.ppermute(a, axis, [(0, 1), (1, 0)])


def shards(attn_float, attn_quant, proj_weight, weight_codes, group_scales):
    tokens, d_in = attn_float.shape
    features, d_out = proj_weight.shape
    groups = group_scales.shape[0]
    half, quarter = d_out // 2, d_out // 4
    inverse = 1.0 / (tokens * 128)
    yh, core, yl, z = (lax.axis_index(a) for a in ("yh", "core", "yl", "z"))

    def weight(kind, col):
        plain = lax.dynamic_slice_in_dim(proj_weight, col, quarter, 1)
        codes = lax.dynamic_slice_in_dim(weight_codes, col, quarter, 1)
        scales = lax.dynamic_slice_in_dim(group_scales, col, quarter, 1)
        values = (codes - 8).astype(F32).reshape(groups, features // groups, quarter)
        quant = (values * scales[:, None, :]).reshape(features, quarter).astype(BF16)
        return jnp.where(kind == 0, plain, quant)

    own = weight(yh, yl * half + core * quarter)
    send = weight(yh ^ core, (1 - yl) * half + core * quarter)
    pairs = []
    for a in range(2):
        for c in range(2):
            for b in range(2):
                pairs.append((a * 4 + c * 2 + b, (a ^ c) * 4 + c * 2 + (1 - b)))
    got = lax.ppermute(send, ("yh", "core", "yl"), pairs)

    payload, block_part = pack(z, attn_float, attn_quant)
    block_all = lax.all_to_all(block_part, PLANE, 0, 0, tiled=True)
    block_all = block_all.reshape(16 * tokens, 2 * BLOCK)

    rows = jnp.concatenate([own, got], axis=0)
    parts = [rows] + [
        lax.ppermute(rows, "z", [((i + j) % 4, i) for i in range(4)]) for j in (1, 2, 3)
    ]
    mine = jnp.concatenate(parts, axis=0)
    other = swap(mine, "core")

    acts = lax.all_to_all(payload, PLANE, 0, 0, tiled=True).reshape(16 * tokens, 8 * features)

    def part(w):
        p = jnp.dot(acts, w, preferred_element_type=F32).astype(BF16)
        return lax.all_to_all(p.reshape(16, tokens, quarter), PLANE, 0, 0, tiled=True)

    float_out, quant_out = finish(core, part(mine), part(other))

    def stats(j):
        picked = acts[:, 2 * j * features : (2 * j + 1) * features]
        return lax.dot_general(
            picked, block_all, (((0,), (0,)), ((), ())), preferred_element_type=F32
        )

    total = stats(0)
    for j in (1, 2, 3):
        total = total + lax.ppermute(
            stats(j).astype(BF16), "z", [(i, (i + j) % 4) for i in range(4)]
        ).astype(F32)
    total = jnp.where(yh == 1, total, swap(total, "yh"))
    total = (total + swap(total, "core")) * inverse
    return float_out, quant_out, total[:, :BLOCK], total[:, BLOCK:]


def solution(mesh):
    fine = Mesh(mesh.devices.reshape(2, 2, 2, 4, 4), FINE)
    rows, tok = P(FINE, None), P(("yl", "z", "x"), None)
    return jax.shard_map(
        shards,
        mesh=fine,
        in_specs=(rows, rows, tok, tok, tok),
        out_specs=(rows, rows, tok, tok),
        check_vma=False,
    )
```

```python
import jax
import jax.numpy as jnp
from jax import lax
from jax.experimental import pallas as pl
from jax.experimental.pallas import tpu as pltpu
from jax.sharding import Mesh
from jax.sharding import PartitionSpec as P

BLOCK = 128
CHUNKS = 4
FINE = ("yh", "core", "yl", "z", "x")
F32 = jnp.float32
BF16 = jnp.bfloat16
WHOLE = pl.BlockSpec(memory_space=pltpu.VMEM)
SCALAR = pl.BlockSpec(memory_space=pltpu.SMEM)
LEFT = pl.BlockSpec(memory_space=pl.ANY)


def params():
    return pltpu.CompilerParams(vmem_limit_bytes=40 << 20)


def pack_kernel(at_ref, float_ref, quant_ref, out_ref):
    width = float_ref.shape[1] // 32
    yl, z = at_ref[0], at_ref[1]
    quant = quant_ref[:, :BLOCK]
    shift = (float_ref[:, :BLOCK].astype(F32) - quant.astype(F32)).astype(BF16)
    for kind, ref in enumerate((float_ref, quant_ref)):
        for x in range(4):
            for j in range(4):
                for r in range(2):
                    block = ((yl ^ r) * 4 + lax.rem(z + j, 4)) * 4 + x
                    start = pl.multiple_of(block * width, width)
                    at = (j * 2 + r) * width
                    out_ref[kind * 4 + x, :, at : at + width] = ref[:, pl.ds(start, width)]
            out_ref[kind * 4 + x, :, 8 * width : 8 * width + BLOCK] = quant
            out_ref[kind * 4 + x, :, 8 * width + BLOCK :] = shift


def pack(at, attn_float, attn_quant):
    tokens, d_in = attn_float.shape
    return pl.pallas_call(
        pack_kernel,
        out_shape=jax.ShapeDtypeStruct((8, tokens, d_in // 4 + 2 * BLOCK), BF16),
        in_specs=[SCALAR, WHOLE, WHOLE],
        out_specs=WHOLE,
        compiler_params=params(),
        name="pack",
    )(at, attn_float, attn_quant)


def join_kernel(*refs):
    own_ref, got_ref, out_ref = refs[0], refs[1], refs[-1]
    n = own_ref.shape[0]
    out_ref[:n] = own_ref[...]
    out_ref[n:] = got_ref[...]


def join(own, got, after):
    n, m = own.shape
    return pl.pallas_call(
        join_kernel,
        out_shape=jax.ShapeDtypeStruct((2 * n, m), BF16),
        in_specs=[WHOLE, WHOLE] + [LEFT] * len(after),
        out_specs=WHOLE,
        compiler_params=params(),
        name="join",
    )(own, got, *after)


def project_kernel(core_ref, mine_ref, other_ref, *refs):
    *parts, out_ref = refs
    core = core_ref[0]
    rows = out_ref.shape[2]
    for n, acts in enumerate((mine_ref, other_ref)):
        where = core if n == 0 else 1 - core
        for yh in range(2):
            total, at = None, 0
            for part in parts:
                depth = part.shape[0]
                term = jnp.dot(
                    acts[yh * rows : (yh + 1) * rows, at : at + depth],
                    part[...],
                    preferred_element_type=F32,
                )
                total = term if total is None else total + term
                at += depth
            out_ref[yh, where] = total.astype(BF16)


def project(core, mine, other, parts):
    rows, cols = mine.shape[0] // 2, parts[0].shape[1]
    return pl.pallas_call(
        project_kernel,
        out_shape=jax.ShapeDtypeStruct((2, 2, rows, cols), BF16),
        in_specs=[SCALAR] + [WHOLE] * (2 + len(parts)),
        out_specs=WHOLE,
        compiler_params=params(),
        cost_estimate=pl.CostEstimate(
            flops=8 * rows * cols * 2048, bytes_accessed=8 << 20, transcendentals=0
        ),
        name="project",
    )(core.reshape(1), mine, other, *parts)


def finish_kernel(*refs):
    *parts, float_ref, quant_ref = refs
    width = parts[0].shape[2]
    for c, ref in enumerate(parts):
        for kind, out in enumerate((float_ref, quant_ref)):
            for half in range(2):
                at = kind * 8 + half * 4
                total = ref[at].astype(F32)
                for x in range(1, 4):
                    total += ref[at + x].astype(F32)
                start = (half * len(parts) + c) * width
                out[:, start : start + width] = total.astype(BF16)


def finish(parts):
    _, tokens, width = parts[0].shape
    return pl.pallas_call(
        finish_kernel,
        out_shape=(jax.ShapeDtypeStruct((tokens, 2 * len(parts) * width), BF16),) * 2,
        in_specs=[WHOLE] * len(parts),
        out_specs=(WHOLE, WHOLE),
        compiler_params=params(),
        name="finish",
    )(*parts)


def swap(a, axis):
    return lax.ppermute(a, axis, [(0, 1), (1, 0)])


def from_z(a, j):
    return lax.ppermute(a, "z", [((i + j) % 4, i) for i in range(4)])


def shards(attn_float, attn_quant, proj_weight, weight_codes, group_scales):
    tokens, d_in = attn_float.shape
    features, d_out = proj_weight.shape
    groups = group_scales.shape[0]
    half, width = d_out // 2, d_out // 2 // CHUNKS
    inverse = 1.0 / (tokens * 128)
    yh, core, yl, z = (lax.axis_index(a) for a in ("yh", "core", "yl", "z"))

    payload = pack(jnp.stack([yl, z]), attn_float, attn_quant)
    mine = lax.all_to_all(payload, ("yh", "x"), 0, 0, tiled=True)
    mine = mine.reshape(8 * tokens, 8 * features + 2 * BLOCK)
    other = swap(mine, "core")

    def weight(kind, col, n):
        plain = lax.dynamic_slice_in_dim(proj_weight, col, n, 1)
        codes = lax.dynamic_slice_in_dim(weight_codes, col, n, 1)
        scales = lax.dynamic_slice_in_dim(group_scales, col, n, 1)
        values = (codes - 8).astype(F32).reshape(groups, features // groups, n)
        quant = (values * scales[:, None, :]).reshape(features, n).astype(BF16)
        return jnp.where(kind == 0, plain, quant)

    pairs = []
    for a in range(2):
        for c in range(2):
            for b in range(2):
                pairs.append((a * 4 + c * 2 + b, (a ^ c) * 4 + c * 2 + (1 - b)))
    own, got = [], []
    for first, n in ((0, width), (width, half - width)):
        col = core * half + first
        mine_w, send_w = weight(yh, col, n), weight(yh ^ core, col, n)
        got_w = lax.ppermute(send_w, ("yh", "core", "yl"), pairs)
        for at in range(0, n, width):
            own.append(mine_w[:, at : at + width])
            got.append(got_w[:, at : at + width])

    after, results = (), []
    for c in range(CHUNKS):
        rows = join(own[c], got[c], after)
        up, down = from_z(rows, 1), from_z(rows, 3)
        after = (up, down)
        far0 = from_z(up[:features], 1)
        far1 = from_z(down[features:], 3)
        partial = project(core, mine, other, (rows, up, far0, far1, down))
        results.append(
            lax.all_to_all(
                partial.reshape(16, tokens, width), ("yh", "core", "x"), 0, 0, tiled=True
            )
        )
    float_out, quant_out = finish(results)

    def stats(j):
        at = 2 * j * features
        total = 0.0
        for acts in (mine, other):
            picked = jnp.where(
                core == 0, acts[:, at : at + features], acts[:, at + features : at + 2 * features]
            )
            total = total + lax.dot_general(
                picked, acts[:, 8 * features :], (((0,), (0,)), ((), ())), preferred_element_type=F32
            )
        return total

    total = 0.0
    for j in range(4):
        pairs = [
            (c * 8 + b * 4 + i, c * 8 + (b ^ c) * 4 + (i + j) % 4)
            for c in range(2)
            for b in range(2)
            for i in range(4)
        ]
        total = total + lax.ppermute(stats(j).astype(BF16), ("core", "yl", "z"), pairs).astype(F32)
    total = (total + swap(total, "core")) * inverse
    total = jnp.where(yh == 1, total, swap(total, "yh"))
    return float_out, quant_out, total[:, :BLOCK], total[:, BLOCK:]


def solution(mesh):
    fine = Mesh(mesh.devices.reshape(2, 2, 2, 4, 4), FINE)
    rows, tok = P(FINE, None), P(("yl", "z", "x"), None)
    return jax.shard_map(
        shards,
        mesh=fine,
        in_specs=(rows, rows, tok, tok, tok),
        out_specs=(rows, rows, tok, tok),
        check_vma=False,
    )
```

```python
import jax
import jax.numpy as jnp
from jax import lax
from jax.experimental import pallas as pl
from jax.experimental.pallas import tpu as pltpu
from jax.sharding import Mesh
from jax.sharding import PartitionSpec as P

BLOCK = 128
WIDTHS = (768, 768, 512)
FINE = ("yh", "core", "yl", "z", "x")
F32 = jnp.float32
BF16 = jnp.bfloat16
WHOLE = pl.BlockSpec(memory_space=pltpu.VMEM)
SCALAR = pl.BlockSpec(memory_space=pltpu.SMEM)
LEFT = pl.BlockSpec(memory_space=pl.ANY)


def params():
    return pltpu.CompilerParams(vmem_limit_bytes=16 << 20)


def pack_kernel(at_ref, float_ref, quant_ref, after_ref, out_ref):
    width = float_ref.shape[1] // 32
    yl, z = at_ref[0], at_ref[1]
    quant = quant_ref[:, :BLOCK]
    shift = (float_ref[:, :BLOCK].astype(F32) - quant.astype(F32)).astype(BF16)
    for kind, ref in enumerate((float_ref, quant_ref)):
        for x in range(4):
            for j in range(4):
                for r in range(2):
                    block = ((yl ^ r) * 4 + lax.rem(z + j, 4)) * 4 + x
                    start = pl.multiple_of(block * width, width)
                    at = (j * 2 + r) * width
                    out_ref[kind * 4 + x, :, at : at + width] = ref[:, pl.ds(start, width)]
            out_ref[kind * 4 + x, :, 8 * width : 8 * width + BLOCK] = quant
            out_ref[kind * 4 + x, :, 8 * width + BLOCK :] = shift


def pack(at, attn_float, attn_quant, after):
    tokens, d_in = attn_float.shape
    return pl.pallas_call(
        pack_kernel,
        out_shape=jax.ShapeDtypeStruct((8, tokens, d_in // 4 + 2 * BLOCK), BF16),
        in_specs=[SCALAR, WHOLE, WHOLE, LEFT],
        out_specs=WHOLE,
        compiler_params=params(),
        name="pack",
    )(at, attn_float, attn_quant, after)


def join_kernel(*refs):
    own_ref, got_ref, out_ref = refs[0], refs[1], refs[-1]
    n = own_ref.shape[0]
    out_ref[:n] = own_ref[...]
    out_ref[n:] = got_ref[...]


def join(own, got, after):
    n, m = own.shape
    return pl.pallas_call(
        join_kernel,
        out_shape=jax.ShapeDtypeStruct((2 * n, m), BF16),
        in_specs=[WHOLE, WHOLE] + [LEFT] * len(after),
        out_specs=WHOLE,
        compiler_params=params(),
        name="join",
    )(own, got, *after)


def project_kernel(core_ref, mine_ref, other_ref, *refs):
    parts, out_ref = refs[:5], refs[-1]
    core = core_ref[0]
    rows = out_ref.shape[2]
    for n, acts in enumerate((mine_ref, other_ref)):
        where = core if n == 0 else 1 - core
        for yh in range(2):
            total, at = None, 0
            for part in parts:
                depth = part.shape[0]
                term = jnp.dot(
                    acts[yh * rows : (yh + 1) * rows, at : at + depth],
                    part[...],
                    preferred_element_type=F32,
                )
                total = term if total is None else total + term
                at += depth
            out_ref[yh, where] = total.astype(BF16)


def project(core, mine, other, parts, after):
    rows, cols = mine.shape[0] // 2, parts[0].shape[1]
    return pl.pallas_call(
        project_kernel,
        out_shape=jax.ShapeDtypeStruct((2, 2, rows, cols), BF16),
        in_specs=[SCALAR] + [WHOLE] * (2 + len(parts)) + [LEFT] * len(after),
        out_specs=WHOLE,
        compiler_params=params(),
        cost_estimate=pl.CostEstimate(
            flops=8 * rows * cols * 2048, bytes_accessed=8 << 20, transcendentals=0
        ),
        name="project",
    )(core.reshape(1), mine, other, *parts, *after)


def finish_kernel(*refs):
    *parts, float_ref, quant_ref = refs
    at_half, start = float_ref.shape[1] // 2, 0
    for ref in parts:
        width = ref.shape[2]
        for kind, out in enumerate((float_ref, quant_ref)):
            for half in range(2):
                at = kind * 8 + half * 4
                total = ref[at].astype(F32)
                for x in range(1, 4):
                    total += ref[at + x].astype(F32)
                col = half * at_half + start
                out[:, col : col + width] = total.astype(BF16)
        start += width


def finish(parts):
    tokens = parts[0].shape[1]
    return pl.pallas_call(
        finish_kernel,
        out_shape=(jax.ShapeDtypeStruct((tokens, 2 * sum(WIDTHS)), BF16),) * 2,
        in_specs=[WHOLE] * len(parts),
        out_specs=(WHOLE, WHOLE),
        compiler_params=params(),
        name="finish",
    )(*parts)


def swap(a, axis):
    return lax.ppermute(a, axis, [(0, 1), (1, 0)])


def from_z(a, j):
    return lax.ppermute(a, "z", [((i + j) % 4, i) for i in range(4)])


def shards(attn_float, attn_quant, proj_weight, weight_codes, group_scales):
    tokens, d_in = attn_float.shape
    features, d_out = proj_weight.shape
    groups = group_scales.shape[0]
    half = d_out // 2
    inverse = 1.0 / (tokens * 128)
    yh, core, yl, z = (lax.axis_index(a) for a in ("yh", "core", "yl", "z"))

    def weight(kind, col, n):
        plain = lax.dynamic_slice_in_dim(proj_weight, col, n, 1)
        codes = lax.dynamic_slice_in_dim(weight_codes, col, n, 1)
        scales = lax.dynamic_slice_in_dim(group_scales, col, n, 1)
        values = (codes - 8).astype(F32).reshape(groups, features // groups, n)
        quant = (values * scales[:, None, :]).reshape(features, n).astype(BF16)
        return jnp.where(kind == 0, plain, quant)

    pairs = []
    for a in range(2):
        for c in range(2):
            for b in range(2):
                pairs.append((a * 4 + c * 2 + b, (a ^ c) * 4 + c * 2 + (1 - b)))

    def exchange(first, n):
        col = core * half + first
        own, send = weight(yh, col, n), weight(yh ^ core, col, n)
        return own, lax.ppermute(send, ("yh", "core", "yl"), pairs)

    def near(rows):
        return from_z(rows, 1), from_z(rows, 3)

    def far(up, down):
        return from_z(up[:features], 1), from_z(down[features:], 3)

    w0, w1, w2 = WIDTHS
    rows0 = join(*exchange(0, w0), ())
    near0 = near(rows0)

    payload = pack(jnp.stack([yl, z]), attn_float, attn_quant, rows0)
    mine = lax.all_to_all(payload, ("yh", "x"), 0, 0, tiled=True)
    mine = mine.reshape(8 * tokens, 8 * features + 2 * BLOCK)

    far0 = far(*near0)
    rows1 = join(*exchange(w0, w1), far0)
    near1 = near(rows1)
    mine, *near0 = lax.optimization_barrier((mine, *near0))
    other = swap(mine, "core")
    far1 = far(*near1)
    rows2 = join(*exchange(w0 + w1, w2), far1)
    near2 = near(rows2)
    far2 = far(*near2)

    def part(rows, near, far, after):
        width = rows.shape[1]
        partial = project(core, mine, other, (rows, near[0], *far, near[1]), after)
        return lax.all_to_all(
            partial.reshape(16, tokens, width), ("yh", "core", "x"), 0, 0, tiled=True
        )

    result0 = part(rows0, near0, far0, ())

    def stats(j):
        at = 2 * j * features
        total = 0.0
        for acts in (mine, other):
            picked = jnp.where(
                core == 0, acts[:, at : at + features], acts[:, at + features : at + 2 * features]
            )
            total = total + lax.dot_general(
                picked, acts[:, 8 * features :], (((0,), (0,)), ((), ())), preferred_element_type=F32
            )
        return total

    total = 0.0
    for j in range(4):
        pairs = [
            (c * 8 + b * 4 + i, c * 8 + (b ^ c) * 4 + (i + j) % 4)
            for c in range(2)
            for b in range(2)
            for i in range(4)
        ]
        total = total + lax.ppermute(stats(j).astype(BF16), ("core", "yl", "z"), pairs).astype(F32)
    total = (total + swap(total, "core")) * inverse

    result1 = part(rows1, near1, far1, ())
    result2 = part(rows2, near2, far2, (total,))
    float_out, quant_out = finish((result0, result1, result2))
    total = jnp.where(yh == 1, total, swap(total, "yh"))
    return float_out, quant_out, total[:, :BLOCK], total[:, BLOCK:]


def solution(mesh):
    fine = Mesh(mesh.devices.reshape(2, 2, 2, 4, 4), FINE)
    rows, tok = P(FINE, None), P(("yl", "z", "x"), None)
    return jax.shard_map(
        shards,
        mesh=fine,
        in_specs=(rows, rows, tok, tok, tok),
        out_specs=(rows, rows, tok, tok),
        check_vma=False,
    )
```

```python
import jax
import jax.numpy as jnp
from jax import lax
from jax.experimental import pallas as pl
from jax.experimental.pallas import tpu as pltpu
from jax.sharding import Mesh
from jax.sharding import PartitionSpec as P

BLOCK = 128
WIDTHS = (768, 768, 512)
FINE = ("yh", "core", "yl", "z", "x")
F32 = jnp.float32
BF16 = jnp.bfloat16
WHOLE = pl.BlockSpec(memory_space=pltpu.VMEM)
SCALAR = pl.BlockSpec(memory_space=pltpu.SMEM)
LEFT = pl.BlockSpec(memory_space=pl.ANY)


def params():
    return pltpu.CompilerParams(vmem_limit_bytes=16 << 20)


def pack_kernel(at_ref, float_ref, quant_ref, after_ref, out_ref, head_ref, sems, head_sem):
    width = float_ref.shape[1] // 32
    yl, z = at_ref[0], at_ref[1]
    heads = [
        pltpu.make_async_copy(ref.at[:, pl.ds(0, BLOCK)], head_ref.at[kind], head_sem.at[kind])
        for kind, ref in enumerate((float_ref, quant_ref))
    ]
    for copy in heads:
        copy.start()
    copies = []
    for kind, ref in enumerate((float_ref, quant_ref)):
        for x in range(4):
            for j in range(4):
                for r in range(2):
                    block = ((yl ^ r) * 4 + lax.rem(z + j, 4)) * 4 + x
                    start = pl.multiple_of(block * width, width)
                    at = (j * 2 + r) * width
                    copies.append(
                        pltpu.make_async_copy(
                            ref.at[:, pl.ds(start, width)],
                            out_ref.at[kind * 4 + x, :, pl.ds(at, width)],
                            sems.at[len(copies)],
                        )
                    )
    for copy in copies:
        copy.start()
    for copy in heads:
        copy.wait()
    quant = head_ref[1]
    shift = (head_ref[0].astype(F32) - quant.astype(F32)).astype(BF16)
    for d in range(8):
        out_ref[d, :, 8 * width : 8 * width + BLOCK] = quant
        out_ref[d, :, 8 * width + BLOCK :] = shift
    for copy in copies:
        copy.wait()


def pack(at, attn_float, attn_quant, after):
    tokens, d_in = attn_float.shape
    return pl.pallas_call(
        pack_kernel,
        out_shape=jax.ShapeDtypeStruct((8, tokens, d_in // 4 + 2 * BLOCK), BF16),
        in_specs=[SCALAR, LEFT, LEFT, LEFT],
        out_specs=WHOLE,
        scratch_shapes=[
            pltpu.VMEM((2, tokens, BLOCK), BF16),
            pltpu.SemaphoreType.DMA((64,)),
            pltpu.SemaphoreType.DMA((2,)),
        ],
        compiler_params=params(),
        name="pack",
    )(at, attn_float, attn_quant, after)


def stats_kernel(core_ref, mine_ref, other_ref, after_ref, *outs):
    core = core_ref[0]
    width = outs[0].shape[0]
    tail = 8 * width
    for j, out in enumerate(outs):
        start = pl.multiple_of((2 * j + core) * width, width)
        total = None
        for acts in (mine_ref, other_ref):
            term = lax.dot_general(
                acts[:, pl.ds(start, width)],
                acts[:, tail:],
                (((0,), (0,)), ((), ())),
                preferred_element_type=F32,
            )
            total = term if total is None else total + term
        out[...] = total.astype(BF16)


def stats(core, mine, other, after):
    width = 2 * BLOCK
    return pl.pallas_call(
        stats_kernel,
        out_shape=(jax.ShapeDtypeStruct((width, width), BF16),) * 4,
        in_specs=[SCALAR, WHOLE, WHOLE, LEFT],
        out_specs=(WHOLE,) * 4,
        compiler_params=params(),
        name="stats",
    )(core.reshape(1), mine, other, after)


def join_kernel(*refs):
    own_ref, got_ref, out_ref = refs[0], refs[1], refs[-1]
    n = own_ref.shape[0]
    out_ref[:n] = own_ref[...]
    out_ref[n:] = got_ref[...]


def join(own, got, after):
    n, m = own.shape
    return pl.pallas_call(
        join_kernel,
        out_shape=jax.ShapeDtypeStruct((2 * n, m), BF16),
        in_specs=[WHOLE, WHOLE] + [LEFT] * len(after),
        out_specs=WHOLE,
        compiler_params=params(),
        name="join",
    )(own, got, *after)


def project_kernel(core_ref, mine_ref, other_ref, *refs):
    parts, out_ref = refs[:5], refs[-1]
    core = core_ref[0]
    rows = out_ref.shape[2]
    for n, acts in enumerate((mine_ref, other_ref)):
        where = core if n == 0 else 1 - core
        for yh in range(2):
            total, at = None, 0
            for part in parts:
                depth = part.shape[0]
                term = jnp.dot(
                    acts[yh * rows : (yh + 1) * rows, at : at + depth],
                    part[...],
                    preferred_element_type=F32,
                )
                total = term if total is None else total + term
                at += depth
            out_ref[yh, where] = total.astype(BF16)


def project(core, mine, other, parts, after):
    rows, cols = mine.shape[0] // 2, parts[0].shape[1]
    return pl.pallas_call(
        project_kernel,
        out_shape=jax.ShapeDtypeStruct((2, 2, rows, cols), BF16),
        in_specs=[SCALAR] + [WHOLE] * (2 + len(parts)) + [LEFT] * len(after),
        out_specs=WHOLE,
        compiler_params=params(),
        cost_estimate=pl.CostEstimate(
            flops=8 * rows * cols * 2048, bytes_accessed=8 << 20, transcendentals=0
        ),
        name="project",
    )(core.reshape(1), mine, other, *parts, *after)


def finish_kernel(*refs):
    *parts, float_ref, quant_ref = refs
    at_half, start = float_ref.shape[1] // 2, 0
    for ref in parts:
        width = ref.shape[2]
        for kind, out in enumerate((float_ref, quant_ref)):
            for half in range(2):
                at = kind * 8 + half * 4
                total = ref[at].astype(F32)
                for x in range(1, 4):
                    total += ref[at + x].astype(F32)
                col = half * at_half + start
                out[:, col : col + width] = total.astype(BF16)
        start += width


def finish(parts):
    tokens = parts[0].shape[1]
    return pl.pallas_call(
        finish_kernel,
        out_shape=(jax.ShapeDtypeStruct((tokens, 2 * sum(WIDTHS)), BF16),) * 2,
        in_specs=[WHOLE] * len(parts),
        out_specs=(WHOLE, WHOLE),
        compiler_params=params(),
        name="finish",
    )(*parts)


def swap(a, axis):
    return lax.ppermute(a, axis, [(0, 1), (1, 0)])


def from_z(a, j):
    return lax.ppermute(a, "z", [((i + j) % 4, i) for i in range(4)])


def shards(attn_float, attn_quant, proj_weight, weight_codes, group_scales):
    tokens, d_in = attn_float.shape
    features, d_out = proj_weight.shape
    groups = group_scales.shape[0]
    half = d_out // 2
    inverse = 1.0 / (tokens * 128)
    yh, core, yl, z = (lax.axis_index(a) for a in ("yh", "core", "yl", "z"))

    def weight(kind, col, n):
        plain = lax.dynamic_slice_in_dim(proj_weight, col, n, 1)
        codes = lax.dynamic_slice_in_dim(weight_codes, col, n, 1)
        scales = lax.dynamic_slice_in_dim(group_scales, col, n, 1)
        values = (codes - 8).astype(F32).reshape(groups, features // groups, n)
        quant = (values * scales[:, None, :]).reshape(features, n).astype(BF16)
        return jnp.where(kind == 0, plain, quant)

    pairs = []
    for a in range(2):
        for c in range(2):
            for b in range(2):
                pairs.append((a * 4 + c * 2 + b, (a ^ c) * 4 + c * 2 + (1 - b)))

    def exchange(first, n):
        col = core * half + first
        own, send = weight(yh, col, n), weight(yh ^ core, col, n)
        return own, lax.ppermute(send, ("yh", "core", "yl"), pairs)

    def near(rows):
        return from_z(rows, 1), from_z(rows, 3)

    def far(up, down):
        return from_z(up[:features], 1), from_z(down[features:], 3)

    def output(partial):
        width = partial.shape[-1]
        return lax.all_to_all(
            partial.reshape(16, tokens, width), ("yh", "core", "x"), 0, 0, tiled=True
        )

    w0, w1, w2 = WIDTHS
    rows0 = join(*exchange(0, w0), ())
    near0 = near(rows0)

    payload = pack(jnp.stack([yl, z]), attn_float, attn_quant, rows0)
    mine = lax.all_to_all(payload, ("yh", "x"), 0, 0, tiled=True)
    mine = mine.reshape(8 * tokens, 8 * features + 2 * BLOCK)

    far0 = far(*near0)
    rows1 = join(*exchange(w0, w1), near0)
    mine, rows1 = lax.optimization_barrier((mine, rows1))
    near1 = near(rows1)
    other = swap(mine, "core")
    partial0 = project(core, mine, other, (rows0, near0[0], *far0, near0[1]), ())
    result0 = output(partial0)

    near1 = lax.optimization_barrier((*near1, partial0))[:2]
    far1 = far(*near1)

    total = 0.0
    for j, block in enumerate(stats(core, mine, other, partial0)):
        homes = [
            (c * 8 + b * 4 + i, c * 8 + (b ^ c) * 4 + (i + j) % 4)
            for c in range(2)
            for b in range(2)
            for i in range(4)
        ]
        total = total + lax.ppermute(block, ("core", "yl", "z"), homes).astype(F32)

    rows2 = join(*exchange(w0 + w1, w2), far1)
    near2 = near(rows2)
    partial1 = project(
        core, mine, other, (rows1, near1[0], *far1, near1[1]), (rows2, total)
    )
    result1 = output(partial1)
    total = (total + swap(total, "core")) * inverse
    near2 = lax.optimization_barrier((*near2, partial1))[:2]
    far2 = far(*near2)

    piece = lax.dynamic_slice_in_dim(total, core * BLOCK, BLOCK, 0)
    piece = swap(piece, "yh")
    partial2 = project(core, mine, other, (rows2, near2[0], *far2, near2[1]), (total,))
    result2 = output(partial2)
    again = swap(piece, "core")
    moved = jnp.where(
        core == 0, jnp.concatenate([piece, again]), jnp.concatenate([again, piece])
    )
    total = jnp.where(yh == 1, total, moved)
    float_out, quant_out = finish((result0, result1, result2))
    return float_out, quant_out, total[:, :BLOCK], total[:, BLOCK:]


def solution(mesh):
    fine = Mesh(mesh.devices.reshape(2, 2, 2, 4, 4), FINE)
    rows, tok = P(FINE, None), P(("yl", "z", "x"), None)
    return jax.shard_map(
        shards,
        mesh=fine,
        in_specs=(rows, rows, tok, tok, tok),
        out_specs=(rows, rows, tok, tok),
        check_vma=False,
    )
```

```python
import jax
import jax.numpy as jnp
from jax import lax
from jax.experimental import pallas as pl
from jax.experimental.pallas import tpu as pltpu
from jax.sharding import Mesh
from jax.sharding import PartitionSpec as P

BLOCK = 128
FINE = ("yh", "core", "yl", "z", "x")
PLANE = ("yh", "yl", "x")
F32 = jnp.float32
BF16 = jnp.bfloat16


WHOLE = pl.BlockSpec(memory_space=pltpu.VMEM)
SCALAR = pl.BlockSpec(memory_space=pltpu.SMEM)


def params():
    return pltpu.CompilerParams(vmem_limit_bytes=16 << 20)


def pack_kernel(z_ref, float_ref, quant_ref, out_ref):
    width = out_ref.shape[2] // 8
    z = z_ref[0]
    for kind, ref in enumerate((float_ref, quant_ref)):
        for j in range(4):
            zj = lax.rem(z + j, 4)
            for yl in range(2):
                for x in range(4):
                    start = pl.multiple_of(((yl * 4 + zj) * 4 + x) * width, width)
                    block = ref[:, pl.ds(start, width)]
                    for half in range(2):
                        at = (j * 2 + (yl ^ half)) * width
                        out_ref[kind * 8 + half * 4 + x, :, at : at + width] = block


def pack(z, attn_float, attn_quant):
    tokens, d_in = attn_float.shape
    return pl.pallas_call(
        pack_kernel,
        out_shape=jax.ShapeDtypeStruct((16, tokens, d_in // 4), BF16),
        in_specs=[SCALAR, WHOLE, WHOLE],
        out_specs=WHOLE,
        compiler_params=params(),
        name="pack",
    )(z.reshape(1), attn_float, attn_quant)


def finish_kernel(core_ref, first_ref, second_ref, float_ref, quant_ref):
    core = core_ref[0]
    width = first_ref.shape[2]
    for n, ref in enumerate((first_ref, second_ref)):
        quarter = core if n == 0 else 1 - core
        for kind, out in enumerate((float_ref, quant_ref)):
            for half in range(2):
                at = kind * 8 + half * 4
                total = ref[at].astype(F32)
                for x in range(1, 4):
                    total += ref[at + x].astype(F32)
                start = pl.multiple_of((half * 2 + quarter) * width, width)
                out[:, pl.ds(start, width)] = total.astype(BF16)


def finish(core, first, second):
    _, tokens, width = first.shape
    return pl.pallas_call(
        finish_kernel,
        out_shape=(jax.ShapeDtypeStruct((tokens, 4 * width), BF16),) * 2,
        in_specs=[SCALAR, WHOLE, WHOLE],
        out_specs=(WHOLE, WHOLE),
        compiler_params=params(),
        name="finish",
    )(core.reshape(1), first, second)


def stats_kernel(at_ref, acts_ref, *refs):
    pieces, outs, block_ref = refs[:4], refs[4:8], refs[8]
    y, x = at_ref[0], at_ref[1]
    tokens = pieces[0].shape[0] // 4
    for dy, piece in enumerate(pieces):
        for dx in range(4):
            start = (lax.rem(y + dy, 4) * 4 + lax.rem(x + dx, 4)) * tokens
            block_ref[pl.ds(pl.multiple_of(start, tokens), tokens)] = piece[
                dx * tokens : (dx + 1) * tokens
            ]
    width = outs[0].shape[0]
    for j, out in enumerate(outs):
        out[...] = lax.dot_general(
            acts_ref[:, 2 * j * width : (2 * j + 1) * width],
            block_ref[...],
            (((0,), (0,)), ((), ())),
            preferred_element_type=F32,
        ).astype(out.dtype)


def stats(at, acts, pieces):
    width = 2 * BLOCK
    return pl.pallas_call(
        stats_kernel,
        out_shape=(jax.ShapeDtypeStruct((width, width), F32),)
        + (jax.ShapeDtypeStruct((width, width), BF16),) * 3,
        in_specs=[SCALAR] + [WHOLE] * 5,
        out_specs=(WHOLE,) * 4,
        scratch_shapes=[pltpu.VMEM((acts.shape[0], width), BF16)],
        compiler_params=params(),
        name="stats",
    )(at, acts, *pieces)


def swap(a, axis):
    return lax.ppermute(a, axis, [(0, 1), (1, 0)])


def ahead(a, axis, j):
    return lax.ppermute(a, axis, [((i + j) % 4, i) for i in range(4)])


def shards(attn_float, attn_quant, proj_weight, weight_codes, group_scales):
    tokens, d_in = attn_float.shape
    features, d_out = proj_weight.shape
    groups = group_scales.shape[0]
    half, quarter = d_out // 2, d_out // 4
    inverse = 1.0 / (tokens * 128)
    yh, core, yl, z = (lax.axis_index(a) for a in ("yh", "core", "yl", "z"))

    def weight(kind, col):
        plain = lax.dynamic_slice_in_dim(proj_weight, col, quarter, 1)
        codes = lax.dynamic_slice_in_dim(weight_codes, col, quarter, 1)
        scales = lax.dynamic_slice_in_dim(group_scales, col, quarter, 1)
        values = (codes - 8).astype(F32).reshape(groups, features // groups, quarter)
        quant = (values * scales[:, None, :]).reshape(features, quarter).astype(BF16)
        return jnp.where(kind == 0, plain, quant)

    own = weight(yh, yl * half + core * quarter)
    send = weight(yh ^ core, (1 - yl) * half + core * quarter)
    pairs = []
    for a in range(2):
        for c in range(2):
            for b in range(2):
                pairs.append((a * 4 + c * 2 + b, (a ^ c) * 4 + c * 2 + (1 - b)))
    got = lax.ppermute(send, ("yh", "core", "yl"), pairs)

    payload = pack(z, attn_float, attn_quant)
    rows = jnp.concatenate([own, got], axis=0)
    parts = [rows] + [ahead(rows, "z", j) for j in (1, 2, 3)]
    mine = jnp.concatenate(parts, axis=0)
    other = swap(mine, "core")

    quant = attn_quant[:, :BLOCK]
    shift = (attn_float[:, :BLOCK].astype(F32) - quant.astype(F32)).astype(BF16)
    block = jnp.concatenate([quant, shift], axis=1)
    block, payload = lax.optimization_barrier((block, payload))
    acts = lax.all_to_all(payload, PLANE, 0, 0, tiled=True).reshape(16 * tokens, 8 * features)

    line = jnp.concatenate([block] + [ahead(block, "x", j) for j in (1, 2, 3)], axis=0)
    pieces = [line] + [ahead(line, ("yh", "yl"), j) for j in (1, 2, 3)]
    acts, mine, *pieces = lax.optimization_barrier((acts, mine, *pieces))

    def part(w):
        return jnp.dot(acts, w, preferred_element_type=F32).astype(BF16)

    def output(p):
        return lax.all_to_all(p.reshape(16, tokens, quarter), PLANE, 0, 0, tiled=True)

    first = part(mine)
    result1 = output(first)

    acts1, first = lax.optimization_barrier((acts, first))
    blocks = stats(jnp.stack([yh * 2 + yl, lax.axis_index("x")]), acts1, pieces)
    total = blocks[0]
    for j in (1, 2, 3):
        total = total + ahead(blocks[j], "z", 4 - j).astype(F32)
    other, total = lax.optimization_barrier((other, total))
    second = part(other)
    total = (total + swap(total, "core")) * inverse
    second, total = lax.optimization_barrier((second, total))
    result2 = output(second)

    piece = swap(lax.dynamic_slice_in_dim(total, core * BLOCK, BLOCK, 0), "yh")
    again = swap(piece, "core")
    moved = jnp.where(
        core == 0, jnp.concatenate([piece, again]), jnp.concatenate([again, piece])
    )
    total = jnp.where(yh == 1, total, moved)
    float_out, quant_out = finish(core, result1, result2)
    return float_out, quant_out, total[:, :BLOCK], total[:, BLOCK:]


def solution(mesh):
    fine = Mesh(mesh.devices.reshape(2, 2, 2, 4, 4), FINE)
    rows, tok = P(FINE, None), P(("yl", "z", "x"), None)
    return jax.shard_map(
        shards,
        mesh=fine,
        in_specs=(rows, rows, tok, tok, tok),
        out_specs=(rows, rows, tok, tok),
        check_vma=False,
    )
```

```python
import jax
import jax.numpy as jnp
from jax import lax
from jax.experimental import pallas as pl
from jax.experimental.pallas import tpu as pltpu
from jax.sharding import Mesh
from jax.sharding import PartitionSpec as P

BLOCK = 128
FINE = ("yh", "core", "yl", "z", "x")
PLANE = ("yh", "yl", "x")
F32 = jnp.float32
BF16 = jnp.bfloat16


WHOLE = pl.BlockSpec(memory_space=pltpu.VMEM)
SCALAR = pl.BlockSpec(memory_space=pltpu.SMEM)


def params():
    return pltpu.CompilerParams(vmem_limit_bytes=16 << 20)


def pack_kernel(z_ref, float_ref, quant_ref, out_ref):
    width = out_ref.shape[2] // 8
    z = z_ref[0]
    for kind, ref in enumerate((float_ref, quant_ref)):
        for j in range(4):
            zj = lax.rem(z + j, 4)
            for yl in range(2):
                for x in range(4):
                    start = pl.multiple_of(((yl * 4 + zj) * 4 + x) * width, width)
                    block = ref[:, pl.ds(start, width)]
                    for half in range(2):
                        at = (j * 2 + (yl ^ half)) * width
                        out_ref[kind * 8 + half * 4 + x, :, at : at + width] = block


def pack(z, attn_float, attn_quant):
    tokens, d_in = attn_float.shape
    return pl.pallas_call(
        pack_kernel,
        out_shape=jax.ShapeDtypeStruct((16, tokens, d_in // 4), BF16),
        in_specs=[SCALAR, WHOLE, WHOLE],
        out_specs=WHOLE,
        compiler_params=params(),
        name="pack",
    )(z.reshape(1), attn_float, attn_quant)


def finish_kernel(core_ref, first_ref, second_ref, float_ref, quant_ref):
    core = core_ref[0]
    width = first_ref.shape[2]
    for n, ref in enumerate((first_ref, second_ref)):
        quarter = core if n == 0 else 1 - core
        for kind, out in enumerate((float_ref, quant_ref)):
            for half in range(2):
                at = kind * 8 + half * 4
                total = ref[at].astype(F32)
                for x in range(1, 4):
                    total += ref[at + x].astype(F32)
                start = pl.multiple_of((half * 2 + quarter) * width, width)
                out[:, pl.ds(start, width)] = total.astype(BF16)


def finish(core, first, second):
    _, tokens, width = first.shape
    return pl.pallas_call(
        finish_kernel,
        out_shape=(jax.ShapeDtypeStruct((tokens, 4 * width), BF16),) * 2,
        in_specs=[SCALAR, WHOLE, WHOLE],
        out_specs=(WHOLE, WHOLE),
        compiler_params=params(),
        name="finish",
    )(core.reshape(1), first, second)


def stats_kernel(acts_ref, block_ref, *outs):
    width = outs[0].shape[0]
    for j, out in enumerate(outs):
        out[...] = lax.dot_general(
            acts_ref[:, 2 * j * width : (2 * j + 1) * width],
            block_ref[...],
            (((0,), (0,)), ((), ())),
            preferred_element_type=F32,
        ).astype(out.dtype)


def stats(acts, block):
    width = 2 * BLOCK
    return pl.pallas_call(
        stats_kernel,
        out_shape=(jax.ShapeDtypeStruct((width, width), F32),)
        + (jax.ShapeDtypeStruct((width, width), BF16),) * 3,
        in_specs=[WHOLE] * 2,
        out_specs=(WHOLE,) * 4,
        compiler_params=params(),
        name="stats",
    )(acts, block)


def swap(a, axis):
    return lax.ppermute(a, axis, [(0, 1), (1, 0)])


def ahead(a, axis, j):
    return lax.ppermute(a, axis, [((i + j) % 4, i) for i in range(4)])


def shards(attn_float, attn_quant, proj_weight, weight_codes, group_scales):
    tokens, d_in = attn_float.shape
    features, d_out = proj_weight.shape
    groups = group_scales.shape[0]
    half, quarter = d_out // 2, d_out // 4
    inverse = 1.0 / (tokens * 128)
    yh, core, yl, z = (lax.axis_index(a) for a in ("yh", "core", "yl", "z"))

    def weight(kind, col):
        plain = lax.dynamic_slice_in_dim(proj_weight, col, quarter, 1)
        codes = lax.dynamic_slice_in_dim(weight_codes, col, quarter, 1)
        scales = lax.dynamic_slice_in_dim(group_scales, col, quarter, 1)
        values = (codes - 8).astype(F32).reshape(groups, features // groups, quarter)
        quant = (values * scales[:, None, :]).reshape(features, quarter).astype(BF16)
        return jnp.where(kind == 0, plain, quant)

    own = weight(yh, yl * half + core * quarter)
    send = weight(yh ^ core, (1 - yl) * half + core * quarter)
    pairs = []
    for a in range(2):
        for c in range(2):
            for b in range(2):
                pairs.append((a * 4 + c * 2 + b, (a ^ c) * 4 + c * 2 + (1 - b)))
    got = lax.ppermute(send, ("yh", "core", "yl"), pairs)

    quant = attn_quant[:, :BLOCK]
    shift = (attn_float[:, :BLOCK].astype(F32) - quant.astype(F32)).astype(BF16)
    block = jnp.concatenate([quant, shift], axis=1)
    block = lax.all_gather(block, PLANE, axis=0, tiled=True)

    payload = pack(z, attn_float, attn_quant)
    rows = jnp.concatenate([own, got], axis=0)
    parts = [rows] + [ahead(rows, "z", j) for j in (1, 2, 3)]
    mine = jnp.concatenate(parts, axis=0)
    other = swap(mine, "core")

    acts = lax.all_to_all(payload, PLANE, 0, 0, tiled=True).reshape(16 * tokens, 8 * features)

    def part(w):
        return jnp.dot(acts, w, preferred_element_type=F32).astype(BF16)

    def output(p):
        return lax.all_to_all(p.reshape(16, tokens, quarter), PLANE, 0, 0, tiled=True)

    first = part(mine)
    result1 = output(first)

    acts1, first = lax.optimization_barrier((acts, first))
    blocks = stats(acts1, block)
    total = blocks[0]
    for j in (1, 2, 3):
        total = total + ahead(blocks[j], "z", 4 - j).astype(F32)
    total = (total + swap(total, "core")) * inverse
    second, total = lax.optimization_barrier((part(other), total))
    result2 = output(second)

    piece = swap(lax.dynamic_slice_in_dim(total, core * BLOCK, BLOCK, 0), "yh")
    again = swap(piece, "core")
    moved = jnp.where(
        core == 0, jnp.concatenate([piece, again]), jnp.concatenate([again, piece])
    )
    total = jnp.where(yh == 1, total, moved)
    float_out, quant_out = finish(core, result1, result2)
    return float_out, quant_out, total[:, :BLOCK], total[:, BLOCK:]


def solution(mesh):
    fine = Mesh(mesh.devices.reshape(2, 2, 2, 4, 4), FINE)
    rows, tok = P(FINE, None), P(("yl", "z", "x"), None)
    return jax.shard_map(
        shards,
        mesh=fine,
        in_specs=(rows, rows, tok, tok, tok),
        out_specs=(rows, rows, tok, tok),
        check_vma=False,
    )
```

```python
import jax
import jax.numpy as jnp
from jax import lax
from jax.experimental import pallas as pl
from jax.experimental.pallas import tpu as pltpu
from jax.sharding import Mesh
from jax.sharding import PartitionSpec as P

BLOCK = 128
FINE = ("yh", "core", "yl", "z", "x")
PLANE = ("yh", "yl", "x")
F32 = jnp.float32
BF16 = jnp.bfloat16


WHOLE = pl.BlockSpec(memory_space=pltpu.VMEM)
SCALAR = pl.BlockSpec(memory_space=pltpu.SMEM)


def params():
    return pltpu.CompilerParams(vmem_limit_bytes=16 << 20)


def pack_kernel(z_ref, float_ref, quant_ref, out_ref):
    width = float_ref.shape[1] // 32
    z = z_ref[0]
    quant = quant_ref[:, :BLOCK]
    shift = (float_ref[:, :BLOCK].astype(F32) - quant.astype(F32)).astype(BF16)
    for kind, ref in enumerate((float_ref, quant_ref)):
        for j in range(4):
            zj = lax.rem(z + j, 4)
            for yl in range(2):
                for x in range(4):
                    start = pl.multiple_of(((yl * 4 + zj) * 4 + x) * width, width)
                    block = ref[:, pl.ds(start, width)]
                    for half in range(2):
                        at = (j * 2 + (yl ^ half)) * width
                        out_ref[kind * 8 + half * 4 + x, :, at : at + width] = block
    for d in range(16):
        out_ref[d, :, 8 * width : 8 * width + BLOCK] = quant
        out_ref[d, :, 8 * width + BLOCK :] = shift


def pack(z, attn_float, attn_quant):
    tokens, d_in = attn_float.shape
    return pl.pallas_call(
        pack_kernel,
        out_shape=jax.ShapeDtypeStruct((16, tokens, d_in // 4 + 2 * BLOCK), BF16),
        in_specs=[SCALAR, WHOLE, WHOLE],
        out_specs=WHOLE,
        compiler_params=params(),
        name="pack",
    )(z.reshape(1), attn_float, attn_quant)


def finish_kernel(core_ref, first_ref, second_ref, float_ref, quant_ref):
    core = core_ref[0]
    width = first_ref.shape[2]
    for n, ref in enumerate((first_ref, second_ref)):
        quarter = core if n == 0 else 1 - core
        for kind, out in enumerate((float_ref, quant_ref)):
            for half in range(2):
                at = kind * 8 + half * 4
                total = ref[at].astype(F32)
                for x in range(1, 4):
                    total += ref[at + x].astype(F32)
                start = pl.multiple_of((half * 2 + quarter) * width, width)
                out[:, pl.ds(start, width)] = total.astype(BF16)


def finish(core, first, second):
    _, tokens, width = first.shape
    return pl.pallas_call(
        finish_kernel,
        out_shape=(jax.ShapeDtypeStruct((tokens, 4 * width), BF16),) * 2,
        in_specs=[SCALAR, WHOLE, WHOLE],
        out_specs=(WHOLE, WHOLE),
        compiler_params=params(),
        name="finish",
    )(core.reshape(1), first, second)


def stats_kernel(acts_ref, *outs):
    width = outs[0].shape[0]
    for j, out in enumerate(outs):
        out[...] = lax.dot_general(
            acts_ref[:, 2 * j * width : (2 * j + 1) * width],
            acts_ref[:, 8 * width :],
            (((0,), (0,)), ((), ())),
            preferred_element_type=F32,
        ).astype(out.dtype)


def stats(acts):
    width = 2 * BLOCK
    return pl.pallas_call(
        stats_kernel,
        out_shape=(jax.ShapeDtypeStruct((width, width), F32),)
        + (jax.ShapeDtypeStruct((width, width), BF16),) * 3,
        in_specs=[WHOLE],
        out_specs=(WHOLE,) * 4,
        compiler_params=params(),
        name="stats",
    )(acts)


def swap(a, axis):
    return lax.ppermute(a, axis, [(0, 1), (1, 0)])


def ahead(a, axis, j):
    return lax.ppermute(a, axis, [((i + j) % 4, i) for i in range(4)])


def shards(attn_float, attn_quant, proj_weight, weight_codes, group_scales):
    tokens, d_in = attn_float.shape
    features, d_out = proj_weight.shape
    groups = group_scales.shape[0]
    half, quarter = d_out // 2, d_out // 4
    inverse = 1.0 / (tokens * 128)
    yh, core, yl, z = (lax.axis_index(a) for a in ("yh", "core", "yl", "z"))

    def weight(kind, col):
        plain = lax.dynamic_slice_in_dim(proj_weight, col, quarter, 1)
        codes = lax.dynamic_slice_in_dim(weight_codes, col, quarter, 1)
        scales = lax.dynamic_slice_in_dim(group_scales, col, quarter, 1)
        values = (codes - 8).astype(F32).reshape(groups, features // groups, quarter)
        quant = (values * scales[:, None, :]).reshape(features, quarter).astype(BF16)
        return jnp.where(kind == 0, plain, quant)

    own = weight(yh, yl * half + core * quarter)
    send = weight(yh ^ core, (1 - yl) * half + core * quarter)
    pairs = []
    for a in range(2):
        for c in range(2):
            for b in range(2):
                pairs.append((a * 4 + c * 2 + b, (a ^ c) * 4 + c * 2 + (1 - b)))
    got = lax.ppermute(send, ("yh", "core", "yl"), pairs)

    payload = pack(z, attn_float, attn_quant)
    rows = jnp.concatenate([own, got], axis=0)
    parts = [rows] + [ahead(rows, "z", j) for j in (1, 2, 3)]
    mine = jnp.concatenate(parts, axis=0)
    other = swap(mine, "core")

    acts = lax.all_to_all(payload, PLANE, 0, 0, tiled=True)
    acts = acts.reshape(16 * tokens, 8 * features + 2 * BLOCK)

    def part(w):
        return jnp.dot(acts[:, : 8 * features], w, preferred_element_type=F32).astype(BF16)

    def output(p):
        return lax.all_to_all(p.reshape(16, tokens, quarter), PLANE, 0, 0, tiled=True)

    first = part(mine)
    result1 = output(first)

    acts1, first = lax.optimization_barrier((acts, first))
    blocks = stats(acts1)
    total = blocks[0]
    for j in (1, 2, 3):
        total = total + ahead(blocks[j], "z", 4 - j).astype(F32)
    total = (total + swap(total, "core")) * inverse
    piece = swap(lax.dynamic_slice_in_dim(total, core * BLOCK, BLOCK, 0), "yh")
    second, piece = lax.optimization_barrier((part(other), piece))
    result2 = output(second)
    again = swap(piece, "core")
    moved = jnp.where(
        core == 0, jnp.concatenate([piece, again]), jnp.concatenate([again, piece])
    )
    total = jnp.where(yh == 1, total, moved)
    float_out, quant_out = finish(core, result1, result2)
    return float_out, quant_out, total[:, :BLOCK], total[:, BLOCK:]


def solution(mesh):
    fine = Mesh(mesh.devices.reshape(2, 2, 2, 4, 4), FINE)
    rows, tok = P(FINE, None), P(("yl", "z", "x"), None)
    return jax.shard_map(
        shards,
        mesh=fine,
        in_specs=(rows, rows, tok, tok, tok),
        out_specs=(rows, rows, tok, tok),
        check_vma=False,
    )
```

```python
import jax
import jax.numpy as jnp
from jax import lax
from jax.experimental import pallas as pl
from jax.experimental.pallas import tpu as pltpu
from jax.sharding import Mesh
from jax.sharding import PartitionSpec as P

BLOCK = 128
SPLIT = (48, 16)
FINE = ("yh", "core", "yl", "z", "x")
PLANE = ("yh", "yl", "x")
F32 = jnp.float32
BF16 = jnp.bfloat16


WHOLE = pl.BlockSpec(memory_space=pltpu.VMEM)
LEFT = pl.BlockSpec(memory_space=pl.ANY)
SCALAR = pl.BlockSpec(memory_space=pltpu.SMEM)


def params():
    return pltpu.CompilerParams(vmem_limit_bytes=16 << 20)


def pack_kernel(z_ref, float_ref, quant_ref, after_ref, *outs):
    width = float_ref.shape[1] // 32
    z = z_ref[0]
    row = 0
    for out_ref in outs:
        rows = slice(row, row + out_ref.shape[1])
        row = rows.stop
        quant = quant_ref[rows, :BLOCK]
        shift = (float_ref[rows, :BLOCK].astype(F32) - quant.astype(F32)).astype(BF16)
        for kind, ref in enumerate((float_ref, quant_ref)):
            for j in range(4):
                zj = lax.rem(z + j, 4)
                for yl in range(2):
                    for x in range(4):
                        start = pl.multiple_of(((yl * 4 + zj) * 4 + x) * width, width)
                        block = ref[rows, pl.ds(start, width)]
                        for half in range(2):
                            at = ((yl ^ half) * 4 + j) * width
                            out_ref[kind * 8 + half * 4 + x, :, at : at + width] = block
        for d in range(16):
            out_ref[d, :, 8 * width : 8 * width + BLOCK] = quant
            out_ref[d, :, 8 * width + BLOCK :] = shift


def pack(z, attn_float, attn_quant, after):
    d_in = attn_float.shape[1]
    return pl.pallas_call(
        pack_kernel,
        out_shape=tuple(
            jax.ShapeDtypeStruct((16, n, d_in // 4 + 2 * BLOCK), BF16) for n in SPLIT
        ),
        in_specs=[SCALAR, WHOLE, WHOLE, LEFT],
        out_specs=(WHOLE,) * len(SPLIT),
        compiler_params=params(),
        name="pack",
    )(z.reshape(1), attn_float, attn_quant, after)


def join_kernel(*refs):
    *parts, out_ref = refs
    row = 0
    for part in parts:
        out_ref[row : row + part.shape[0]] = part[...]
        row += part.shape[0]


def join(parts):
    rows, cols = parts[0].shape
    return pl.pallas_call(
        join_kernel,
        out_shape=jax.ShapeDtypeStruct((len(parts) * rows, cols), BF16),
        in_specs=[WHOLE] * len(parts),
        out_specs=WHOLE,
        compiler_params=params(),
        name="join",
    )(*parts)


def project_kernel(acts_ref, *refs):
    *weights, out_ref = refs
    tile = 256
    depth, width = weights[0].shape
    for q in range(2):
        for row in range(0, out_ref.shape[0], tile):
            rows = slice(row, row + tile)
            total = jnp.dot(
                acts_ref[rows, :depth], weights[2 * q][...], preferred_element_type=F32
            ) + jnp.dot(
                acts_ref[rows, depth : 2 * depth],
                weights[2 * q + 1][...],
                preferred_element_type=F32,
            )
            out_ref[rows, q * width : (q + 1) * width] = total.astype(BF16)


def project(acts, weights):
    rows, (depth, width) = acts.shape[0], weights[0].shape
    return pl.pallas_call(
        project_kernel,
        out_shape=jax.ShapeDtypeStruct((rows, 2 * width), BF16),
        in_specs=[WHOLE] * 5,
        out_specs=WHOLE,
        compiler_params=params(),
        cost_estimate=pl.CostEstimate(
            flops=16 * rows * depth * width, bytes_accessed=16 << 20, transcendentals=0
        ),
        name="project",
    )(acts, *weights)


def stats_kernel(*refs):
    acts, outs = refs[: len(SPLIT)], refs[len(SPLIT) + 1 :]
    width = outs[0].shape[0]
    for j, out in enumerate(outs):
        total = None
        for ref in acts:
            term = lax.dot_general(
                ref[:, j * width : (j + 1) * width],
                ref[:, 8 * width :],
                (((0,), (0,)), ((), ())),
                preferred_element_type=F32,
            )
            total = term if total is None else total + term
        out[...] = total.astype(out.dtype)


def stats(acts, after):
    width = 2 * BLOCK
    return pl.pallas_call(
        stats_kernel,
        out_shape=(jax.ShapeDtypeStruct((width, width), F32),)
        + (jax.ShapeDtypeStruct((width, width), BF16),) * 3,
        in_specs=[WHOLE] * len(acts) + [LEFT],
        out_specs=(WHOLE,) * 4,
        compiler_params=params(),
        name="stats",
    )(*acts, after)


def finish_kernel(core_ref, *refs):
    *parts, float_ref, quant_ref = refs
    core = core_ref[0]
    row = 0
    for ref in parts:
        rows, width = slice(row, row + ref.shape[1]), ref.shape[2] // 2
        row = rows.stop
        for q in range(2):
            quarter = core if q == 0 else 1 - core
            for kind, out in enumerate((float_ref, quant_ref)):
                for half in range(2):
                    at = kind * 8 + half * 4
                    cols = slice(q * width, (q + 1) * width)
                    total = ref[at, :, cols].astype(F32)
                    for x in range(1, 4):
                        total += ref[at + x, :, cols].astype(F32)
                    start = pl.multiple_of((half * 2 + quarter) * width, width)
                    out[rows, pl.ds(start, width)] = total.astype(BF16)


def finish(core, parts):
    tokens = sum(p.shape[1] for p in parts)
    return pl.pallas_call(
        finish_kernel,
        out_shape=(jax.ShapeDtypeStruct((tokens, 2 * parts[0].shape[2]), BF16),) * 2,
        in_specs=[SCALAR] + [WHOLE] * len(parts),
        out_specs=(WHOLE, WHOLE),
        compiler_params=params(),
        name="finish",
    )(core.reshape(1), *parts)


def swap(a, axis):
    return lax.ppermute(a, axis, [(0, 1), (1, 0)])


def ahead(a, axis, j):
    return lax.ppermute(a, axis, [((i + j) % 4, i) for i in range(4)])


def shards(attn_float, attn_quant, proj_weight, weight_codes, group_scales):
    tokens, d_in = attn_float.shape
    features, d_out = proj_weight.shape
    groups = group_scales.shape[0]
    half, quarter = d_out // 2, d_out // 4
    inverse = 1.0 / (tokens * 128)
    yh, core, yl, z = (lax.axis_index(a) for a in ("yh", "core", "yl", "z"))

    def weight(kind, col):
        plain = lax.dynamic_slice_in_dim(proj_weight, col, quarter, 1)
        codes = lax.dynamic_slice_in_dim(weight_codes, col, quarter, 1)
        scales = lax.dynamic_slice_in_dim(group_scales, col, quarter, 1)
        values = (codes - 8).astype(F32).reshape(groups, features // groups, quarter)
        quant = (values * scales[:, None, :]).reshape(features, quarter).astype(BF16)
        return jnp.where(kind == 0, plain, quant)

    own = weight(yh, yl * half + core * quarter)
    send = weight(yh ^ core, (1 - yl) * half + core * quarter)
    pairs = []
    for a in range(2):
        for c in range(2):
            for b in range(2):
                pairs.append((a * 4 + c * 2 + b, (a ^ c) * 4 + c * 2 + (1 - b)))
    got = lax.ppermute(send, ("yh", "core", "yl"), pairs)

    payload1, payload2 = pack(z, attn_float, attn_quant, send)

    def gather(rows):
        parts = join([rows] + [ahead(rows, "z", j) for j in (1, 2, 3)])
        return parts, swap(parts, "core")

    mine_own, other_own = gather(own)
    mine_got, other_got = gather(got)
    weights = (mine_own, mine_got, other_own, other_got)

    def exchange(p):
        return lax.all_to_all(p, PLANE, 0, 0, tiled=True)

    acts1 = exchange(payload1).reshape(16 * SPLIT[0], -1)
    payload2, acts1 = lax.optimization_barrier((payload2, acts1))
    acts2 = exchange(payload2).reshape(16 * SPLIT[1], -1)

    partial1 = project(acts1, weights)
    partial1, acts2 = lax.optimization_barrier((partial1, acts2))
    result1 = exchange(partial1.reshape(16, SPLIT[0], half))
    partial2 = project(acts2, weights)

    blocks = stats((acts1, acts2), partial2)
    total = blocks[0]
    for j in (1, 2, 3):
        total = total + ahead(blocks[j], "z", 4 - j).astype(F32)
    total = (total + swap(total, "core")) * inverse

    piece = swap(lax.dynamic_slice_in_dim(total, core * BLOCK, BLOCK, 0), "yh")
    partial2, piece, result1 = lax.optimization_barrier((partial2, piece, result1))
    result2 = exchange(partial2.reshape(16, SPLIT[1], half))
    again = swap(piece, "core")
    moved = jnp.where(
        core == 0, jnp.concatenate([piece, again]), jnp.concatenate([again, piece])
    )
    total = jnp.where(yh == 1, total, moved)
    float_out, quant_out = finish(core, (result1, result2))
    return float_out, quant_out, total[:, :BLOCK], total[:, BLOCK:]


def solution(mesh):
    fine = Mesh(mesh.devices.reshape(2, 2, 2, 4, 4), FINE)
    rows, tok = P(FINE, None), P(("yl", "z", "x"), None)
    return jax.shard_map(
        shards,
        mesh=fine,
        in_specs=(rows, rows, tok, tok, tok),
        out_specs=(rows, rows, tok, tok),
        check_vma=False,
    )
```

```python
import functools

import jax
import jax.numpy as jnp
from jax import lax
from jax.experimental import pallas as pl
from jax.experimental.pallas import tpu as pltpu
from jax.sharding import Mesh
from jax.sharding import PartitionSpec as P

BLOCK = 128
GROUPS = (
    ((0, 1), (0, 3), (1, 0), (3, 0)),
    ((1, 1), (3, 3), (1, 3), (3, 1)),
    ((1, 2), (3, 2), (2, 1), (2, 3)),
    ((0, 2), (2, 0), (2, 2), (0, 0)),
)
FINE = ("yh", "core", "yl", "z", "x")
PLANE = ("yh", "yl", "x")
F32 = jnp.float32
BF16 = jnp.bfloat16


WHOLE = pl.BlockSpec(memory_space=pltpu.VMEM)
LEFT = pl.BlockSpec(memory_space=pl.ANY)
SCALAR = pl.BlockSpec(memory_space=pltpu.SMEM)


def params():
    return pltpu.CompilerParams(vmem_limit_bytes=16 << 20)


def pack_kernel(z_ref, float_ref, quant_ref, after_ref, out_ref):
    width = float_ref.shape[1] // 32
    z = z_ref[0]
    quant = quant_ref[:, :BLOCK]
    shift = (float_ref[:, :BLOCK].astype(F32) - quant.astype(F32)).astype(BF16)
    for kind, ref in enumerate((float_ref, quant_ref)):
        for j in range(4):
            zj = lax.rem(z + j, 4)
            for yl in range(2):
                for x in range(4):
                    start = pl.multiple_of(((yl * 4 + zj) * 4 + x) * width, width)
                    block = ref[:, pl.ds(start, width)]
                    for half in range(2):
                        at = ((yl ^ half) * 4 + j) * width
                        out_ref[kind * 8 + half * 4 + x, :, at : at + width] = block
    for d in range(16):
        out_ref[d, :, 8 * width : 8 * width + BLOCK] = quant
        out_ref[d, :, 8 * width + BLOCK :] = shift


def pack(z, attn_float, attn_quant, after):
    tokens, d_in = attn_float.shape
    return pl.pallas_call(
        pack_kernel,
        out_shape=jax.ShapeDtypeStruct((16, tokens, d_in // 4 + 2 * BLOCK), BF16),
        in_specs=[SCALAR, WHOLE, WHOLE, LEFT],
        out_specs=WHOLE,
        compiler_params=params(),
        name="pack",
    )(z.reshape(1), attn_float, attn_quant, after)


def join_kernel(*refs):
    *parts, out_ref = refs
    row = 0
    for part in parts:
        out_ref[row : row + part.shape[0]] = part[...]
        row += part.shape[0]


def join(parts):
    rows, cols = parts[0].shape
    return pl.pallas_call(
        join_kernel,
        out_shape=jax.ShapeDtypeStruct((len(parts) * rows, cols), BF16),
        in_specs=[WHOLE] * len(parts),
        out_specs=WHOLE,
        compiler_params=params(),
        name="join",
    )(*parts)


def project_kernel(group, at_ref, acts_ref, *refs):
    weights, outs, rows_ref, part_ref = refs[:4], refs[-6:-2], refs[-2], refs[-1]
    y, x = at_ref[0], at_ref[1]
    depth, width = weights[0].shape
    tokens = outs[0].shape[0]
    for n, (dy, dx) in enumerate(group):
        start = (lax.rem(y + dy, 4) * 4 + lax.rem(x + dx, 4)) * tokens
        rows_ref[n * tokens : (n + 1) * tokens] = acts_ref[
            pl.ds(pl.multiple_of(start, tokens), tokens), : 2 * depth
        ]
    for q in range(2):
        cols = slice(q * width, (q + 1) * width)
        total = jnp.dot(
            rows_ref[:, :depth], weights[2 * q][...], preferred_element_type=F32
        ) + jnp.dot(rows_ref[:, depth:], weights[2 * q + 1][...], preferred_element_type=F32)
        part_ref[...] = total.astype(BF16)
        for n, out in enumerate(outs):
            out[:, cols] = part_ref[n * tokens : (n + 1) * tokens]


def project(group, at, acts, weights, after):
    depth, width = weights[0].shape
    tokens = acts.shape[0] // 16
    return pl.pallas_call(
        functools.partial(project_kernel, group),
        out_shape=(jax.ShapeDtypeStruct((tokens, 2 * width), BF16),) * 4,
        in_specs=[SCALAR] + [WHOLE] * 5 + [LEFT] * len(after),
        out_specs=(WHOLE,) * 4,
        scratch_shapes=[
            pltpu.VMEM((4 * tokens, 2 * depth), BF16),
            pltpu.VMEM((4 * tokens, width), BF16),
        ],
        compiler_params=params(),
        cost_estimate=pl.CostEstimate(
            flops=32 * tokens * depth * width, bytes_accessed=10 << 20, transcendentals=0
        ),
        name="project",
    )(at, acts, *weights, *after)


def stats_kernel(acts_ref, after_ref, *outs):
    width = outs[0].shape[0]
    for j, out in enumerate(outs):
        out[...] = lax.dot_general(
            acts_ref[:, j * width : (j + 1) * width],
            acts_ref[:, 8 * width :],
            (((0,), (0,)), ((), ())),
            preferred_element_type=F32,
        ).astype(out.dtype)


def stats(acts, after):
    width = 2 * BLOCK
    return pl.pallas_call(
        stats_kernel,
        out_shape=(jax.ShapeDtypeStruct((width, width), F32),)
        + (jax.ShapeDtypeStruct((width, width), BF16),) * 3,
        in_specs=[WHOLE, LEFT],
        out_specs=(WHOLE,) * 4,
        compiler_params=params(),
        name="stats",
    )(acts, after)


def finish_kernel(at_ref, *refs):
    parts, outs = refs[:16], refs[16:]
    y, core = at_ref[0], at_ref[1]
    width = parts[0].shape[1] // 2
    for dy in range(4):
        source = lax.rem(y + 4 - dy, 4)
        for q in range(2):
            cols = slice(q * width, (q + 1) * width)
            quarter = core if q == 0 else 1 - core
            start = pl.multiple_of(((source & 1) * 2 + quarter) * width, width)
            total = parts[4 * dy][:, cols].astype(F32)
            for dx in range(1, 4):
                total += parts[4 * dy + dx][:, cols].astype(F32)
            total = total.astype(BF16)
            for kind, out in enumerate(outs):

                @pl.when((source >> 1) == kind)
                def _(out=out, start=start, total=total):
                    out[:, pl.ds(start, width)] = total


def finish(at, parts):
    tokens, width = parts[0].shape
    return pl.pallas_call(
        finish_kernel,
        out_shape=(jax.ShapeDtypeStruct((tokens, 2 * width), BF16),) * 2,
        in_specs=[SCALAR] + [WHOLE] * 16,
        out_specs=(WHOLE, WHOLE),
        compiler_params=params(),
        name="finish",
    )(at, *parts)


def swap(a, axis):
    return lax.ppermute(a, axis, [(0, 1), (1, 0)])


def ahead(a, axis, j):
    return lax.ppermute(a, axis, [((i + j) % 4, i) for i in range(4)])


def shards(attn_float, attn_quant, proj_weight, weight_codes, group_scales):
    tokens, d_in = attn_float.shape
    features, d_out = proj_weight.shape
    groups = group_scales.shape[0]
    half, quarter = d_out // 2, d_out // 4
    inverse = 1.0 / (tokens * 128)
    yh, core, yl, z = (lax.axis_index(a) for a in ("yh", "core", "yl", "z"))

    def weight(kind, col):
        plain = lax.dynamic_slice_in_dim(proj_weight, col, quarter, 1)
        codes = lax.dynamic_slice_in_dim(weight_codes, col, quarter, 1)
        scales = lax.dynamic_slice_in_dim(group_scales, col, quarter, 1)
        values = (codes - 8).astype(F32).reshape(groups, features // groups, quarter)
        quant = (values * scales[:, None, :]).reshape(features, quarter).astype(BF16)
        return jnp.where(kind == 0, plain, quant)

    send = weight(yh ^ core, (1 - yl) * half + core * quarter)
    pairs = []
    for a in range(2):
        for c in range(2):
            for b in range(2):
                pairs.append((a * 4 + c * 2 + b, (a ^ c) * 4 + c * 2 + (1 - b)))
    got = lax.ppermute(send, ("yh", "core", "yl"), pairs)
    col, send = lax.optimization_barrier((yl * half + core * quarter, send))
    own = weight(yh, col)

    payload = pack(z, attn_float, attn_quant, send)
    payload, got = lax.optimization_barrier((payload, got))

    def gather(rows):
        parts = join([rows] + [ahead(rows, "z", j) for j in (1, 2, 3)])
        return parts, swap(parts, "core")

    mine_own, other_own = gather(own)
    mine_got, other_got = gather(got)
    weights = (mine_own, mine_got, other_own, other_got)

    acts = lax.all_to_all(payload, PLANE, 0, 0, tiled=True).reshape(16 * tokens, -1)

    y, x = yh * 2 + yl, lax.axis_index("x")
    arrived, after = {}, [(), ()]
    for n, group in enumerate(GROUPS):
        partials = project(group, jnp.stack([y, x]), acts, weights, after[n])
        if n == 1:
            blocks = stats(acts, partials[0])
        for (dy, dx), partial in zip(group, partials):
            if (dy, dx) != (0, 0):
                to = [
                    (i * 4 + j, (i + dy) % 4 * 4 + (j + dx) % 4)
                    for i in range(4)
                    for j in range(4)
                ]
                partial = lax.ppermute(partial, PLANE, to)
            arrived[dy, dx] = partial
        after.append((arrived[group[0]], arrived[group[1]]))
    results = [arrived[dy, dx] for dy in range(4) for dx in range(4)]
    float_out, quant_out = finish(jnp.stack([y, core]), results)

    total = blocks[0]
    for j in (1, 2, 3):
        total = total + ahead(blocks[j], "z", 4 - j).astype(F32)
    total = (total + swap(total, "core")) * inverse

    piece = swap(lax.dynamic_slice_in_dim(total, core * BLOCK, BLOCK, 0), "yh")
    again = swap(piece, "core")
    moved = jnp.where(
        core == 0, jnp.concatenate([piece, again]), jnp.concatenate([again, piece])
    )
    total = jnp.where(yh == 1, total, moved)
    return float_out, quant_out, total[:, :BLOCK], total[:, BLOCK:]


def solution(mesh):
    fine = Mesh(mesh.devices.reshape(2, 2, 2, 4, 4), FINE)
    rows, tok = P(FINE, None), P(("yl", "z", "x"), None)
    return jax.shard_map(
        shards,
        mesh=fine,
        in_specs=(rows, rows, tok, tok, tok),
        out_specs=(rows, rows, tok, tok),
        check_vma=False,
    )
```

```python
import jax
import jax.numpy as jnp
from jax import lax
from jax.experimental import pallas as pl
from jax.experimental.pallas import tpu as pltpu
from jax.sharding import Mesh
from jax.sharding import PartitionSpec as P

BLOCK = 128
FINE = ("yh", "core", "yl", "z", "x")
PLANE = ("yh", "yl", "x")
F32 = jnp.float32
BF16 = jnp.bfloat16


WHOLE = pl.BlockSpec(memory_space=pltpu.VMEM)
SCALAR = pl.BlockSpec(memory_space=pltpu.SMEM)


def params():
    return pltpu.CompilerParams(vmem_limit_bytes=16 << 20)


def pack_kernel(z_ref, float_ref, quant_ref, out_ref):
    width = out_ref.shape[2] // 8
    z = z_ref[0]
    for kind, ref in enumerate((float_ref, quant_ref)):
        for j in range(4):
            zj = lax.rem(z + j, 4)
            for yl in range(2):
                for x in range(4):
                    start = pl.multiple_of(((yl * 4 + zj) * 4 + x) * width, width)
                    block = ref[:, pl.ds(start, width)]
                    for half in range(2):
                        at = (j * 2 + (yl ^ half)) * width
                        out_ref[kind * 8 + half * 4 + x, :, at : at + width] = block


def pack(z, attn_float, attn_quant):
    tokens, d_in = attn_float.shape
    return pl.pallas_call(
        pack_kernel,
        out_shape=jax.ShapeDtypeStruct((16, tokens, d_in // 4), BF16),
        in_specs=[SCALAR, WHOLE, WHOLE],
        out_specs=WHOLE,
        compiler_params=params(),
        name="pack",
    )(z.reshape(1), attn_float, attn_quant)


def finish_kernel(core_ref, first_ref, second_ref, float_ref, quant_ref):
    core = core_ref[0]
    width = first_ref.shape[2]
    for n, ref in enumerate((first_ref, second_ref)):
        quarter = core if n == 0 else 1 - core
        for kind, out in enumerate((float_ref, quant_ref)):
            for half in range(2):
                at = kind * 8 + half * 4
                total = ref[at].astype(F32)
                for x in range(1, 4):
                    total += ref[at + x].astype(F32)
                start = pl.multiple_of((half * 2 + quarter) * width, width)
                out[:, pl.ds(start, width)] = total.astype(BF16)


def finish(core, first, second):
    _, tokens, width = first.shape
    return pl.pallas_call(
        finish_kernel,
        out_shape=(jax.ShapeDtypeStruct((tokens, 4 * width), BF16),) * 2,
        in_specs=[SCALAR, WHOLE, WHOLE],
        out_specs=(WHOLE, WHOLE),
        compiler_params=params(),
        name="finish",
    )(core.reshape(1), first, second)


def stats_kernel(at_ref, acts_ref, *refs):
    pieces, outs, block_ref = refs[:4], refs[4:8], refs[8]
    y, x = at_ref[0], at_ref[1]
    tokens = pieces[0].shape[0] // 4
    for dy, piece in enumerate(pieces):
        for dx in range(4):
            start = (lax.rem(y + dy, 4) * 4 + lax.rem(x + dx, 4)) * tokens
            block_ref[pl.ds(pl.multiple_of(start, tokens), tokens)] = piece[
                dx * tokens : (dx + 1) * tokens
            ]
    width = outs[0].shape[0]
    for j, out in enumerate(outs):
        out[...] = lax.dot_general(
            acts_ref[:, 2 * j * width : (2 * j + 1) * width],
            block_ref[...],
            (((0,), (0,)), ((), ())),
            preferred_element_type=F32,
        ).astype(out.dtype)


def stats(at, acts, pieces):
    width = 2 * BLOCK
    return pl.pallas_call(
        stats_kernel,
        out_shape=(jax.ShapeDtypeStruct((width, width), F32),)
        + (jax.ShapeDtypeStruct((width, width), BF16),) * 3,
        in_specs=[SCALAR] + [WHOLE] * 5,
        out_specs=(WHOLE,) * 4,
        scratch_shapes=[pltpu.VMEM((acts.shape[0], width), BF16)],
        compiler_params=params(),
        name="stats",
    )(at, acts, *pieces)


def swap(a, axis):
    return lax.ppermute(a, axis, [(0, 1), (1, 0)])


def ahead(a, axis, j):
    return lax.ppermute(a, axis, [((i + j) % 4, i) for i in range(4)])


def shards(attn_float, attn_quant, proj_weight, weight_codes, group_scales):
    tokens, d_in = attn_float.shape
    features, d_out = proj_weight.shape
    groups = group_scales.shape[0]
    half, quarter = d_out // 2, d_out // 4
    inverse = 1.0 / (tokens * 128)
    yh, core, yl, z = (lax.axis_index(a) for a in ("yh", "core", "yl", "z"))

    def weight(kind, col):
        plain = lax.dynamic_slice_in_dim(proj_weight, col, quarter, 1)
        codes = lax.dynamic_slice_in_dim(weight_codes, col, quarter, 1)
        scales = lax.dynamic_slice_in_dim(group_scales, col, quarter, 1)
        values = (codes - 8).astype(F32).reshape(groups, features // groups, quarter)
        quant = (values * scales[:, None, :]).reshape(features, quarter).astype(BF16)
        return jnp.where(kind == 0, plain, quant)

    quant = attn_quant[:, :BLOCK]
    shift = (attn_float[:, :BLOCK].astype(F32) - quant.astype(F32)).astype(BF16)
    block = jnp.concatenate([quant, shift], axis=1)
    line = jnp.concatenate([block] + [ahead(block, "x", j) for j in (1, 2, 3)], axis=0)
    pieces = [line] + [ahead(line, ("yh", "yl"), j) for j in (1, 2, 3)]

    send = weight(yh ^ core, (1 - yl) * half + core * quarter)
    pairs = []
    for a in range(2):
        for c in range(2):
            for b in range(2):
                pairs.append((a * 4 + c * 2 + b, (a ^ c) * 4 + c * 2 + (1 - b)))
    got = lax.ppermute(send, ("yh", "core", "yl"), pairs)
    col, send = lax.optimization_barrier((yl * half + core * quarter, send))
    own = weight(yh, col)

    payload = pack(z, attn_float, attn_quant)
    payload, got, *pieces = lax.optimization_barrier((payload, got, *pieces))

    acts = lax.all_to_all(payload, PLANE, 0, 0, tiled=True).reshape(16 * tokens, 8 * features)

    rows = jnp.concatenate([own, got], axis=0)
    parts = [rows] + [ahead(rows, "z", j) for j in (1, 2, 3)]
    mine = jnp.concatenate(parts, axis=0)
    other = swap(mine, "core")

    def part(w):
        return jnp.dot(acts, w, preferred_element_type=F32).astype(BF16)

    def output(p):
        return lax.all_to_all(p.reshape(16, tokens, quarter), PLANE, 0, 0, tiled=True)

    result1 = output(part(mine))
    second = part(other)

    acts1, second = lax.optimization_barrier((acts, second))
    blocks = stats(jnp.stack([yh * 2 + yl, lax.axis_index("x")]), acts1, pieces)
    result2 = output(second)
    total = blocks[0]
    for j in (1, 2, 3):
        total = total + ahead(blocks[j], "z", 4 - j).astype(F32)
    total = (total + swap(total, "core")) * inverse

    piece = swap(lax.dynamic_slice_in_dim(total, core * BLOCK, BLOCK, 0), "yh")
    again = swap(piece, "core")
    moved = jnp.where(
        core == 0, jnp.concatenate([piece, again]), jnp.concatenate([again, piece])
    )
    total = jnp.where(yh == 1, total, moved)
    float_out, quant_out = finish(core, result1, result2)
    return float_out, quant_out, total[:, :BLOCK], total[:, BLOCK:]


def solution(mesh):
    fine = Mesh(mesh.devices.reshape(2, 2, 2, 4, 4), FINE)
    rows, tok = P(FINE, None), P(("yl", "z", "x"), None)
    return jax.shard_map(
        shards,
        mesh=fine,
        in_specs=(rows, rows, tok, tok, tok),
        out_specs=(rows, rows, tok, tok),
        check_vma=False,
    )
```

```python
import functools

import jax
import jax.numpy as jnp
from jax import lax
from jax.experimental import pallas as pl
from jax.experimental.pallas import tpu as pltpu
from jax.sharding import Mesh
from jax.sharding import PartitionSpec as P

BLOCK = 128
FIRST = 512
FINE = ("yh", "core", "yl", "z", "x")
PLANE = ("yh", "yl", "x")
F32 = jnp.float32
BF16 = jnp.bfloat16


WHOLE = pl.BlockSpec(memory_space=pltpu.VMEM)
SCALAR = pl.BlockSpec(memory_space=pltpu.SMEM)


def params():
    return pltpu.CompilerParams(vmem_limit_bytes=16 << 20)


def pack_kernel(z_ref, float_ref, quant_ref, out_ref):
    width = out_ref.shape[2] // 8
    z = z_ref[0]
    for kind, ref in enumerate((float_ref, quant_ref)):
        for j in range(4):
            zj = lax.rem(z + j, 4)
            for yl in range(2):
                for x in range(4):
                    start = pl.multiple_of(((yl * 4 + zj) * 4 + x) * width, width)
                    block = ref[:, pl.ds(start, width)]
                    for half in range(2):
                        at = (j * 2 + (yl ^ half)) * width
                        out_ref[kind * 8 + half * 4 + x, :, at : at + width] = block


def pack(z, attn_float, attn_quant):
    tokens, d_in = attn_float.shape
    return pl.pallas_call(
        pack_kernel,
        out_shape=jax.ShapeDtypeStruct((16, tokens, d_in // 4), BF16),
        in_specs=[SCALAR, WHOLE, WHOLE],
        out_specs=WHOLE,
        compiler_params=params(),
        name="pack",
    )(z.reshape(1), attn_float, attn_quant)


def join_kernel(*refs):
    *parts, out_ref = refs
    row = 0
    for part in parts:
        out_ref[row : row + part.shape[0]] = part[...]
        row += part.shape[0]


def join(parts):
    cols = parts[0].shape[1]
    return pl.pallas_call(
        join_kernel,
        out_shape=jax.ShapeDtypeStruct((sum(p.shape[0] for p in parts), cols), BF16),
        in_specs=[WHOLE] * len(parts),
        out_specs=WHOLE,
        compiler_params=params(),
        name="join",
    )(*parts)


def project_kernel(first, acts_ref, *refs):
    *weights, out_ref = refs
    at = 0
    for n, ref in enumerate(weights):
        for col in range(first if n == 0 else 0, ref.shape[1], FIRST):
            for row in range(0, acts_ref.shape[0], 256):
                out_ref[row : row + 256, at : at + FIRST] = jnp.dot(
                    acts_ref[row : row + 256, :],
                    ref[:, col : col + FIRST],
                    preferred_element_type=F32,
                ).astype(BF16)
            at += FIRST


def project(acts, weights, first):
    rows, depth = acts.shape
    cols = sum(w.shape[1] for w in weights) - first
    return pl.pallas_call(
        functools.partial(project_kernel, first),
        out_shape=jax.ShapeDtypeStruct((rows, cols), BF16),
        in_specs=[WHOLE] * (1 + len(weights)),
        out_specs=WHOLE,
        compiler_params=params(),
        cost_estimate=pl.CostEstimate(
            flops=2 * rows * depth * cols, bytes_accessed=14 << 20, transcendentals=0
        ),
        name="project",
    )(acts, *weights)


def finish_kernel(core_ref, first_ref, second_ref, float_ref, quant_ref):
    core = core_ref[0]
    quarter = float_ref.shape[1] // 4
    pieces = [(first_ref, 0, FIRST, core, 0), (second_ref, 0, quarter - FIRST, core, FIRST)]
    pieces.append((second_ref, quarter - FIRST, quarter, 1 - core, 0))
    for ref, col, width, place, shift in pieces:
        for kind, out in enumerate((float_ref, quant_ref)):
            for half in range(2):
                at = kind * 8 + half * 4
                cols = slice(col, col + width)
                total = ref[at, :, cols].astype(F32)
                for x in range(1, 4):
                    total += ref[at + x, :, cols].astype(F32)
                start = pl.multiple_of((half * 2 + place) * quarter + shift, FIRST)
                out[:, pl.ds(start, width)] = total.astype(BF16)


def finish(core, first, second):
    tokens = first.shape[1]
    cols = 2 * (first.shape[2] + second.shape[2])
    return pl.pallas_call(
        finish_kernel,
        out_shape=(jax.ShapeDtypeStruct((tokens, cols), BF16),) * 2,
        in_specs=[SCALAR, WHOLE, WHOLE],
        out_specs=(WHOLE, WHOLE),
        compiler_params=params(),
        name="finish",
    )(core.reshape(1), first, second)


def stats_kernel(at_ref, acts_ref, *refs):
    pieces, outs, block_ref = refs[:4], refs[4:8], refs[8]
    y, x = at_ref[0], at_ref[1]
    tokens = pieces[0].shape[0] // 4
    for dy, piece in enumerate(pieces):
        for dx in range(4):
            start = (lax.rem(y + dy, 4) * 4 + lax.rem(x + dx, 4)) * tokens
            block_ref[pl.ds(pl.multiple_of(start, tokens), tokens)] = piece[
                dx * tokens : (dx + 1) * tokens
            ]
    width = outs[0].shape[0]
    for j, out in enumerate(outs):
        out[...] = lax.dot_general(
            acts_ref[:, 2 * j * width : (2 * j + 1) * width],
            block_ref[...],
            (((0,), (0,)), ((), ())),
            preferred_element_type=F32,
        ).astype(out.dtype)


def stats(at, acts, pieces):
    width = 2 * BLOCK
    return pl.pallas_call(
        stats_kernel,
        out_shape=(jax.ShapeDtypeStruct((width, width), F32),)
        + (jax.ShapeDtypeStruct((width, width), BF16),) * 3,
        in_specs=[SCALAR] + [WHOLE] * 5,
        out_specs=(WHOLE,) * 4,
        scratch_shapes=[pltpu.VMEM((acts.shape[0], width), BF16)],
        compiler_params=params(),
        name="stats",
    )(at, acts, *pieces)


def swap(a, axis):
    return lax.ppermute(a, axis, [(0, 1), (1, 0)])


def ahead(a, axis, j):
    return lax.ppermute(a, axis, [((i + j) % 4, i) for i in range(4)])


def shards(attn_float, attn_quant, proj_weight, weight_codes, group_scales):
    tokens, d_in = attn_float.shape
    features, d_out = proj_weight.shape
    groups = group_scales.shape[0]
    half, quarter = d_out // 2, d_out // 4
    inverse = 1.0 / (tokens * 128)
    yh, core, yl, z = (lax.axis_index(a) for a in ("yh", "core", "yl", "z"))

    def weight(kind, col):
        plain = lax.dynamic_slice_in_dim(proj_weight, col, quarter, 1)
        codes = lax.dynamic_slice_in_dim(weight_codes, col, quarter, 1)
        scales = lax.dynamic_slice_in_dim(group_scales, col, quarter, 1)
        values = (codes - 8).astype(F32).reshape(groups, features // groups, quarter)
        quant = (values * scales[:, None, :]).reshape(features, quarter).astype(BF16)
        return jnp.where(kind == 0, plain, quant)

    send = weight(yh ^ core, (1 - yl) * half + core * quarter)
    pairs = []
    for a in range(2):
        for c in range(2):
            for b in range(2):
                pairs.append((a * 4 + c * 2 + b, (a ^ c) * 4 + c * 2 + (1 - b)))
    got = lax.ppermute(send, ("yh", "core", "yl"), pairs)
    col, send = lax.optimization_barrier((yl * half + core * quarter, send))
    own = weight(yh, col)

    payload = pack(z, attn_float, attn_quant)
    payload, got = lax.optimization_barrier((payload, got))

    acts = lax.all_to_all(payload, PLANE, 0, 0, tiled=True).reshape(16 * tokens, 8 * features)

    rows = join((own, got))
    mine = join([rows] + [ahead(rows, "z", j) for j in (1, 2, 3)])
    other = swap(mine, "core")

    quant = attn_quant[:, :BLOCK]
    shift = (attn_float[:, :BLOCK].astype(F32) - quant.astype(F32)).astype(BF16)
    block = jnp.concatenate([quant, shift], axis=1)
    block, mine = lax.optimization_barrier((block, mine))
    line = jnp.concatenate([block] + [ahead(block, "x", j) for j in (1, 2, 3)], axis=0)

    def output(p):
        return lax.all_to_all(p.reshape(16, tokens, -1), PLANE, 0, 0, tiled=True)

    first = jnp.dot(acts, mine[:, :FIRST], preferred_element_type=F32).astype(BF16)
    line, first = lax.optimization_barrier((line, first))
    result1 = output(first)
    pieces = [line] + [ahead(line, ("yh", "yl"), j) for j in (1, 2, 3)]
    second = project(acts, (mine, other), FIRST)
    second, result1, *pieces = lax.optimization_barrier((second, result1, *pieces))
    result2 = output(second)

    blocks = stats(jnp.stack([yh * 2 + yl, lax.axis_index("x")]), acts, pieces)
    total = blocks[0]
    for j in (1, 2, 3):
        total = total + ahead(blocks[j], "z", 4 - j).astype(F32)
    total = (total + swap(total, "core")) * inverse

    piece = swap(lax.dynamic_slice_in_dim(total, core * BLOCK, BLOCK, 0), "yh")
    again = swap(piece, "core")
    moved = jnp.where(
        core == 0, jnp.concatenate([piece, again]), jnp.concatenate([again, piece])
    )
    total = jnp.where(yh == 1, total, moved)
    float_out, quant_out = finish(core, result1, result2)
    return float_out, quant_out, total[:, :BLOCK], total[:, BLOCK:]


def solution(mesh):
    fine = Mesh(mesh.devices.reshape(2, 2, 2, 4, 4), FINE)
    rows, tok = P(FINE, None), P(("yl", "z", "x"), None)
    return jax.shard_map(
        shards,
        mesh=fine,
        in_specs=(rows, rows, tok, tok, tok),
        out_specs=(rows, rows, tok, tok),
        check_vma=False,
    )
```

```python
import jax
import jax.numpy as jnp
from jax import lax
from jax.experimental import pallas as pl
from jax.experimental.pallas import tpu as pltpu
from jax.sharding import Mesh
from jax.sharding import PartitionSpec as P

BLOCK = 128
FINE = ("yh", "core", "yl", "z", "x")
PLANE = ("yh", "yl", "x")
F32 = jnp.float32
BF16 = jnp.bfloat16


WHOLE = pl.BlockSpec(memory_space=pltpu.VMEM)
LEFT = pl.BlockSpec(memory_space=pl.ANY)
SCALAR = pl.BlockSpec(memory_space=pltpu.SMEM)


def params():
    return pltpu.CompilerParams(vmem_limit_bytes=16 << 20)


def pack_kernel(z_ref, float_ref, quant_ref, out_ref):
    width = out_ref.shape[2] // 8
    z = z_ref[0]
    for kind, ref in enumerate((float_ref, quant_ref)):
        for j in range(4):
            zj = lax.rem(z + j, 4)
            for yl in range(2):
                for x in range(4):
                    start = pl.multiple_of(((yl * 4 + zj) * 4 + x) * width, width)
                    block = ref[:, pl.ds(start, width)]
                    for half in range(2):
                        at = (j * 2 + (yl ^ half)) * width
                        out_ref[kind * 8 + half * 4 + x, :, at : at + width] = block


def pack(z, attn_float, attn_quant):
    tokens, d_in = attn_float.shape
    return pl.pallas_call(
        pack_kernel,
        out_shape=jax.ShapeDtypeStruct((16, tokens, d_in // 4), BF16),
        in_specs=[SCALAR, WHOLE, WHOLE],
        out_specs=WHOLE,
        compiler_params=params(),
        name="pack",
    )(z.reshape(1), attn_float, attn_quant)


def project_kernel(acts_ref, *refs):
    *weights, out_ref = refs
    depth, width = weights[0].shape
    tile = 512
    for q in range(2):
        for col in range(0, width, tile):
            for row in range(0, acts_ref.shape[0], 256):
                rows, total = slice(row, row + 256), None
                for j in range(4):
                    term = jnp.dot(
                        acts_ref[rows, j * depth : (j + 1) * depth],
                        weights[4 * q + j][:, col : col + tile],
                        preferred_element_type=F32,
                    )
                    total = term if total is None else total + term
                at = q * width + col
                out_ref[rows, at : at + tile] = total.astype(BF16)


def project(acts, weights):
    rows, depth = acts.shape
    cols = 2 * weights[0].shape[1]
    return pl.pallas_call(
        project_kernel,
        out_shape=jax.ShapeDtypeStruct((rows, cols), BF16),
        in_specs=[WHOLE] * (1 + len(weights)),
        out_specs=WHOLE,
        compiler_params=params(),
        cost_estimate=pl.CostEstimate(
            flops=2 * rows * depth * cols, bytes_accessed=16 << 20, transcendentals=0
        ),
        name="project",
    )(acts, *weights)


def finish_kernel(at_ref, parts_ref, total_ref, moved_ref, *outs):
    core, yh = at_ref[0], at_ref[1]
    width = parts_ref.shape[2] // 2
    for q in range(2):
        quarter = core if q == 0 else 1 - core
        for kind, out in enumerate(outs[:2]):
            for half in range(2):
                at = kind * 8 + half * 4
                cols = slice(q * width, (q + 1) * width)
                total = parts_ref[at, :, cols].astype(F32)
                for x in range(1, 4):
                    total += parts_ref[at + x, :, cols].astype(F32)
                start = pl.multiple_of((half * 2 + quarter) * width, width)
                out[:, pl.ds(start, width)] = total.astype(BF16)
    total = jnp.where(yh == 1, total_ref[...], moved_ref[...])
    outs[2][...] = total[:, :BLOCK]
    outs[3][...] = total[:, BLOCK:]


def finish(at, parts, total, moved):
    tokens, cols = parts.shape[1:]
    rows = total.shape[0]
    return pl.pallas_call(
        finish_kernel,
        out_shape=(jax.ShapeDtypeStruct((tokens, 2 * cols), BF16),) * 2
        + (jax.ShapeDtypeStruct((rows, BLOCK), F32),) * 2,
        in_specs=[SCALAR] + [WHOLE] * 3,
        out_specs=(WHOLE,) * 4,
        compiler_params=params(),
        name="finish",
    )(at, parts, total, moved)


def stats_kernel(at_ref, acts_ref, *refs):
    pieces, outs, block_ref = refs[:4], refs[5:9], refs[9]
    y, x = at_ref[0], at_ref[1]
    tokens = pieces[0].shape[0] // 4
    for dy, piece in enumerate(pieces):
        for dx in range(4):
            start = (lax.rem(y + dy, 4) * 4 + lax.rem(x + dx, 4)) * tokens
            block_ref[pl.ds(pl.multiple_of(start, tokens), tokens)] = piece[
                dx * tokens : (dx + 1) * tokens
            ]
    width = outs[0].shape[0]
    for j, out in enumerate(outs):
        out[...] = lax.dot_general(
            acts_ref[:, 2 * j * width : (2 * j + 1) * width],
            block_ref[...],
            (((0,), (0,)), ((), ())),
            preferred_element_type=F32,
        ).astype(out.dtype)


def stats(at, acts, pieces, after):
    width = 2 * BLOCK
    return pl.pallas_call(
        stats_kernel,
        out_shape=(jax.ShapeDtypeStruct((width, width), F32),)
        + (jax.ShapeDtypeStruct((width, width), BF16),) * 3,
        in_specs=[SCALAR] + [WHOLE] * 5 + [LEFT],
        out_specs=(WHOLE,) * 4,
        scratch_shapes=[pltpu.VMEM((acts.shape[0], width), BF16)],
        compiler_params=params(),
        name="stats",
    )(at, acts, *pieces, after)


def swap(a, axis):
    return lax.ppermute(a, axis, [(0, 1), (1, 0)])


def ahead(a, axis, j):
    return lax.ppermute(a, axis, [((i + j) % 4, i) for i in range(4)])


def shards(attn_float, attn_quant, proj_weight, weight_codes, group_scales):
    tokens, d_in = attn_float.shape
    features, d_out = proj_weight.shape
    groups = group_scales.shape[0]
    half, quarter = d_out // 2, d_out // 4
    inverse = 1.0 / (tokens * 128)
    yh, core, yl, z = (lax.axis_index(a) for a in ("yh", "core", "yl", "z"))

    def weight(kind, col):
        plain = lax.dynamic_slice_in_dim(proj_weight, col, quarter, 1)
        codes = lax.dynamic_slice_in_dim(weight_codes, col, quarter, 1)
        scales = lax.dynamic_slice_in_dim(group_scales, col, quarter, 1)
        values = (codes - 8).astype(F32).reshape(groups, features // groups, quarter)
        quant = (values * scales[:, None, :]).reshape(features, quarter).astype(BF16)
        return jnp.where(kind == 0, plain, quant)

    send = weight(yh ^ core, (1 - yl) * half + core * quarter)
    pairs = []
    for a in range(2):
        for c in range(2):
            for b in range(2):
                pairs.append((a * 4 + c * 2 + b, (a ^ c) * 4 + c * 2 + (1 - b)))
    got = lax.ppermute(send, ("yh", "core", "yl"), pairs)
    col, send = lax.optimization_barrier((yl * half + core * quarter, send))
    own = weight(yh, col)

    payload = pack(z, attn_float, attn_quant)
    payload, got = lax.optimization_barrier((payload, got))

    acts = lax.all_to_all(payload, PLANE, 0, 0, tiled=True).reshape(16 * tokens, 8 * features)

    rows = jnp.concatenate([own, got], axis=0)
    parts = [rows] + [ahead(rows, "z", j) for j in (1, 2, 3)]
    weights = parts + [swap(p, "core") for p in parts]

    quant = attn_quant[:, :BLOCK]
    shift = (attn_float[:, :BLOCK].astype(F32) - quant.astype(F32)).astype(BF16)
    block = jnp.concatenate([quant, shift], axis=1)
    block, *parts = lax.optimization_barrier((block, *parts))
    line = jnp.concatenate([block] + [ahead(block, "x", j) for j in (1, 2, 3)], axis=0)
    line, acts = lax.optimization_barrier((line, acts))
    pieces = [line] + [ahead(line, ("yh", "yl"), j) for j in (1, 2, 3)]

    partial = project(acts, weights)
    partial, *pieces = lax.optimization_barrier((partial, *pieces))
    result = lax.all_to_all(partial.reshape(16, tokens, half), PLANE, 0, 0, tiled=True)

    blocks = stats(jnp.stack([yh * 2 + yl, lax.axis_index("x")]), acts, pieces, partial)
    total = blocks[0]
    for j in (1, 2, 3):
        total = total + ahead(blocks[j], "z", 4 - j).astype(F32)
    total = (total + swap(total, "core")) * inverse
    return finish(jnp.stack([core, yh]), result, total, swap(total, "yh"))


def solution(mesh):
    fine = Mesh(mesh.devices.reshape(2, 2, 2, 4, 4), FINE)
    rows, tok = P(FINE, None), P(("yl", "z", "x"), None)
    return jax.shard_map(
        shards,
        mesh=fine,
        in_specs=(rows, rows, tok, tok, tok),
        out_specs=(rows, rows, tok, tok),
        check_vma=False,
    )
```

```python
import jax
import jax.numpy as jnp
from jax import lax
from jax.experimental import pallas as pl
from jax.experimental.pallas import tpu as pltpu
from jax.sharding import Mesh
from jax.sharding import PartitionSpec as P

BLOCK = 128
FINE = ("yh", "core", "yl", "z", "x")
PLANE = ("yh", "yl", "x")
F32 = jnp.float32
BF16 = jnp.bfloat16


WHOLE = pl.BlockSpec(memory_space=pltpu.VMEM)
LEFT = pl.BlockSpec(memory_space=pl.ANY)
SCALAR = pl.BlockSpec(memory_space=pltpu.SMEM)


def params():
    return pltpu.CompilerParams(vmem_limit_bytes=16 << 20)


def pack_kernel(z_ref, float_ref, quant_ref, after_ref, out_ref, sem):
    width = float_ref.shape[1] // 32
    z = z_ref[0]
    copies = []
    for kind, ref in enumerate((float_ref, quant_ref)):
        for j in range(4):
            zj = lax.rem(z + j, 4)
            for yl in range(2):
                for x in range(4):
                    start = pl.multiple_of(((yl * 4 + zj) * 4 + x) * width, width)
                    for half in range(2):
                        at = (j * 2 + (yl ^ half)) * width
                        copies.append(
                            pltpu.make_async_copy(
                                ref.at[:, pl.ds(start, width)],
                                out_ref.at[kind * 8 + half * 4 + x, :, pl.ds(at, width)],
                                sem.at[len(copies)],
                            )
                        )
    for copy in copies:
        copy.start()
    for copy in copies:
        copy.wait()


def pack(z, attn_float, attn_quant, after):
    tokens, d_in = attn_float.shape
    return pl.pallas_call(
        pack_kernel,
        out_shape=jax.ShapeDtypeStruct((16, tokens, d_in // 4), BF16),
        in_specs=[SCALAR, LEFT, LEFT, LEFT],
        out_specs=LEFT,
        scratch_shapes=[pltpu.SemaphoreType.DMA((128,))],
        compiler_params=params(),
        name="pack",
    )(z.reshape(1), attn_float, attn_quant, after)


def project_kernel(acts_ref, *refs):
    weights, out_ref, buffer, sems = refs[:-3], refs[-3], refs[-2], refs[-1]
    depth, width = weights[0].shape
    tile, step = 512, buffer.shape[1]
    copies = []
    for n in range(acts_ref.shape[0] // step):
        if n >= 2:
            copies[n - 2].wait()
        rows = slice(n * step, (n + 1) * step)
        for q in range(2):
            for col in range(0, width, tile):
                total = None
                for j in range(4):
                    term = jnp.dot(
                        acts_ref[rows, j * depth : (j + 1) * depth],
                        weights[4 * q + j][:, col : col + tile],
                        preferred_element_type=F32,
                    )
                    total = term if total is None else total + term
                at = q * width + col
                buffer[n % 2, :, at : at + tile] = total.astype(BF16)
        copies.append(
            pltpu.make_async_copy(
                buffer.at[n % 2], out_ref.at[pl.ds(n * step, step)], sems.at[n % 2]
            )
        )
        copies[n].start()
    for copy in copies[-2:]:
        copy.wait()


def project(acts, weights):
    rows, depth = acts.shape
    cols = 2 * weights[0].shape[1]
    return pl.pallas_call(
        project_kernel,
        out_shape=jax.ShapeDtypeStruct((rows, cols), BF16),
        in_specs=[WHOLE] * (1 + len(weights)),
        out_specs=LEFT,
        scratch_shapes=[
            pltpu.VMEM((2, 256, cols), BF16),
            pltpu.SemaphoreType.DMA((2,)),
        ],
        compiler_params=params(),
        cost_estimate=pl.CostEstimate(
            flops=2 * rows * depth * cols, bytes_accessed=16 << 20, transcendentals=0
        ),
        name="project",
    )(acts, *weights)


def finish_kernel(at_ref, parts_ref, total_ref, moved_ref, *outs):
    core, yh = at_ref[0], at_ref[1]
    width = parts_ref.shape[2] // 2
    for q in range(2):
        quarter = core if q == 0 else 1 - core
        for kind, out in enumerate(outs[:2]):
            for half in range(2):
                at = kind * 8 + half * 4
                cols = slice(q * width, (q + 1) * width)
                total = parts_ref[at, :, cols].astype(F32)
                for x in range(1, 4):
                    total += parts_ref[at + x, :, cols].astype(F32)
                start = pl.multiple_of((half * 2 + quarter) * width, width)
                out[:, pl.ds(start, width)] = total.astype(BF16)
    total = jnp.where(yh == 1, total_ref[...], moved_ref[...])
    outs[2][...] = total[:, :BLOCK]
    outs[3][...] = total[:, BLOCK:]


def finish(at, parts, total, moved):
    tokens, cols = parts.shape[1:]
    rows = total.shape[0]
    return pl.pallas_call(
        finish_kernel,
        out_shape=(jax.ShapeDtypeStruct((tokens, 2 * cols), BF16),) * 2
        + (jax.ShapeDtypeStruct((rows, BLOCK), F32),) * 2,
        in_specs=[SCALAR] + [WHOLE] * 3,
        out_specs=(WHOLE,) * 4,
        compiler_params=params(),
        name="finish",
    )(at, parts, total, moved)


def stats_kernel(at_ref, acts_ref, *refs):
    pieces, outs, block_ref = refs[:4], refs[5:9], refs[9]
    y, x = at_ref[0], at_ref[1]
    tokens = pieces[0].shape[0] // 4
    for dy, piece in enumerate(pieces):
        for dx in range(4):
            start = (lax.rem(y + dy, 4) * 4 + lax.rem(x + dx, 4)) * tokens
            block_ref[pl.ds(pl.multiple_of(start, tokens), tokens)] = piece[
                dx * tokens : (dx + 1) * tokens
            ]
    width = outs[0].shape[0]
    for j, out in enumerate(outs):
        out[...] = lax.dot_general(
            acts_ref[:, 2 * j * width : (2 * j + 1) * width],
            block_ref[...],
            (((0,), (0,)), ((), ())),
            preferred_element_type=F32,
        ).astype(out.dtype)


def stats(at, acts, pieces, after):
    width = 2 * BLOCK
    return pl.pallas_call(
        stats_kernel,
        out_shape=(jax.ShapeDtypeStruct((width, width), F32),)
        + (jax.ShapeDtypeStruct((width, width), BF16),) * 3,
        in_specs=[SCALAR] + [WHOLE] * 5 + [LEFT],
        out_specs=(WHOLE,) * 4,
        scratch_shapes=[pltpu.VMEM((acts.shape[0], width), BF16)],
        compiler_params=params(),
        name="stats",
    )(at, acts, *pieces, after)


def swap(a, axis):
    return lax.ppermute(a, axis, [(0, 1), (1, 0)])


def ahead(a, axis, j):
    return lax.ppermute(a, axis, [((i + j) % 4, i) for i in range(4)])


def shards(attn_float, attn_quant, proj_weight, weight_codes, group_scales):
    tokens, d_in = attn_float.shape
    features, d_out = proj_weight.shape
    groups = group_scales.shape[0]
    half, quarter = d_out // 2, d_out // 4
    inverse = 1.0 / (tokens * 128)
    yh, core, yl, z = (lax.axis_index(a) for a in ("yh", "core", "yl", "z"))

    def weight(kind, col):
        plain = lax.dynamic_slice_in_dim(proj_weight, col, quarter, 1)
        codes = lax.dynamic_slice_in_dim(weight_codes, col, quarter, 1)
        scales = lax.dynamic_slice_in_dim(group_scales, col, quarter, 1)
        values = (codes - 8).astype(F32).reshape(groups, features // groups, quarter)
        quant = (values * scales[:, None, :]).reshape(features, quarter).astype(BF16)
        return jnp.where(kind == 0, plain, quant)

    quant = attn_quant[:, :BLOCK]
    shift = (attn_float[:, :BLOCK].astype(F32) - quant.astype(F32)).astype(BF16)
    block = jnp.concatenate([quant, shift], axis=1)
    col = (1 - yl) * half + core * quarter
    block, col = lax.optimization_barrier((block, col))
    line = jnp.concatenate([block] + [ahead(block, "x", j) for j in (1, 2, 3)], axis=0)

    send = weight(yh ^ core, col)
    line, send = lax.optimization_barrier((line, send))
    pieces = [line] + [ahead(line, ("yh", "yl"), j) for j in (1, 2, 3)]
    pairs = []
    for a in range(2):
        for c in range(2):
            for b in range(2):
                pairs.append((a * 4 + c * 2 + b, (a ^ c) * 4 + c * 2 + (1 - b)))
    got = lax.ppermute(send, ("yh", "core", "yl"), pairs)
    col, send = lax.optimization_barrier((yl * half + core * quarter, send))
    own = weight(yh, col)

    payload = pack(z, attn_float, attn_quant, send)
    payload, got, *pieces = lax.optimization_barrier((payload, got, *pieces))

    acts = lax.all_to_all(payload, PLANE, 0, 0, tiled=True).reshape(16 * tokens, 8 * features)

    rows = jnp.concatenate([own, got], axis=0)
    parts = [rows] + [ahead(rows, "z", j) for j in (1, 2, 3)]
    weights = parts + [swap(p, "core") for p in parts]

    partial = project(acts, weights)
    result = lax.all_to_all(partial.reshape(16, tokens, half), PLANE, 0, 0, tiled=True)

    blocks = stats(jnp.stack([yh * 2 + yl, lax.axis_index("x")]), acts, pieces, partial)
    total = blocks[0]
    for j in (1, 2, 3):
        total = total + ahead(blocks[j], "z", 4 - j).astype(F32)
    total = (total + swap(total, "core")) * inverse
    return finish(jnp.stack([core, yh]), result, total, swap(total, "yh"))


def solution(mesh):
    fine = Mesh(mesh.devices.reshape(2, 2, 2, 4, 4), FINE)
    rows, tok = P(FINE, None), P(("yl", "z", "x"), None)
    return jax.shard_map(
        shards,
        mesh=fine,
        in_specs=(rows, rows, tok, tok, tok),
        out_specs=(rows, rows, tok, tok),
        check_vma=False,
    )
```

```python
import jax
import jax.numpy as jnp
from jax import lax
from jax.experimental import pallas as pl
from jax.experimental.pallas import tpu as pltpu
from jax.sharding import Mesh
from jax.sharding import PartitionSpec as P

BLOCK = 128
FINE = ("yh", "core", "yl", "z", "x")
PLANE = ("yh", "yl", "x")
F32 = jnp.float32
BF16 = jnp.bfloat16


WHOLE = pl.BlockSpec(memory_space=pltpu.VMEM)
LEFT = pl.BlockSpec(memory_space=pl.ANY)
SCALAR = pl.BlockSpec(memory_space=pltpu.SMEM)


def params():
    return pltpu.CompilerParams(vmem_limit_bytes=16 << 20)


def pack_kernel(z_ref, float_ref, quant_ref, out_ref):
    width = float_ref.shape[1] // 32
    z = z_ref[0]
    for kind, ref in enumerate((float_ref, quant_ref)):
        for j in range(4):
            zj = lax.rem(z + j, 4)
            for yl in range(2):
                for x in range(4):
                    start = pl.multiple_of(((yl * 4 + zj) * 4 + x) * width, width)
                    block = ref[:, pl.ds(start, width)]
                    for half in range(2):
                        at = (j * 2 + (yl ^ half)) * width
                        out_ref[kind * 8 + half * 4 + x, :, at : at + width] = block
    quant = quant_ref[:, :BLOCK]
    shift = (float_ref[:, :BLOCK].astype(F32) - quant.astype(F32)).astype(BF16)
    for d in range(16):
        out_ref[d, :, 8 * width :] = shift if d // 4 % 2 else quant


def pack(z, attn_float, attn_quant):
    tokens, d_in = attn_float.shape
    return pl.pallas_call(
        pack_kernel,
        out_shape=jax.ShapeDtypeStruct((16, tokens, d_in // 4 + BLOCK), BF16),
        in_specs=[SCALAR, WHOLE, WHOLE],
        out_specs=WHOLE,
        compiler_params=params(),
        name="pack",
    )(z.reshape(1), attn_float, attn_quant)


def project_kernel(acts_ref, *refs):
    *weights, out_ref = refs
    depth, width = weights[0].shape
    tile = 512
    for q in range(2):
        for col in range(0, width, tile):
            for row in range(0, acts_ref.shape[0], 256):
                rows, total = slice(row, row + 256), None
                for j in range(4):
                    term = jnp.dot(
                        acts_ref[rows, j * depth : (j + 1) * depth],
                        weights[4 * q + j][:, col : col + tile],
                        preferred_element_type=F32,
                    )
                    total = term if total is None else total + term
                at = q * width + col
                out_ref[rows, at : at + tile] = total.astype(BF16)


def project(acts, weights):
    rows, depth = acts.shape[0], 4 * weights[0].shape[0]
    cols = 2 * weights[0].shape[1]
    return pl.pallas_call(
        project_kernel,
        out_shape=jax.ShapeDtypeStruct((rows, cols), BF16),
        in_specs=[WHOLE] * (1 + len(weights)),
        out_specs=WHOLE,
        compiler_params=params(),
        cost_estimate=pl.CostEstimate(
            flops=2 * rows * depth * cols, bytes_accessed=16 << 20, transcendentals=0
        ),
        name="project",
    )(acts, *weights)


def finish_kernel(at_ref, parts_ref, total_ref, *refs):
    (side_ref, down_ref, cross_ref), outs = refs[:3], refs[3:]
    core, yh, yl = at_ref[0], at_ref[1], at_ref[2]
    width = parts_ref.shape[2] // 2
    for q in range(2):
        quarter = core if q == 0 else 1 - core
        for kind, out in enumerate(outs[:2]):
            for half in range(2):
                at = kind * 8 + half * 4
                cols = slice(q * width, (q + 1) * width)
                total = parts_ref[at, :, cols].astype(F32)
                for x in range(1, 4):
                    total += parts_ref[at + x, :, cols].astype(F32)
                start = pl.multiple_of((half * 2 + quarter) * width, width)
                out[:, pl.ds(start, width)] = total.astype(BF16)
    rows = outs[2].shape[0]
    own = jnp.where(yh == 1, total_ref[:rows], down_ref[...].astype(F32))
    other = jnp.where(yh == 1, side_ref[...].astype(F32), cross_ref[...].astype(F32))
    outs[2][...] = jnp.where(yl == 0, own, other)
    outs[3][...] = jnp.where(yl == 0, other, own)


def finish(at, parts, total, moved):
    tokens, cols = parts.shape[1:]
    rows = total.shape[0] // 2
    return pl.pallas_call(
        finish_kernel,
        out_shape=(jax.ShapeDtypeStruct((tokens, 2 * cols), BF16),) * 2
        + (jax.ShapeDtypeStruct((rows, BLOCK), F32),) * 2,
        in_specs=[SCALAR] + [WHOLE] * (2 + len(moved)),
        out_specs=(WHOLE,) * 4,
        compiler_params=params(),
        name="finish",
    )(at, parts, total, *moved)


def stats_kernel(acts_ref, after_ref, *outs):
    width = outs[0].shape[0]
    for j, out in enumerate(outs):
        out[...] = lax.dot_general(
            acts_ref[:, j * width : (j + 1) * width],
            acts_ref[:, 4 * width :],
            (((0,), (0,)), ((), ())),
            preferred_element_type=F32,
        ).astype(out.dtype)


def stats(acts, after):
    width = (acts.shape[1] - BLOCK) // 4
    return pl.pallas_call(
        stats_kernel,
        out_shape=(jax.ShapeDtypeStruct((width, BLOCK), F32),)
        + (jax.ShapeDtypeStruct((width, BLOCK), BF16),) * 3,
        in_specs=[WHOLE, LEFT],
        out_specs=(WHOLE,) * 4,
        compiler_params=params(),
        name="stats",
    )(acts, after)


def swap(a, axis):
    return lax.ppermute(a, axis, [(0, 1), (1, 0)])


def ahead(a, axis, j):
    return lax.ppermute(a, axis, [((i + j) % 4, i) for i in range(4)])


def shards(attn_float, attn_quant, proj_weight, weight_codes, group_scales):
    tokens, d_in = attn_float.shape
    features, d_out = proj_weight.shape
    groups = group_scales.shape[0]
    half, quarter = d_out // 2, d_out // 4
    inverse = 1.0 / (tokens * 128)
    yh, core, yl, z = (lax.axis_index(a) for a in ("yh", "core", "yl", "z"))

    def weight(kind, col):
        plain = lax.dynamic_slice_in_dim(proj_weight, col, quarter, 1)
        codes = lax.dynamic_slice_in_dim(weight_codes, col, quarter, 1)
        scales = lax.dynamic_slice_in_dim(group_scales, col, quarter, 1)
        values = (codes - 8).astype(F32).reshape(groups, features // groups, quarter)
        quant = (values * scales[:, None, :]).reshape(features, quarter).astype(BF16)
        return jnp.where(kind == 0, plain, quant)

    send = weight(yh ^ core, (1 - yl) * half + core * quarter)
    pairs = []
    for a in range(2):
        for c in range(2):
            for b in range(2):
                pairs.append((a * 4 + c * 2 + b, (a ^ c) * 4 + c * 2 + (1 - b)))
    got = lax.ppermute(send, ("yh", "core", "yl"), pairs)
    col, send = lax.optimization_barrier((yl * half + core * quarter, send))
    own = weight(yh, col)

    payload = pack(z, attn_float, attn_quant)
    payload, got = lax.optimization_barrier((payload, got))

    acts = lax.all_to_all(payload, PLANE, 0, 0, tiled=True).reshape(16 * tokens, -1)

    rows = jnp.concatenate([own, got], axis=0)
    parts = [rows] + [ahead(rows, "z", j) for j in (1, 2, 3)]
    weights = parts + [swap(p, "core") for p in parts]

    partial = project(acts, weights)
    result = lax.all_to_all(partial.reshape(16, tokens, half), PLANE, 0, 0, tiled=True)

    blocks = stats(acts, partial)
    total = blocks[0]
    for j in (1, 2, 3):
        total = total + ahead(blocks[j], "z", 4 - j).astype(F32)
    total = (total + swap(total, "core")) * inverse
    here, there = total[:features].astype(BF16), total[features:].astype(BF16)
    moved = (
        swap(there, "yl"),
        swap(here, "yh"),
        lax.ppermute(there, ("yh", "yl"), [(i, 3 - i) for i in range(4)]),
    )
    return finish(jnp.stack([core, yh, yl]), result, total, moved)


def solution(mesh):
    fine = Mesh(mesh.devices.reshape(2, 2, 2, 4, 4), FINE)
    rows, tok = P(FINE, None), P(("yl", "z", "x"), None)
    return jax.shard_map(
        shards,
        mesh=fine,
        in_specs=(rows, rows, tok, tok, tok),
        out_specs=(rows, rows, tok, tok),
        check_vma=False,
    )
```

```python
import jax
import jax.numpy as jnp
from jax import lax
from jax.experimental import pallas as pl
from jax.experimental.pallas import tpu as pltpu
from jax.sharding import Mesh
from jax.sharding import PartitionSpec as P

BLOCK = 128
FINE = ("yh", "core", "yl", "z", "x")
PLANE = ("yh", "yl", "x")
F32 = jnp.float32
BF16 = jnp.bfloat16


WHOLE = pl.BlockSpec(memory_space=pltpu.VMEM)
LEFT = pl.BlockSpec(memory_space=pl.ANY)
SCALAR = pl.BlockSpec(memory_space=pltpu.SMEM)


def params():
    return pltpu.CompilerParams(vmem_limit_bytes=16 << 20)


def pack_kernel(z_ref, float_ref, quant_ref, out_ref):
    width = float_ref.shape[1] // 32
    z = z_ref[0]
    for kind, ref in enumerate((float_ref, quant_ref)):
        for j in range(4):
            zj = lax.rem(z + j, 4)
            for yl in range(2):
                for x in range(4):
                    start = pl.multiple_of(((yl * 4 + zj) * 4 + x) * width, width)
                    block = ref[:, pl.ds(start, width)]
                    for half in range(2):
                        at = (j * 2 + (yl ^ half)) * width
                        out_ref[kind * 8 + half * 4 + x, :, at : at + width] = block
    quant = quant_ref[:, :BLOCK]
    shift = (float_ref[:, :BLOCK].astype(F32) - quant.astype(F32)).astype(BF16)
    for d in range(16):
        out_ref[d, :, 8 * width :] = shift if d // 4 % 2 else quant


def pack(z, attn_float, attn_quant):
    tokens, d_in = attn_float.shape
    return pl.pallas_call(
        pack_kernel,
        out_shape=jax.ShapeDtypeStruct((16, tokens, d_in // 4 + BLOCK), BF16),
        in_specs=[SCALAR, WHOLE, WHOLE],
        out_specs=WHOLE,
        compiler_params=params(),
        name="pack",
    )(z.reshape(1), attn_float, attn_quant)


def project_kernel(acts_ref, *refs):
    *weights, out_ref = refs
    depth, width = weights[0].shape
    tile = 512
    for col in range(0, width, tile):
        total = None
        for j, ref in enumerate(weights):
            term = jnp.dot(
                acts_ref[:, j * depth : (j + 1) * depth],
                ref[:, col : col + tile],
                preferred_element_type=F32,
            )
            total = term if total is None else total + term
        out_ref[:, col : col + tile] = total.astype(BF16)


def project(acts, weights):
    rows, cols = acts.shape[0], weights[0].shape[1]
    step = 256
    return pl.pallas_call(
        project_kernel,
        out_shape=jax.ShapeDtypeStruct((rows, cols), BF16),
        grid=(rows // step,),
        in_specs=[pl.BlockSpec((step, acts.shape[1]), lambda i: (i, 0))] + [WHOLE] * len(weights),
        out_specs=pl.BlockSpec((step, cols), lambda i: (i, 0)),
        compiler_params=params(),
        cost_estimate=pl.CostEstimate(
            flops=2 * rows * 2048 * cols, bytes_accessed=12 << 20, transcendentals=0
        ),
        name="project",
    )(acts, *weights)


def finish_kernel(at_ref, first_ref, second_ref, total_ref, *refs):
    (side_ref, down_ref, cross_ref), outs = refs[:3], refs[3:]
    core, yh, yl = at_ref[0], at_ref[1], at_ref[2]
    width = first_ref.shape[2]
    for q, ref in enumerate((first_ref, second_ref)):
        quarter = core if q == 0 else 1 - core
        for kind, out in enumerate(outs[:2]):
            for half in range(2):
                at = kind * 8 + half * 4
                total = ref[at].astype(F32)
                for x in range(1, 4):
                    total += ref[at + x].astype(F32)
                start = pl.multiple_of((half * 2 + quarter) * width, width)
                out[:, pl.ds(start, width)] = total.astype(BF16)
    rows = outs[2].shape[0]
    own = jnp.where(yh == 1, total_ref[:rows], down_ref[...].astype(F32))
    other = jnp.where(yh == 1, side_ref[...].astype(F32), cross_ref[...].astype(F32))
    outs[2][...] = jnp.where(yl == 0, own, other)
    outs[3][...] = jnp.where(yl == 0, other, own)


def finish(at, first, second, total, moved):
    tokens, cols = first.shape[1:]
    rows = total.shape[0] // 2
    return pl.pallas_call(
        finish_kernel,
        out_shape=(jax.ShapeDtypeStruct((tokens, 4 * cols), BF16),) * 2
        + (jax.ShapeDtypeStruct((rows, BLOCK), F32),) * 2,
        in_specs=[SCALAR] + [WHOLE] * (3 + len(moved)),
        out_specs=(WHOLE,) * 4,
        compiler_params=params(),
        name="finish",
    )(at, first, second, total, *moved)


def stats_kernel(acts_ref, after_ref, *outs):
    width = outs[0].shape[0]
    for j, out in enumerate(outs):
        out[...] = lax.dot_general(
            acts_ref[:, j * width : (j + 1) * width],
            acts_ref[:, 4 * width :],
            (((0,), (0,)), ((), ())),
            preferred_element_type=F32,
        ).astype(out.dtype)


def stats(acts, after):
    width = (acts.shape[1] - BLOCK) // 4
    return pl.pallas_call(
        stats_kernel,
        out_shape=(jax.ShapeDtypeStruct((width, BLOCK), F32),)
        + (jax.ShapeDtypeStruct((width, BLOCK), BF16),) * 3,
        in_specs=[WHOLE, LEFT],
        out_specs=(WHOLE,) * 4,
        compiler_params=params(),
        name="stats",
    )(acts, after)


def swap(a, axis):
    return lax.ppermute(a, axis, [(0, 1), (1, 0)])


def ahead(a, axis, j):
    return lax.ppermute(a, axis, [((i + j) % 4, i) for i in range(4)])


def shards(attn_float, attn_quant, proj_weight, weight_codes, group_scales):
    tokens, d_in = attn_float.shape
    features, d_out = proj_weight.shape
    groups = group_scales.shape[0]
    half, quarter = d_out // 2, d_out // 4
    inverse = 1.0 / (tokens * 128)
    yh, core, yl, z = (lax.axis_index(a) for a in ("yh", "core", "yl", "z"))

    def weight(kind, col):
        plain = lax.dynamic_slice_in_dim(proj_weight, col, quarter, 1)
        codes = lax.dynamic_slice_in_dim(weight_codes, col, quarter, 1)
        scales = lax.dynamic_slice_in_dim(group_scales, col, quarter, 1)
        values = (codes - 8).astype(F32).reshape(groups, features // groups, quarter)
        quant = (values * scales[:, None, :]).reshape(features, quarter).astype(BF16)
        return jnp.where(kind == 0, plain, quant)

    send = weight(yh ^ core, (1 - yl) * half + core * quarter)
    pairs = []
    for a in range(2):
        for c in range(2):
            for b in range(2):
                pairs.append((a * 4 + c * 2 + b, (a ^ c) * 4 + c * 2 + (1 - b)))
    got = lax.ppermute(send, ("yh", "core", "yl"), pairs)
    col, send = lax.optimization_barrier((yl * half + core * quarter, send))
    own = weight(yh, col)

    payload = pack(z, attn_float, attn_quant)
    payload, got = lax.optimization_barrier((payload, got))

    acts = lax.all_to_all(payload, PLANE, 0, 0, tiled=True).reshape(16 * tokens, -1)

    rows = jnp.concatenate([own, got], axis=0)
    parts = [rows] + [ahead(rows, "z", j) for j in (1, 2, 3)]
    others = [swap(p, "core") for p in parts]

    def output(p):
        return lax.all_to_all(p.reshape(16, tokens, quarter), PLANE, 0, 0, tiled=True)

    result1 = output(project(acts, parts))
    second = project(acts, others)

    blocks = stats(acts, second)
    result2 = output(second)
    total = blocks[0]
    for j in (1, 2, 3):
        total = total + ahead(blocks[j], "z", 4 - j).astype(F32)
    total = (total + swap(total, "core")) * inverse
    here, there = total[:features].astype(BF16), total[features:].astype(BF16)
    moved = (
        swap(there, "yl"),
        swap(here, "yh"),
        lax.ppermute(there, ("yh", "yl"), [(i, 3 - i) for i in range(4)]),
    )
    return finish(jnp.stack([core, yh, yl]), result1, result2, total, moved)


def solution(mesh):
    fine = Mesh(mesh.devices.reshape(2, 2, 2, 4, 4), FINE)
    rows, tok = P(FINE, None), P(("yl", "z", "x"), None)
    return jax.shard_map(
        shards,
        mesh=fine,
        in_specs=(rows, rows, tok, tok, tok),
        out_specs=(rows, rows, tok, tok),
        check_vma=False,
    )
```

```python
import jax
import jax.numpy as jnp
from jax import lax
from jax.experimental import pallas as pl
from jax.experimental.pallas import tpu as pltpu
from jax.sharding import Mesh
from jax.sharding import PartitionSpec as P

BLOCK = 128
FINE = ("yh", "core", "yl", "z", "x")
PLANE = ("yh", "yl", "x")
F32 = jnp.float32
BF16 = jnp.bfloat16


WHOLE = pl.BlockSpec(memory_space=pltpu.VMEM)
LEFT = pl.BlockSpec(memory_space=pl.ANY)
SCALAR = pl.BlockSpec(memory_space=pltpu.SMEM)


def params():
    return pltpu.CompilerParams(vmem_limit_bytes=16 << 20)


def pack_kernel(z_ref, float_ref, quant_ref, out_ref):
    width = float_ref.shape[1] // 32
    z = z_ref[0]
    for kind, ref in enumerate((float_ref, quant_ref)):
        for j in range(4):
            zj = lax.rem(z + j, 4)
            for yl in range(2):
                for x in range(4):
                    start = pl.multiple_of(((yl * 4 + zj) * 4 + x) * width, width)
                    block = ref[:, pl.ds(start, width)]
                    for half in range(2):
                        at = (j * 2 + (yl ^ half)) * width
                        out_ref[kind * 8 + half * 4 + x, :, at : at + width] = block
    quant = quant_ref[:, :BLOCK]
    shift = (float_ref[:, :BLOCK].astype(F32) - quant.astype(F32)).astype(BF16)
    for d in range(16):
        out_ref[d, :, 8 * width :] = shift if d // 4 % 2 else quant


def pack(z, attn_float, attn_quant):
    tokens, d_in = attn_float.shape
    return pl.pallas_call(
        pack_kernel,
        out_shape=jax.ShapeDtypeStruct((16, tokens, d_in // 4 + BLOCK), BF16),
        in_specs=[SCALAR, WHOLE, WHOLE],
        out_specs=WHOLE,
        compiler_params=params(),
        name="pack",
    )(z.reshape(1), attn_float, attn_quant)


def project_kernel(acts_ref, *refs):
    weights, out_ref = refs[:4], refs[-1]
    depth, width = weights[0].shape
    tile = 512
    for col in range(0, width, tile):
        total = None
        for j, ref in enumerate(weights):
            term = jnp.dot(
                acts_ref[:, j * depth : (j + 1) * depth],
                ref[:, col : col + tile],
                preferred_element_type=F32,
            )
            total = term if total is None else total + term
        out_ref[:, col : col + tile] = total.astype(BF16)


def project(acts, weights, after):
    rows, cols = acts.shape[0], weights[0].shape[1]
    step = 256
    return pl.pallas_call(
        project_kernel,
        out_shape=jax.ShapeDtypeStruct((rows, cols), BF16),
        grid=(rows // step,),
        in_specs=[pl.BlockSpec((step, acts.shape[1]), lambda i: (i, 0))] + [WHOLE] * len(weights)
        + [LEFT] * len(after),
        out_specs=pl.BlockSpec((step, cols), lambda i: (i, 0)),
        compiler_params=params(),
        cost_estimate=pl.CostEstimate(
            flops=2 * rows * 2048 * cols, bytes_accessed=12 << 20, transcendentals=0
        ),
        name="project",
    )(acts, *weights, *after)


def finish_kernel(at_ref, first_ref, second_ref, total_ref, *refs):
    (side_ref, down_ref, cross_ref), outs = refs[:3], refs[3:]
    core, yh, yl = at_ref[0], at_ref[1], at_ref[2]
    width = first_ref.shape[2]
    for q, ref in enumerate((first_ref, second_ref)):
        quarter = core if q == 0 else 1 - core
        for kind, out in enumerate(outs[:2]):
            for half in range(2):
                at = kind * 8 + half * 4
                total = ref[at].astype(F32)
                for x in range(1, 4):
                    total += ref[at + x].astype(F32)
                start = pl.multiple_of((half * 2 + quarter) * width, width)
                out[:, pl.ds(start, width)] = total.astype(BF16)
    rows = outs[2].shape[0]
    own = jnp.where(yh == 1, total_ref[:rows], down_ref[...].astype(F32))
    other = jnp.where(yh == 1, side_ref[...].astype(F32), cross_ref[...].astype(F32))
    outs[2][...] = jnp.where(yl == 0, own, other)
    outs[3][...] = jnp.where(yl == 0, other, own)


def finish(at, first, second, total, moved):
    tokens, cols = first.shape[1:]
    rows = total.shape[0] // 2
    return pl.pallas_call(
        finish_kernel,
        out_shape=(jax.ShapeDtypeStruct((tokens, 4 * cols), BF16),) * 2
        + (jax.ShapeDtypeStruct((rows, BLOCK), F32),) * 2,
        in_specs=[SCALAR] + [WHOLE] * (3 + len(moved)),
        out_specs=(WHOLE,) * 4,
        compiler_params=params(),
        name="finish",
    )(at, first, second, total, *moved)


def stats_kernel(acts_ref, after_ref, *outs):
    width = outs[0].shape[0]
    for j, out in enumerate(outs):
        out[...] = lax.dot_general(
            acts_ref[:, j * width : (j + 1) * width],
            acts_ref[:, 4 * width :],
            (((0,), (0,)), ((), ())),
            preferred_element_type=F32,
        ).astype(out.dtype)


def stats(acts, after):
    width = (acts.shape[1] - BLOCK) // 4
    return pl.pallas_call(
        stats_kernel,
        out_shape=(jax.ShapeDtypeStruct((width, BLOCK), F32),)
        + (jax.ShapeDtypeStruct((width, BLOCK), BF16),) * 3,
        in_specs=[WHOLE, LEFT],
        out_specs=(WHOLE,) * 4,
        compiler_params=params(),
        name="stats",
    )(acts, after)


def swap(a, axis):
    return lax.ppermute(a, axis, [(0, 1), (1, 0)])


def ahead(a, axis, j):
    return lax.ppermute(a, axis, [((i + j) % 4, i) for i in range(4)])


def shards(attn_float, attn_quant, proj_weight, weight_codes, group_scales):
    tokens, d_in = attn_float.shape
    features, d_out = proj_weight.shape
    groups = group_scales.shape[0]
    half, quarter = d_out // 2, d_out // 4
    inverse = 1.0 / (tokens * 128)
    yh, core, yl, z = (lax.axis_index(a) for a in ("yh", "core", "yl", "z"))

    def weight(kind, col):
        plain = lax.dynamic_slice_in_dim(proj_weight, col, quarter, 1)
        codes = lax.dynamic_slice_in_dim(weight_codes, col, quarter, 1)
        scales = lax.dynamic_slice_in_dim(group_scales, col, quarter, 1)
        values = (codes - 8).astype(F32).reshape(groups, features // groups, quarter)
        quant = (values * scales[:, None, :]).reshape(features, quarter).astype(BF16)
        return jnp.where(kind == 0, plain, quant)

    send = weight(yh ^ core, (1 - yl) * half + core * quarter)
    pairs = []
    for a in range(2):
        for c in range(2):
            for b in range(2):
                pairs.append((a * 4 + c * 2 + b, (a ^ c) * 4 + c * 2 + (1 - b)))
    got = lax.ppermute(send, ("yh", "core", "yl"), pairs)
    col, send = lax.optimization_barrier((yl * half + core * quarter, send))
    own = weight(yh, col)

    payload = pack(z, attn_float, attn_quant)
    rows = jnp.concatenate([own, got], axis=0)
    payload, rows = lax.optimization_barrier((payload, rows))
    parts = [rows] + [ahead(rows, "z", j) for j in (1, 2, 3)]

    acts = lax.all_to_all(payload, PLANE, 0, 0, tiled=True).reshape(16 * tokens, -1)
    acts, *parts = lax.optimization_barrier((acts, *parts))

    def output(p):
        return lax.all_to_all(p.reshape(16, tokens, quarter), PLANE, 0, 0, tiled=True)

    first = project(acts, parts, ())
    first, *parts = lax.optimization_barrier((first, *parts))
    result1 = output(first)
    others = [swap(p, "core") for p in parts]

    blocks = stats(acts, first)
    total = blocks[0]
    for j in (1, 2, 3):
        total = total + ahead(blocks[j], "z", 4 - j).astype(F32)
    second = project(acts, others, (total,))
    total = (total + swap(total, "core")) * inverse
    here, there = total[:features].astype(BF16), total[features:].astype(BF16)
    moved = (
        swap(there, "yl"),
        swap(here, "yh"),
        lax.ppermute(there, ("yh", "yl"), [(i, 3 - i) for i in range(4)]),
    )
    second, total, *moved = lax.optimization_barrier((second, total, *moved))
    result2 = output(second)
    return finish(jnp.stack([core, yh, yl]), result1, result2, total, moved)


def solution(mesh):
    fine = Mesh(mesh.devices.reshape(2, 2, 2, 4, 4), FINE)
    rows, tok = P(FINE, None), P(("yl", "z", "x"), None)
    return jax.shard_map(
        shards,
        mesh=fine,
        in_specs=(rows, rows, tok, tok, tok),
        out_specs=(rows, rows, tok, tok),
        check_vma=False,
    )
```

```python
import jax
import jax.numpy as jnp
from jax import lax
from jax.experimental import pallas as pl
from jax.experimental.pallas import tpu as pltpu
from jax.sharding import Mesh
from jax.sharding import PartitionSpec as P

BLOCK = 128
FINE = ("yh", "core", "yl", "z", "x")
PLANE = ("yh", "yl", "x")
F32 = jnp.float32
BF16 = jnp.bfloat16


WHOLE = pl.BlockSpec(memory_space=pltpu.VMEM)
LEFT = pl.BlockSpec(memory_space=pl.ANY)
SCALAR = pl.BlockSpec(memory_space=pltpu.SMEM)


def params():
    return pltpu.CompilerParams(vmem_limit_bytes=6 << 20)


def pack_kernel(z_ref, float_ref, quant_ref, out_ref):
    width = float_ref.shape[1] // 32
    z = z_ref[0]
    for kind, ref in enumerate((float_ref, quant_ref)):
        for j in range(4):
            zj = lax.rem(z + j, 4)
            for yl in range(2):
                for x in range(4):
                    start = pl.multiple_of(((yl * 4 + zj) * 4 + x) * width, width)
                    block = ref[:, pl.ds(start, width)]
                    for half in range(2):
                        at = (j * 2 + (yl ^ half)) * width
                        out_ref[kind * 8 + half * 4 + x, :, at : at + width] = block
    quant = quant_ref[:, :BLOCK]
    shift = (float_ref[:, :BLOCK].astype(F32) - quant.astype(F32)).astype(BF16)
    for d in range(16):
        out_ref[d, :, 8 * width :] = shift if d // 4 % 2 else quant


def pack(z, attn_float, attn_quant):
    tokens, d_in = attn_float.shape
    return pl.pallas_call(
        pack_kernel,
        out_shape=jax.ShapeDtypeStruct((16, tokens, d_in // 4 + BLOCK), BF16),
        in_specs=[SCALAR, WHOLE, WHOLE],
        out_specs=WHOLE,
        compiler_params=params(),
        name="pack",
    )(z.reshape(1), attn_float, attn_quant)


def project_kernel(acts_ref, *refs):
    weights, out_ref = refs[:4], refs[-1]
    depth, width = weights[0].shape
    tile = 512
    for col in range(0, width, tile):
        total = None
        for j, ref in enumerate(weights):
            term = jnp.dot(
                acts_ref[:, j * depth : (j + 1) * depth],
                ref[:, col : col + tile],
                preferred_element_type=F32,
            )
            total = term if total is None else total + term
        out_ref[:, col : col + tile] = total.astype(BF16)


def project(acts, weights, after):
    rows, cols = acts.shape[0], weights[0].shape[1]
    step = 256
    return pl.pallas_call(
        project_kernel,
        out_shape=jax.ShapeDtypeStruct((rows, cols), BF16),
        grid=(rows // step,),
        in_specs=[pl.BlockSpec((step, acts.shape[1]), lambda i: (i, 0))] + [WHOLE] * len(weights)
        + [LEFT] * len(after),
        out_specs=pl.BlockSpec((step, cols), lambda i: (i, 0)),
        compiler_params=params(),
        cost_estimate=pl.CostEstimate(
            flops=2 * rows * 2048 * cols, bytes_accessed=12 << 20, transcendentals=0
        ),
        name="project",
    )(acts, *weights, *after)


def finish_kernel(at_ref, first_ref, second_ref, total_ref, *refs):
    (side_ref, down_ref, cross_ref), outs = refs[:3], refs[3:]
    core, yh, yl = at_ref[0], at_ref[1], at_ref[2]
    width = first_ref.shape[2]
    for q, ref in enumerate((first_ref, second_ref)):
        quarter = core if q == 0 else 1 - core
        for kind, out in enumerate(outs[:2]):
            for half in range(2):
                at = kind * 8 + half * 4
                total = ref[at].astype(F32)
                for x in range(1, 4):
                    total += ref[at + x].astype(F32)
                start = pl.multiple_of((half * 2 + quarter) * width, width)
                out[:, pl.ds(start, width)] = total.astype(BF16)
    rows = outs[2].shape[0]
    own = jnp.where(yh == 1, total_ref[:rows], down_ref[...].astype(F32))
    other = jnp.where(yh == 1, side_ref[...].astype(F32), cross_ref[...].astype(F32))
    outs[2][...] = jnp.where(yl == 0, own, other)
    outs[3][...] = jnp.where(yl == 0, other, own)


def finish(at, first, second, total, moved):
    tokens, cols = first.shape[1:]
    rows = total.shape[0] // 2
    return pl.pallas_call(
        finish_kernel,
        out_shape=(jax.ShapeDtypeStruct((tokens, 4 * cols), BF16),) * 2
        + (jax.ShapeDtypeStruct((rows, BLOCK), F32),) * 2,
        in_specs=[SCALAR] + [WHOLE] * (3 + len(moved)),
        out_specs=(WHOLE,) * 4,
        compiler_params=params(),
        name="finish",
    )(at, first, second, total, *moved)


def stats_kernel(acts_ref, after_ref, *outs):
    width = outs[0].shape[0]
    for j, out in enumerate(outs):
        out[...] = lax.dot_general(
            acts_ref[:, j * width : (j + 1) * width],
            acts_ref[:, 4 * width :],
            (((0,), (0,)), ((), ())),
            preferred_element_type=F32,
        ).astype(out.dtype)


def stats(acts, after):
    width = (acts.shape[1] - BLOCK) // 4
    return pl.pallas_call(
        stats_kernel,
        out_shape=(jax.ShapeDtypeStruct((width, BLOCK), F32),)
        + (jax.ShapeDtypeStruct((width, BLOCK), BF16),) * 3,
        in_specs=[WHOLE, LEFT],
        out_specs=(WHOLE,) * 4,
        compiler_params=params(),
        name="stats",
    )(acts, after)


def swap(a, axis):
    return lax.ppermute(a, axis, [(0, 1), (1, 0)])


def ahead(a, axis, j):
    return lax.ppermute(a, axis, [((i + j) % 4, i) for i in range(4)])


def shards(attn_float, attn_quant, proj_weight, weight_codes, group_scales):
    tokens, d_in = attn_float.shape
    features, d_out = proj_weight.shape
    groups = group_scales.shape[0]
    half, quarter = d_out // 2, d_out // 4
    inverse = 1.0 / (tokens * 128)
    yh, core, yl, z = (lax.axis_index(a) for a in ("yh", "core", "yl", "z"))

    def weight(kind, col):
        plain = lax.dynamic_slice_in_dim(proj_weight, col, quarter, 1)
        codes = lax.dynamic_slice_in_dim(weight_codes, col, quarter, 1)
        scales = lax.dynamic_slice_in_dim(group_scales, col, quarter, 1)
        values = (codes - 8).astype(F32).reshape(groups, features // groups, quarter)
        quant = (values * scales[:, None, :]).reshape(features, quarter).astype(BF16)
        return jnp.where(kind == 0, plain, quant)

    send = weight(yh ^ core, (1 - yl) * half + core * quarter)
    pairs = []
    for a in range(2):
        for c in range(2):
            for b in range(2):
                pairs.append((a * 4 + c * 2 + b, (a ^ c) * 4 + c * 2 + (1 - b)))
    got = lax.ppermute(send, ("yh", "core", "yl"), pairs)
    col, send = lax.optimization_barrier((yl * half + core * quarter, send))
    own = weight(yh, col)

    payload = pack(z, attn_float, attn_quant)
    payload, got = lax.optimization_barrier((payload, got))
    rows = jnp.concatenate([own, got], axis=0)
    parts = [rows] + [ahead(rows, "z", j) for j in (1, 2, 3)]

    acts = lax.all_to_all(payload, PLANE, 0, 0, tiled=True).reshape(16 * tokens, -1)
    others = [swap(p, "core") for p in parts]

    def output(p):
        return lax.all_to_all(p.reshape(16, tokens, quarter), PLANE, 0, 0, tiled=True)

    first = project(acts, parts, ())
    result1 = output(first)

    blocks = stats(acts, first)
    total = blocks[0]
    for j in (1, 2, 3):
        total = total + ahead(blocks[j], "z", 4 - j).astype(F32)
    second = project(acts, others, (total,))
    total = (total + swap(total, "core")) * inverse
    here, there = total[:features].astype(BF16), total[features:].astype(BF16)
    moved = (
        swap(there, "yl"),
        swap(here, "yh"),
        lax.ppermute(there, ("yh", "yl"), [(i, 3 - i) for i in range(4)]),
    )
    at = jnp.stack([core, yh, yl])
    at, second, total, *moved = lax.optimization_barrier((at, second, total, *moved))
    result2 = output(second)
    return finish(at, result1, result2, total, moved)


def solution(mesh):
    fine = Mesh(mesh.devices.reshape(2, 2, 2, 4, 4), FINE)
    rows, tok = P(FINE, None), P(("yl", "z", "x"), None)
    return jax.shard_map(
        shards,
        mesh=fine,
        in_specs=(rows, rows, tok, tok, tok),
        out_specs=(rows, rows, tok, tok),
        check_vma=False,
    )
```

```python
import jax
import jax.numpy as jnp
from jax import lax
from jax.experimental import pallas as pl
from jax.experimental.pallas import tpu as pltpu
from jax.sharding import Mesh
from jax.sharding import PartitionSpec as P

BLOCK = 128
FINE = ("yh", "core", "yl", "z", "x")
PLANE = ("yh", "yl", "x")
F32 = jnp.float32
BF16 = jnp.bfloat16


WHOLE = pl.BlockSpec(memory_space=pltpu.VMEM)
LEFT = pl.BlockSpec(memory_space=pl.ANY)
SCALAR = pl.BlockSpec(memory_space=pltpu.SMEM)


def params():
    return pltpu.CompilerParams(vmem_limit_bytes=6 << 20)


def pack_kernel(z_ref, float_ref, quant_ref, out_ref):
    width = float_ref.shape[1] // 32
    z = z_ref[0]
    for kind, ref in enumerate((float_ref, quant_ref)):
        for j in range(4):
            zj = lax.rem(z + j, 4)
            for yl in range(2):
                for x in range(4):
                    start = pl.multiple_of(((yl * 4 + zj) * 4 + x) * width, width)
                    block = ref[:, pl.ds(start, width)]
                    for half in range(2):
                        at = (j * 2 + (yl ^ half)) * width
                        out_ref[kind * 8 + half * 4 + x, :, at : at + width] = block
    quant = quant_ref[:, :BLOCK]
    shift = (float_ref[:, :BLOCK].astype(F32) - quant.astype(F32)).astype(BF16)
    for d in range(16):
        out_ref[d, :, 8 * width :] = shift if d // 4 % 2 else quant


def pack(z, attn_float, attn_quant):
    tokens, d_in = attn_float.shape
    return pl.pallas_call(
        pack_kernel,
        out_shape=jax.ShapeDtypeStruct((16, tokens, d_in // 4 + BLOCK), BF16),
        in_specs=[SCALAR, WHOLE, WHOLE],
        out_specs=WHOLE,
        compiler_params=params(),
        name="pack",
    )(z.reshape(1), attn_float, attn_quant)


def project_kernel(acts_ref, *refs):
    weights, out_ref = refs[:4], refs[-1]
    depth, width = weights[0].shape
    tile = 512
    for col in range(0, width, tile):
        total = None
        for j, ref in enumerate(weights):
            term = jnp.dot(
                acts_ref[:, j * depth : (j + 1) * depth],
                ref[:, col : col + tile],
                preferred_element_type=F32,
            )
            total = term if total is None else total + term
        out_ref[:, col : col + tile] = total.astype(BF16)


def project(acts, weights, after):
    rows, cols = acts.shape[0], weights[0].shape[1]
    step = 256
    return pl.pallas_call(
        project_kernel,
        out_shape=jax.ShapeDtypeStruct((rows, cols), BF16),
        grid=(rows // step,),
        in_specs=[pl.BlockSpec((step, acts.shape[1]), lambda i: (i, 0))] + [WHOLE] * len(weights)
        + [LEFT] * len(after),
        out_specs=pl.BlockSpec((step, cols), lambda i: (i, 0)),
        compiler_params=params(),
        cost_estimate=pl.CostEstimate(
            flops=2 * rows * 2048 * cols, bytes_accessed=12 << 20, transcendentals=0
        ),
        name="project",
    )(acts, *weights, *after)


def finish_kernel(at_ref, first_ref, second_ref, total_ref, *refs):
    (side_ref, down_ref, cross_ref), outs = refs[:3], refs[3:]
    core, yh, yl = at_ref[0], at_ref[1], at_ref[2]
    width = first_ref.shape[2]
    for q, ref in enumerate((first_ref, second_ref)):
        quarter = core if q == 0 else 1 - core
        for kind, out in enumerate(outs[:2]):
            for half in range(2):
                at = kind * 8 + half * 4
                total = ref[at].astype(F32)
                for x in range(1, 4):
                    total += ref[at + x].astype(F32)
                start = pl.multiple_of((half * 2 + quarter) * width, width)
                out[:, pl.ds(start, width)] = total.astype(BF16)
    rows = outs[2].shape[0]
    own = jnp.where(yh == 1, total_ref[:rows], down_ref[...].astype(F32))
    other = jnp.where(yh == 1, side_ref[...].astype(F32), cross_ref[...].astype(F32))
    outs[2][...] = jnp.where(yl == 0, own, other)
    outs[3][...] = jnp.where(yl == 0, other, own)


def finish(at, first, second, total, moved):
    tokens, cols = first.shape[1:]
    rows = total.shape[0] // 2
    return pl.pallas_call(
        finish_kernel,
        out_shape=(jax.ShapeDtypeStruct((tokens, 4 * cols), BF16),) * 2
        + (jax.ShapeDtypeStruct((rows, BLOCK), F32),) * 2,
        in_specs=[SCALAR] + [WHOLE] * (3 + len(moved)),
        out_specs=(WHOLE,) * 4,
        compiler_params=params(),
        name="finish",
    )(at, first, second, total, *moved)


def stats_kernel(acts_ref, after_ref, *outs):
    width = outs[0].shape[0]
    for j, out in enumerate(outs):
        out[...] = lax.dot_general(
            acts_ref[:, j * width : (j + 1) * width],
            acts_ref[:, 4 * width :],
            (((0,), (0,)), ((), ())),
            preferred_element_type=F32,
        ).astype(out.dtype)


def stats(acts, after):
    width = (acts.shape[1] - BLOCK) // 4
    return pl.pallas_call(
        stats_kernel,
        out_shape=(jax.ShapeDtypeStruct((width, BLOCK), F32),)
        + (jax.ShapeDtypeStruct((width, BLOCK), BF16),) * 3,
        in_specs=[WHOLE, LEFT],
        out_specs=(WHOLE,) * 4,
        compiler_params=params(),
        name="stats",
    )(acts, after)


def swap(a, axis):
    return lax.ppermute(a, axis, [(0, 1), (1, 0)])


def ahead(a, axis, j):
    return lax.ppermute(a, axis, [((i + j) % 4, i) for i in range(4)])


def shards(attn_float, attn_quant, proj_weight, weight_codes, group_scales):
    tokens, d_in = attn_float.shape
    features, d_out = proj_weight.shape
    groups = group_scales.shape[0]
    half, quarter = d_out // 2, d_out // 4
    inverse = 1.0 / (tokens * 128)
    yh, core, yl, z = (lax.axis_index(a) for a in ("yh", "core", "yl", "z"))

    def weight(kind, col):
        plain = lax.dynamic_slice_in_dim(proj_weight, col, quarter, 1)
        codes = lax.dynamic_slice_in_dim(weight_codes, col, quarter, 1)
        scales = lax.dynamic_slice_in_dim(group_scales, col, quarter, 1)
        values = (codes - 8).astype(F32).reshape(groups, features // groups, quarter)
        quant = (values * scales[:, None, :]).reshape(features, quarter).astype(BF16)
        return jnp.where(kind == 0, plain, quant)

    send = weight(yh ^ core, (1 - yl) * half + core * quarter)
    pairs = []
    for a in range(2):
        for c in range(2):
            for b in range(2):
                pairs.append((a * 4 + c * 2 + b, (a ^ c) * 4 + c * 2 + (1 - b)))
    got = lax.ppermute(send, ("yh", "core", "yl"), pairs)
    col, send = lax.optimization_barrier((yl * half + core * quarter, send))
    own = weight(yh, col)

    payload = pack(z, attn_float, attn_quant)
    payload, got = lax.optimization_barrier((payload, got))
    rows = jnp.concatenate([own, got], axis=0)
    parts = [rows] + [ahead(rows, "z", j) for j in (1, 2, 3)]

    acts = lax.all_to_all(payload, PLANE, 0, 0, tiled=True).reshape(16 * tokens, -1)
    others = [swap(p, "core") for p in parts]

    def output(p):
        return lax.all_to_all(p.reshape(16, tokens, quarter), PLANE, 0, 0, tiled=True)

    first = project(acts, parts, others)
    result1 = output(first)

    blocks = stats(acts, first)
    total = blocks[0]
    for j in (1, 2, 3):
        total = total + ahead(blocks[j], "z", 4 - j).astype(F32)
    second = project(acts, others, (total,))
    total = (total + swap(total, "core")) * inverse
    here, there = total[:features].astype(BF16), total[features:].astype(BF16)
    moved = (
        swap(there, "yl"),
        swap(here, "yh"),
        lax.ppermute(there, ("yh", "yl"), [(i, 3 - i) for i in range(4)]),
    )
    at = jnp.stack([core, yh, yl])
    at, second, total, *moved = lax.optimization_barrier((at, second, total, *moved))
    result2 = output(second)
    return finish(at, result1, result2, total, moved)


def solution(mesh):
    fine = Mesh(mesh.devices.reshape(2, 2, 2, 4, 4), FINE)
    rows, tok = P(FINE, None), P(("yl", "z", "x"), None)
    return jax.shard_map(
        shards,
        mesh=fine,
        in_specs=(rows, rows, tok, tok, tok),
        out_specs=(rows, rows, tok, tok),
        check_vma=False,
    )
```

```python
import jax
import jax.numpy as jnp
from jax import lax
from jax.experimental import pallas as pl
from jax.experimental.pallas import tpu as pltpu
from jax.sharding import Mesh
from jax.sharding import PartitionSpec as P

BLOCK = 128
FINE = ("yh", "core", "yl", "z", "x")
PLANE = ("yh", "yl", "x")
F32 = jnp.float32
BF16 = jnp.bfloat16


WHOLE = pl.BlockSpec(memory_space=pltpu.VMEM)
LEFT = pl.BlockSpec(memory_space=pl.ANY)
SCALAR = pl.BlockSpec(memory_space=pltpu.SMEM)


def params():
    return pltpu.CompilerParams(vmem_limit_bytes=12 << 20)


def pack_kernel(z_ref, float_ref, quant_ref, out_ref):
    width = float_ref.shape[1] // 32
    z = z_ref[0]
    for kind, ref in enumerate((float_ref, quant_ref)):
        for j in range(4):
            zj = lax.rem(z + j, 4)
            for yl in range(2):
                for x in range(4):
                    start = pl.multiple_of(((yl * 4 + zj) * 4 + x) * width, width)
                    block = ref[:, pl.ds(start, width)]
                    for half in range(2):
                        at = (j * 2 + (yl ^ half)) * width
                        out_ref[kind * 8 + half * 4 + x, :, at : at + width] = block
    quant = quant_ref[:, :BLOCK]
    shift = (float_ref[:, :BLOCK].astype(F32) - quant.astype(F32)).astype(BF16)
    for d in range(16):
        out_ref[d, :, 8 * width :] = shift if d // 4 % 2 else quant


def pack(z, attn_float, attn_quant):
    tokens, d_in = attn_float.shape
    return pl.pallas_call(
        pack_kernel,
        out_shape=jax.ShapeDtypeStruct((16, tokens, d_in // 4 + BLOCK), BF16),
        in_specs=[SCALAR, WHOLE, WHOLE],
        out_specs=WHOLE,
        compiler_params=params(),
        name="pack",
    )(z.reshape(1), attn_float, attn_quant)


def project_kernel(acts_ref, *refs):
    weights, out_ref = refs[:4], refs[-1]
    depth, width = weights[0].shape
    tile = 512
    for col in range(0, width, tile):
        total = None
        for j, ref in enumerate(weights):
            term = jnp.dot(
                acts_ref[:, j * depth : (j + 1) * depth],
                ref[:, col : col + tile],
                preferred_element_type=F32,
            )
            total = term if total is None else total + term
        out_ref[:, col : col + tile] = total.astype(BF16)


def project(acts, weights, after):
    rows, cols = acts.shape[0], weights[0].shape[1]
    step = 256
    return pl.pallas_call(
        project_kernel,
        out_shape=jax.ShapeDtypeStruct((rows, cols), BF16),
        grid=(rows // step,),
        in_specs=[pl.BlockSpec((step, acts.shape[1]), lambda i: (i, 0))]
        + [
            pl.BlockSpec(w.shape, lambda i: (0, 0), pipeline_mode=pl.Buffered(1)) for w in weights
        ]
        + [LEFT] * len(after),
        out_specs=pl.BlockSpec((step, cols), lambda i: (i, 0)),
        compiler_params=params(),
        cost_estimate=pl.CostEstimate(
            flops=2 * rows * 2048 * cols, bytes_accessed=12 << 20, transcendentals=0
        ),
        name="project",
    )(acts, *weights, *after)


def finish_kernel(at_ref, first_ref, second_ref, total_ref, *refs):
    (side_ref, down_ref, cross_ref), outs = refs[:3], refs[3:]
    core, yh, yl = at_ref[0], at_ref[1], at_ref[2]
    width = first_ref.shape[2]
    for q, ref in enumerate((first_ref, second_ref)):
        quarter = core if q == 0 else 1 - core
        for kind, out in enumerate(outs[:2]):
            for half in range(2):
                at = kind * 8 + half * 4
                total = ref[at].astype(F32)
                for x in range(1, 4):
                    total += ref[at + x].astype(F32)
                start = pl.multiple_of((half * 2 + quarter) * width, width)
                out[:, pl.ds(start, width)] = total.astype(BF16)
    rows = outs[2].shape[0]
    own = jnp.where(yh == 1, total_ref[:rows], down_ref[...].astype(F32))
    other = jnp.where(yh == 1, side_ref[...].astype(F32), cross_ref[...].astype(F32))
    outs[2][...] = jnp.where(yl == 0, own, other)
    outs[3][...] = jnp.where(yl == 0, other, own)


def finish(at, first, second, total, moved):
    tokens, cols = first.shape[1:]
    rows = total.shape[0] // 2
    return pl.pallas_call(
        finish_kernel,
        out_shape=(jax.ShapeDtypeStruct((tokens, 4 * cols), BF16),) * 2
        + (jax.ShapeDtypeStruct((rows, BLOCK), F32),) * 2,
        in_specs=[SCALAR] + [WHOLE] * (3 + len(moved)),
        out_specs=(WHOLE,) * 4,
        compiler_params=params(),
        name="finish",
    )(at, first, second, total, *moved)


def stats_kernel(acts_ref, after_ref, *outs):
    width = outs[0].shape[0]
    for j, out in enumerate(outs):
        out[...] = lax.dot_general(
            acts_ref[:, j * width : (j + 1) * width],
            acts_ref[:, 4 * width :],
            (((0,), (0,)), ((), ())),
            preferred_element_type=F32,
        ).astype(out.dtype)


def stats(acts, after):
    width = (acts.shape[1] - BLOCK) // 4
    return pl.pallas_call(
        stats_kernel,
        out_shape=(jax.ShapeDtypeStruct((width, BLOCK), F32),)
        + (jax.ShapeDtypeStruct((width, BLOCK), BF16),) * 3,
        in_specs=[WHOLE, LEFT],
        out_specs=(WHOLE,) * 4,
        compiler_params=params(),
        name="stats",
    )(acts, after)


def swap(a, axis):
    return lax.ppermute(a, axis, [(0, 1), (1, 0)])


def ahead(a, axis, j):
    return lax.ppermute(a, axis, [((i + j) % 4, i) for i in range(4)])


def shards(attn_float, attn_quant, proj_weight, weight_codes, group_scales):
    tokens, d_in = attn_float.shape
    features, d_out = proj_weight.shape
    groups = group_scales.shape[0]
    half, quarter = d_out // 2, d_out // 4
    inverse = 1.0 / (tokens * 128)
    yh, core, yl, z = (lax.axis_index(a) for a in ("yh", "core", "yl", "z"))

    def weight(kind, col):
        plain = lax.dynamic_slice_in_dim(proj_weight, col, quarter, 1)
        codes = lax.dynamic_slice_in_dim(weight_codes, col, quarter, 1)
        scales = lax.dynamic_slice_in_dim(group_scales, col, quarter, 1)
        values = (codes - 8).astype(F32).reshape(groups, features // groups, quarter)
        quant = (values * scales[:, None, :]).reshape(features, quarter).astype(BF16)
        return jnp.where(kind == 0, plain, quant)

    send = weight(yh ^ core, (1 - yl) * half + core * quarter)
    pairs = []
    for a in range(2):
        for c in range(2):
            for b in range(2):
                pairs.append((a * 4 + c * 2 + b, (a ^ c) * 4 + c * 2 + (1 - b)))
    got = lax.ppermute(send, ("yh", "core", "yl"), pairs)
    col, send = lax.optimization_barrier((yl * half + core * quarter, send))
    own = weight(yh, col)

    payload = pack(z, attn_float, attn_quant)
    payload, got = lax.optimization_barrier((payload, got))
    rows = jnp.concatenate([own, got], axis=0)
    parts = [rows] + [ahead(rows, "z", j) for j in (1, 2, 3)]

    acts = lax.all_to_all(payload, PLANE, 0, 0, tiled=True).reshape(16 * tokens, -1)
    others = [swap(p, "core") for p in parts]

    def output(p):
        return lax.all_to_all(p.reshape(16, tokens, quarter), PLANE, 0, 0, tiled=True)

    first = project(acts, parts, others)
    result1 = output(first)

    blocks = stats(acts, first)
    total = blocks[0]
    for j in (1, 2, 3):
        total = total + ahead(blocks[j], "z", 4 - j).astype(F32)
    second = project(acts, others, (blocks[0],))
    total = (total + swap(total, "core")) * inverse
    here, there = total[:features].astype(BF16), total[features:].astype(BF16)
    moved = (
        swap(there, "yl"),
        swap(here, "yh"),
        lax.ppermute(there, ("yh", "yl"), [(i, 3 - i) for i in range(4)]),
    )
    at = jnp.stack([core, yh, yl])
    at, second, total, *moved = lax.optimization_barrier((at, second, total, *moved))
    result2 = output(second)
    return finish(at, result1, result2, total, moved)


def solution(mesh):
    fine = Mesh(mesh.devices.reshape(2, 2, 2, 4, 4), FINE)
    rows, tok = P(FINE, None), P(("yl", "z", "x"), None)
    return jax.shard_map(
        shards,
        mesh=fine,
        in_specs=(rows, rows, tok, tok, tok),
        out_specs=(rows, rows, tok, tok),
        check_vma=False,
    )
```

```python
import jax
import jax.numpy as jnp
from jax import lax
from jax.experimental import pallas as pl
from jax.experimental.pallas import tpu as pltpu
from jax.sharding import Mesh
from jax.sharding import PartitionSpec as P

BLOCK = 128
FINE = ("yh", "core", "yl", "z", "x")
PLANE = ("yh", "yl", "x")
F32 = jnp.float32
BF16 = jnp.bfloat16


WHOLE = pl.BlockSpec(memory_space=pltpu.VMEM)
LEFT = pl.BlockSpec(memory_space=pl.ANY)
SCALAR = pl.BlockSpec(memory_space=pltpu.SMEM)


def params():
    return pltpu.CompilerParams(vmem_limit_bytes=16 << 20)


def pack_kernel(z_ref, float_ref, quant_ref, out_ref):
    width = float_ref.shape[1] // 32
    z = z_ref[0]
    for kind, ref in enumerate((float_ref, quant_ref)):
        for j in range(4):
            zj = lax.rem(z + j, 4)
            for yl in range(2):
                for x in range(4):
                    start = pl.multiple_of(((yl * 4 + zj) * 4 + x) * width, width)
                    block = ref[:, pl.ds(start, width)]
                    for half in range(2):
                        at = (j * 2 + (yl ^ half)) * width
                        out_ref[kind * 8 + half * 4 + x, :, at : at + width] = block
    quant = quant_ref[:, :BLOCK]
    shift = (float_ref[:, :BLOCK].astype(F32) - quant.astype(F32)).astype(BF16)
    for d in range(16):
        out_ref[d, :, 8 * width :] = shift if d // 4 % 2 else quant


def pack(z, attn_float, attn_quant):
    tokens, d_in = attn_float.shape
    return pl.pallas_call(
        pack_kernel,
        out_shape=jax.ShapeDtypeStruct((16, tokens, d_in // 4 + BLOCK), BF16),
        in_specs=[SCALAR, WHOLE, WHOLE],
        out_specs=WHOLE,
        compiler_params=params(),
        name="pack",
    )(z.reshape(1), attn_float, attn_quant)


def project_kernel(acts_ref, weight_ref, out_ref):
    depth, width = weight_ref.shape
    tile = 512
    for col in range(0, width, tile):
        out_ref[:, col : col + tile] = jnp.dot(
            acts_ref[:, :depth], weight_ref[:, col : col + tile], preferred_element_type=F32
        ).astype(BF16)


def project(acts, weight):
    rows, (depth, cols) = acts.shape[0], weight.shape
    step = 256
    return pl.pallas_call(
        project_kernel,
        out_shape=jax.ShapeDtypeStruct((rows, cols), BF16),
        grid=(rows // step,),
        in_specs=[pl.BlockSpec((step, acts.shape[1]), lambda i: (i, 0)), WHOLE],
        out_specs=pl.BlockSpec((step, cols), lambda i: (i, 0)),
        compiler_params=params(),
        cost_estimate=pl.CostEstimate(
            flops=2 * rows * depth * cols, bytes_accessed=12 << 20, transcendentals=0
        ),
        name="project",
    )(acts, weight)


def finish_kernel(at_ref, first_ref, second_ref, total_ref, *refs):
    (side_ref, down_ref, cross_ref), outs = refs[:3], refs[3:]
    core, yh, yl = at_ref[0], at_ref[1], at_ref[2]
    width = first_ref.shape[2]
    for q, ref in enumerate((first_ref, second_ref)):
        quarter = core if q == 0 else 1 - core
        for kind, out in enumerate(outs[:2]):
            for half in range(2):
                at = kind * 8 + half * 4
                total = ref[at].astype(F32)
                for x in range(1, 4):
                    total += ref[at + x].astype(F32)
                start = pl.multiple_of((half * 2 + quarter) * width, width)
                out[:, pl.ds(start, width)] = total.astype(BF16)
    rows = outs[2].shape[0]
    own = jnp.where(yh == 1, total_ref[:rows], down_ref[...].astype(F32))
    other = jnp.where(yh == 1, side_ref[...].astype(F32), cross_ref[...].astype(F32))
    outs[2][...] = jnp.where(yl == 0, own, other)
    outs[3][...] = jnp.where(yl == 0, other, own)


def finish(at, first, second, total, moved):
    tokens, cols = first.shape[1:]
    rows = total.shape[0] // 2
    return pl.pallas_call(
        finish_kernel,
        out_shape=(jax.ShapeDtypeStruct((tokens, 4 * cols), BF16),) * 2
        + (jax.ShapeDtypeStruct((rows, BLOCK), F32),) * 2,
        in_specs=[SCALAR] + [WHOLE] * (3 + len(moved)),
        out_specs=(WHOLE,) * 4,
        compiler_params=params(),
        name="finish",
    )(at, first, second, total, *moved)


def stats_kernel(acts_ref, after_ref, *outs):
    width = outs[0].shape[0]
    for j, out in enumerate(outs):
        out[...] = lax.dot_general(
            acts_ref[:, j * width : (j + 1) * width],
            acts_ref[:, 4 * width :],
            (((0,), (0,)), ((), ())),
            preferred_element_type=F32,
        ).astype(out.dtype)


def stats(acts, after):
    width = (acts.shape[1] - BLOCK) // 4
    return pl.pallas_call(
        stats_kernel,
        out_shape=(jax.ShapeDtypeStruct((width, BLOCK), F32),)
        + (jax.ShapeDtypeStruct((width, BLOCK), BF16),) * 3,
        in_specs=[WHOLE, LEFT],
        out_specs=(WHOLE,) * 4,
        compiler_params=params(),
        name="stats",
    )(acts, after)


def swap(a, axis):
    return lax.ppermute(a, axis, [(0, 1), (1, 0)])


def ahead(a, axis, j):
    return lax.ppermute(a, axis, [((i + j) % 4, i) for i in range(4)])


def shards(attn_float, attn_quant, proj_weight, weight_codes, group_scales):
    tokens, d_in = attn_float.shape
    features, d_out = proj_weight.shape
    groups = group_scales.shape[0]
    half, quarter = d_out // 2, d_out // 4
    inverse = 1.0 / (tokens * 128)
    yh, core, yl, z = (lax.axis_index(a) for a in ("yh", "core", "yl", "z"))

    def weight(kind, col):
        plain = lax.dynamic_slice_in_dim(proj_weight, col, quarter, 1)
        codes = lax.dynamic_slice_in_dim(weight_codes, col, quarter, 1)
        scales = lax.dynamic_slice_in_dim(group_scales, col, quarter, 1)
        values = (codes - 8).astype(F32).reshape(groups, features // groups, quarter)
        quant = (values * scales[:, None, :]).reshape(features, quarter).astype(BF16)
        return jnp.where(kind == 0, plain, quant)

    send = weight(yh ^ core, (1 - yl) * half + core * quarter)
    pairs = []
    for a in range(2):
        for c in range(2):
            for b in range(2):
                pairs.append((a * 4 + c * 2 + b, (a ^ c) * 4 + c * 2 + (1 - b)))
    got = lax.ppermute(send, ("yh", "core", "yl"), pairs)
    col, send = lax.optimization_barrier((yl * half + core * quarter, send))
    own = weight(yh, col)

    payload = pack(z, attn_float, attn_quant)
    payload, got = lax.optimization_barrier((payload, got))
    rows = jnp.concatenate([own, got], axis=0)
    parts = [rows] + [ahead(rows, "z", j) for j in (1, 2, 3)]

    acts = lax.all_to_all(payload, PLANE, 0, 0, tiled=True).reshape(16 * tokens, -1)
    mine = jnp.concatenate(parts, axis=0)
    other = swap(mine, "core")

    def output(p):
        return lax.all_to_all(p.reshape(16, tokens, quarter), PLANE, 0, 0, tiled=True)

    first = project(acts, mine)
    result1 = output(first)

    blocks = stats(acts, first)
    total = blocks[0]
    for j in (1, 2, 3):
        total = total + ahead(blocks[j], "z", 4 - j).astype(F32)
    second = project(acts, other)
    total = (total + swap(total, "core")) * inverse
    here, there = total[:features].astype(BF16), total[features:].astype(BF16)
    moved = (
        swap(there, "yl"),
        swap(here, "yh"),
        lax.ppermute(there, ("yh", "yl"), [(i, 3 - i) for i in range(4)]),
    )
    at = jnp.stack([core, yh, yl])
    at, second, total, *moved = lax.optimization_barrier((at, second, total, *moved))
    result2 = output(second)
    return finish(at, result1, result2, total, moved)


def solution(mesh):
    fine = Mesh(mesh.devices.reshape(2, 2, 2, 4, 4), FINE)
    rows, tok = P(FINE, None), P(("yl", "z", "x"), None)
    return jax.shard_map(
        shards,
        mesh=fine,
        in_specs=(rows, rows, tok, tok, tok),
        out_specs=(rows, rows, tok, tok),
        check_vma=False,
    )
```

```python
import jax
import jax.numpy as jnp
from jax import lax
from jax.experimental import pallas as pl
from jax.experimental.pallas import tpu as pltpu
from jax.sharding import Mesh
from jax.sharding import PartitionSpec as P

BLOCK = 128
FINE = ("yh", "core", "yl", "z", "x")
PLANE = ("yh", "yl", "x")
F32 = jnp.float32
BF16 = jnp.bfloat16


WHOLE = pl.BlockSpec(memory_space=pltpu.VMEM)
LEFT = pl.BlockSpec(memory_space=pl.ANY)
SCALAR = pl.BlockSpec(memory_space=pltpu.SMEM)


def params():
    return pltpu.CompilerParams(vmem_limit_bytes=16 << 20)


def pack_kernel(z_ref, float_ref, quant_ref, out_ref):
    width = float_ref.shape[1] // 32
    z = z_ref[0]
    for kind, ref in enumerate((float_ref, quant_ref)):
        for j in range(4):
            zj = lax.rem(z + j, 4)
            for yl in range(2):
                for x in range(4):
                    start = pl.multiple_of(((yl * 4 + zj) * 4 + x) * width, width)
                    block = ref[:, pl.ds(start, width)]
                    for half in range(2):
                        at = (j * 2 + (yl ^ half)) * width
                        out_ref[kind * 8 + half * 4 + x, :, at : at + width] = block
    quant = quant_ref[:, :BLOCK]
    shift = (float_ref[:, :BLOCK].astype(F32) - quant.astype(F32)).astype(BF16)
    for d in range(16):
        out_ref[d, :, 8 * width :] = shift if d // 4 % 2 else quant


def pack(z, attn_float, attn_quant):
    tokens, d_in = attn_float.shape
    return pl.pallas_call(
        pack_kernel,
        out_shape=jax.ShapeDtypeStruct((16, tokens, d_in // 4 + BLOCK), BF16),
        in_specs=[SCALAR, WHOLE, WHOLE],
        out_specs=WHOLE,
        compiler_params=params(),
        name="pack",
    )(z.reshape(1), attn_float, attn_quant)


def project_kernel(acts_ref, weight_ref, out_ref):
    depth, width = weight_ref.shape
    tile = 512
    for col in range(0, width, tile):
        out_ref[:, col : col + tile] = jnp.dot(
            acts_ref[:, :depth], weight_ref[:, col : col + tile], preferred_element_type=F32
        ).astype(BF16)


def project(acts, weight):
    rows, (depth, cols) = acts.shape[0], weight.shape
    step = 256
    return pl.pallas_call(
        project_kernel,
        out_shape=jax.ShapeDtypeStruct((rows, cols), BF16),
        grid=(rows // step,),
        in_specs=[pl.BlockSpec((step, acts.shape[1]), lambda i: (i, 0)), WHOLE],
        out_specs=pl.BlockSpec((step, cols), lambda i: (i, 0)),
        compiler_params=params(),
        cost_estimate=pl.CostEstimate(
            flops=2 * rows * depth * cols, bytes_accessed=12 << 20, transcendentals=0
        ),
        name="project",
    )(acts, weight)


def finish_kernel(at_ref, first_ref, second_ref, total_ref, *refs):
    (side_ref, down_ref, cross_ref), outs = refs[:3], refs[3:]
    core, yh, yl = at_ref[0], at_ref[1], at_ref[2]
    width = first_ref.shape[2]
    for q, ref in enumerate((first_ref, second_ref)):
        quarter = core if q == 0 else 1 - core
        for kind, out in enumerate(outs[:2]):
            for half in range(2):
                at = kind * 8 + half * 4
                total = ref[at].astype(F32)
                for x in range(1, 4):
                    total += ref[at + x].astype(F32)
                start = pl.multiple_of((half * 2 + quarter) * width, width)
                out[:, pl.ds(start, width)] = total.astype(BF16)
    rows = outs[2].shape[0]
    own = jnp.where(yh == 1, total_ref[:rows], down_ref[...].astype(F32))
    other = jnp.where(yh == 1, side_ref[...].astype(F32), cross_ref[...].astype(F32))
    outs[2][...] = jnp.where(yl == 0, own, other)
    outs[3][...] = jnp.where(yl == 0, other, own)


def finish(at, first, second, total, moved):
    tokens, cols = first.shape[1:]
    rows = total.shape[0] // 2
    return pl.pallas_call(
        finish_kernel,
        out_shape=(jax.ShapeDtypeStruct((tokens, 4 * cols), BF16),) * 2
        + (jax.ShapeDtypeStruct((rows, BLOCK), F32),) * 2,
        in_specs=[SCALAR] + [WHOLE] * (3 + len(moved)),
        out_specs=(WHOLE,) * 4,
        compiler_params=params(),
        name="finish",
    )(at, first, second, total, *moved)


def stats_kernel(acts_ref, after_ref, *outs):
    width = outs[0].shape[0]
    for j, out in enumerate(outs):
        out[...] = lax.dot_general(
            acts_ref[:, j * width : (j + 1) * width],
            acts_ref[:, 4 * width :],
            (((0,), (0,)), ((), ())),
            preferred_element_type=F32,
        ).astype(out.dtype)


def stats(acts, after):
    width = (acts.shape[1] - BLOCK) // 4
    return pl.pallas_call(
        stats_kernel,
        out_shape=(jax.ShapeDtypeStruct((width, BLOCK), F32),)
        + (jax.ShapeDtypeStruct((width, BLOCK), BF16),) * 3,
        in_specs=[WHOLE, LEFT],
        out_specs=(WHOLE,) * 4,
        compiler_params=params(),
        name="stats",
    )(acts, after)


def swap(a, axis):
    return lax.ppermute(a, axis, [(0, 1), (1, 0)])


def ahead(a, axis, j):
    return lax.ppermute(a, axis, [((i + j) % 4, i) for i in range(4)])


def shards(attn_float, attn_quant, proj_weight, weight_codes, group_scales):
    tokens, d_in = attn_float.shape
    features, d_out = proj_weight.shape
    groups = group_scales.shape[0]
    half, quarter = d_out // 2, d_out // 4
    inverse = 1.0 / (tokens * 128)
    yh, core, yl, z = (lax.axis_index(a) for a in ("yh", "core", "yl", "z"))

    def weight(kind, col):
        plain = lax.dynamic_slice_in_dim(proj_weight, col, quarter, 1)
        codes = lax.dynamic_slice_in_dim(weight_codes, col, quarter, 1)
        scales = lax.dynamic_slice_in_dim(group_scales, col, quarter, 1)
        values = (codes - 8).astype(F32).reshape(groups, features // groups, quarter)
        quant = (values * scales[:, None, :]).reshape(features, quarter).astype(BF16)
        return jnp.where(kind == 0, plain, quant)

    own = weight(yh, yl * half + core * quarter)
    send = weight(yh ^ core, (1 - yl) * half + core * quarter)
    pairs = []
    for a in range(2):
        for c in range(2):
            for b in range(2):
                pairs.append((a * 4 + c * 2 + b, (a ^ c) * 4 + c * 2 + (1 - b)))
    got = lax.ppermute(send, ("yh", "core", "yl"), pairs)
    payload = pack(z, attn_float, attn_quant)
    rows = jnp.concatenate([own, got], axis=0)
    parts = [rows] + [ahead(rows, "z", j) for j in (1, 2, 3)]

    acts = lax.all_to_all(payload, PLANE, 0, 0, tiled=True).reshape(16 * tokens, -1)
    mine = jnp.concatenate(parts, axis=0)
    other = swap(mine, "core")

    def output(p):
        return lax.all_to_all(p.reshape(16, tokens, quarter), PLANE, 0, 0, tiled=True)

    first = project(acts, mine)
    result1 = output(first)

    blocks = stats(acts, first)
    total = blocks[0]
    came = [ahead(blocks[j], "z", 4 - j) for j in (1, 2, 3)]
    second = project(acts, other)
    second, *came = lax.optimization_barrier((second, *came))
    for block in came:
        total = total + block.astype(F32)
    total = (total + swap(total, "core")) * inverse
    here, there = total[:features].astype(BF16), total[features:].astype(BF16)
    moved = (
        swap(there, "yl"),
        swap(here, "yh"),
        lax.ppermute(there, ("yh", "yl"), [(i, 3 - i) for i in range(4)]),
    )
    at = jnp.stack([core, yh, yl])
    at, second, total, *moved = lax.optimization_barrier((at, second, total, *moved))
    result2 = output(second)
    return finish(at, result1, result2, total, moved)


def solution(mesh):
    fine = Mesh(mesh.devices.reshape(2, 2, 2, 4, 4), FINE)
    rows, tok = P(FINE, None), P(("yl", "z", "x"), None)
    return jax.shard_map(
        shards,
        mesh=fine,
        in_specs=(rows, rows, tok, tok, tok),
        out_specs=(rows, rows, tok, tok),
        check_vma=False,
    )
```

```python
import jax
import jax.numpy as jnp
from jax import lax
from jax.experimental import pallas as pl
from jax.experimental.pallas import tpu as pltpu
from jax.sharding import Mesh
from jax.sharding import PartitionSpec as P

BLOCK = 128
FINE = ("yh", "core", "yl", "z", "x")
PLANE = ("yh", "yl", "x")
F32 = jnp.float32
BF16 = jnp.bfloat16


WHOLE = pl.BlockSpec(memory_space=pltpu.VMEM)
LEFT = pl.BlockSpec(memory_space=pl.ANY)
SCALAR = pl.BlockSpec(memory_space=pltpu.SMEM)


def params():
    return pltpu.CompilerParams(vmem_limit_bytes=16 << 20)


def pack_kernel(z_ref, float_ref, quant_ref, out_ref):
    width = float_ref.shape[1] // 32
    z = z_ref[0]
    for kind, ref in enumerate((float_ref, quant_ref)):
        for j in range(4):
            zj = lax.rem(z + j, 4)
            for yl in range(2):
                for x in range(4):
                    start = pl.multiple_of(((yl * 4 + zj) * 4 + x) * width, width)
                    block = ref[:, pl.ds(start, width)]
                    for half in range(2):
                        at = (j * 2 + (yl ^ half)) * width
                        out_ref[kind * 8 + half * 4 + x, :, at : at + width] = block
    quant = quant_ref[:, :BLOCK]
    shift = (float_ref[:, :BLOCK].astype(F32) - quant.astype(F32)).astype(BF16)
    for d in range(16):
        out_ref[d, :, 8 * width :] = shift if d // 4 % 2 else quant


def pack(z, attn_float, attn_quant):
    tokens, d_in = attn_float.shape
    return pl.pallas_call(
        pack_kernel,
        out_shape=jax.ShapeDtypeStruct((16, tokens, d_in // 4 + BLOCK), BF16),
        in_specs=[SCALAR, WHOLE, WHOLE],
        out_specs=WHOLE,
        compiler_params=params(),
        name="pack",
    )(z.reshape(1), attn_float, attn_quant)


def project_kernel(acts_ref, weight_ref, out_ref):
    depth, width = weight_ref.shape
    tile = 512
    for col in range(0, width, tile):
        out_ref[:, col : col + tile] = jnp.dot(
            acts_ref[:, :depth], weight_ref[:, col : col + tile], preferred_element_type=F32
        ).astype(BF16)


def project(acts, weight):
    rows, (depth, cols) = acts.shape[0], weight.shape
    step = 256
    return pl.pallas_call(
        project_kernel,
        out_shape=jax.ShapeDtypeStruct((rows, cols), BF16),
        grid=(rows // step,),
        in_specs=[pl.BlockSpec((step, acts.shape[1]), lambda i: (i, 0)), WHOLE],
        out_specs=pl.BlockSpec((step, cols), lambda i: (i, 0)),
        compiler_params=params(),
        cost_estimate=pl.CostEstimate(
            flops=2 * rows * depth * cols, bytes_accessed=12 << 20, transcendentals=0
        ),
        name="project",
    )(acts, weight)


def finish_kernel(at_ref, first_ref, second_ref, total_ref, *refs):
    (side_ref, down_ref, cross_ref), outs = refs[:3], refs[3:]
    core, yh, yl = at_ref[0], at_ref[1], at_ref[2]
    width = first_ref.shape[2]
    for q, ref in enumerate((first_ref, second_ref)):
        quarter = core if q == 0 else 1 - core
        for kind, out in enumerate(outs[:2]):
            for half in range(2):
                at = kind * 8 + half * 4
                total = ref[at].astype(F32)
                for x in range(1, 4):
                    total += ref[at + x].astype(F32)
                start = pl.multiple_of((half * 2 + quarter) * width, width)
                out[:, pl.ds(start, width)] = total.astype(BF16)
    rows = outs[2].shape[0]
    own = jnp.where(yh == 1, total_ref[:rows], down_ref[...].astype(F32))
    other = jnp.where(yh == 1, side_ref[...].astype(F32), cross_ref[...].astype(F32))
    outs[2][...] = jnp.where(yl == 0, own, other)
    outs[3][...] = jnp.where(yl == 0, other, own)


def finish(at, first, second, total, moved):
    tokens, cols = first.shape[1:]
    rows = total.shape[0] // 2
    return pl.pallas_call(
        finish_kernel,
        out_shape=(jax.ShapeDtypeStruct((tokens, 4 * cols), BF16),) * 2
        + (jax.ShapeDtypeStruct((rows, BLOCK), F32),) * 2,
        in_specs=[SCALAR] + [WHOLE] * (3 + len(moved)),
        out_specs=(WHOLE,) * 4,
        compiler_params=params(),
        name="finish",
    )(at, first, second, total, *moved)


def stats_kernel(acts_ref, after_ref, *outs):
    width = outs[0].shape[0]
    for j, out in enumerate(outs):
        out[...] = lax.dot_general(
            acts_ref[:, j * width : (j + 1) * width],
            acts_ref[:, 4 * width :],
            (((0,), (0,)), ((), ())),
            preferred_element_type=F32,
        ).astype(out.dtype)


def stats(acts, after):
    width = (acts.shape[1] - BLOCK) // 4
    return pl.pallas_call(
        stats_kernel,
        out_shape=(jax.ShapeDtypeStruct((width, BLOCK), F32),)
        + (jax.ShapeDtypeStruct((width, BLOCK), BF16),) * 3,
        in_specs=[WHOLE, LEFT],
        out_specs=(WHOLE,) * 4,
        compiler_params=params(),
        name="stats",
    )(acts, after)


def swap(a, axis):
    return lax.ppermute(a, axis, [(0, 1), (1, 0)])


def ahead(a, axis, j):
    return lax.ppermute(a, axis, [((i + j) % 4, i) for i in range(4)])


def shards(attn_float, attn_quant, proj_weight, weight_codes, group_scales):
    tokens, d_in = attn_float.shape
    features, d_out = proj_weight.shape
    groups = group_scales.shape[0]
    half, quarter = d_out // 2, d_out // 4
    inverse = 1.0 / (tokens * 128)
    yh, core, yl, z = (lax.axis_index(a) for a in ("yh", "core", "yl", "z"))

    def weight(kind, col):
        plain = lax.dynamic_slice_in_dim(proj_weight, col, quarter, 1)
        codes = lax.dynamic_slice_in_dim(weight_codes, col, quarter, 1)
        scales = lax.dynamic_slice_in_dim(group_scales, col, quarter, 1)
        values = (codes - 8).astype(F32).reshape(groups, features // groups, quarter)
        quant = (values * scales[:, None, :]).reshape(features, quarter).astype(BF16)
        return jnp.where(kind == 0, plain, quant)

    send = weight(yh ^ core, (1 - yl) * half + core * quarter)
    pairs = []
    for a in range(2):
        for c in range(2):
            for b in range(2):
                pairs.append((a * 4 + c * 2 + b, (a ^ c) * 4 + c * 2 + (1 - b)))
    got = lax.ppermute(send, ("yh", "core", "yl"), pairs)
    col, send = lax.optimization_barrier((yl * half + core * quarter, send))
    own = weight(yh, col)

    payload = pack(z, attn_float, attn_quant)
    payload, got = lax.optimization_barrier((payload, got))
    rows = jnp.concatenate([own, got], axis=0)
    parts = [rows] + [ahead(rows, "z", j) for j in (1, 2, 3)]

    acts = lax.all_to_all(payload, PLANE, 0, 0, tiled=True).reshape(16 * tokens, -1)
    mine = jnp.concatenate(parts, axis=0)
    other = swap(mine, "core")

    def output(p):
        return lax.all_to_all(p.reshape(16, tokens, quarter), PLANE, 0, 0, tiled=True)

    first = project(acts, mine)
    result1 = output(first)

    blocks = stats(acts, first)
    total = blocks[0]
    came = [ahead(blocks[j], "z", 4 - j) for j in (1, 2, 3)]
    second = project(acts, other)
    second, *came = lax.optimization_barrier((second, *came))
    for block in came:
        total = total + block.astype(F32)
    total = (total + swap(total, "core")) * inverse
    here, there = total[:features].astype(BF16), total[features:].astype(BF16)
    moved = (
        swap(there, "yl"),
        swap(here, "yh"),
        lax.ppermute(there, ("yh", "yl"), [(i, 3 - i) for i in range(4)]),
    )
    at = jnp.stack([core, yh, yl])
    at, second, total, *moved = lax.optimization_barrier((at, second, total, *moved))
    result2 = output(second)
    return finish(at, result1, result2, total, moved)


def solution(mesh):
    fine = Mesh(mesh.devices.reshape(2, 2, 2, 4, 4), FINE)
    rows, tok = P(FINE, None), P(("yl", "z", "x"), None)
    return jax.shard_map(
        shards,
        mesh=fine,
        in_specs=(rows, rows, tok, tok, tok),
        out_specs=(rows, rows, tok, tok),
        check_vma=False,
    )
```

```python
import jax
import jax.numpy as jnp
from jax import lax
from jax.experimental import pallas as pl
from jax.experimental.pallas import tpu as pltpu
from jax.sharding import Mesh
from jax.sharding import PartitionSpec as P

BLOCK = 128
FINE = ("yh", "core", "yl", "z", "x")
PLANE = ("yh", "yl", "x")
F32 = jnp.float32
BF16 = jnp.bfloat16


WHOLE = pl.BlockSpec(memory_space=pltpu.VMEM)
SCALAR = pl.BlockSpec(memory_space=pltpu.SMEM)
LEFT = pl.BlockSpec(memory_space=pl.ANY)


def params(mib=16):
    return pltpu.CompilerParams(vmem_limit_bytes=mib << 20)


def pack_kernel(z_ref, float_ref, quant_ref, out_ref, block_ref):
    width = out_ref.shape[2] // 8
    z = z_ref[0]
    for kind, ref in enumerate((float_ref, quant_ref)):
        for j in range(4):
            zj = lax.rem(z + j, 4)
            for yl in range(2):
                for x in range(4):
                    start = pl.multiple_of(((yl * 4 + zj) * 4 + x) * width, width)
                    block = ref[:, pl.ds(start, width)]
                    for half in range(2):
                        at = (j * 2 + (yl ^ half)) * width
                        out_ref[kind * 8 + half * 4 + x, :, at : at + width] = block
    quant = quant_ref[:, :BLOCK]
    shift = (float_ref[:, :BLOCK].astype(F32) - quant.astype(F32)).astype(BF16)
    for d in range(16):
        block_ref[d, :, :BLOCK] = quant
        block_ref[d, :, BLOCK:] = shift


def pack(z, attn_float, attn_quant):
    tokens, d_in = attn_float.shape
    whole = pl.BlockSpec(memory_space=pltpu.VMEM)
    return pl.pallas_call(
        pack_kernel,
        out_shape=(
            jax.ShapeDtypeStruct((16, tokens, d_in // 4), BF16),
            jax.ShapeDtypeStruct((16, tokens, 2 * BLOCK), BF16),
        ),
        in_specs=[pl.BlockSpec(memory_space=pltpu.SMEM), whole, whole],
        out_specs=(whole, whole),
        compiler_params=params(40),
        name="pack",
    )(z.reshape(1), attn_float, attn_quant)


def project_kernel(acts_ref, weight_ref, out_ref):
    depth, width = weight_ref.shape
    tile = 512
    for col in range(0, width, tile):
        out_ref[:, col : col + tile] = jnp.dot(
            acts_ref[:, :depth], weight_ref[:, col : col + tile], preferred_element_type=F32
        ).astype(BF16)


def project(acts, weight):
    rows, (depth, cols) = acts.shape[0], weight.shape
    step = 256
    return pl.pallas_call(
        project_kernel,
        out_shape=jax.ShapeDtypeStruct((rows, cols), BF16),
        grid=(rows // step,),
        in_specs=[pl.BlockSpec((step, acts.shape[1]), lambda i: (i, 0)), WHOLE],
        out_specs=pl.BlockSpec((step, cols), lambda i: (i, 0)),
        compiler_params=params(),
        cost_estimate=pl.CostEstimate(
            flops=2 * rows * depth * cols, bytes_accessed=12 << 20, transcendentals=0
        ),
        name="project",
    )(acts, weight)


def finish_kernel(at_ref, first_ref, second_ref, total_ref, *refs):
    moved_ref, outs = refs[0], refs[1:]
    core, yh = at_ref[0], at_ref[1]
    width = first_ref.shape[2]
    for q, ref in enumerate((first_ref, second_ref)):
        quarter = core if q == 0 else 1 - core
        for kind, out in enumerate(outs[:2]):
            for half in range(2):
                at = kind * 8 + half * 4
                total = ref[at].astype(F32)
                for x in range(1, 4):
                    total += ref[at + x].astype(F32)
                start = pl.multiple_of((half * 2 + quarter) * width, width)
                out[:, pl.ds(start, width)] = total.astype(BF16)
    total = jnp.where(yh == 1, total_ref[...], moved_ref[...].astype(F32))
    outs[2][...] = total[:, :BLOCK]
    outs[3][...] = total[:, BLOCK:]


def finish(at, first, second, total, moved):
    tokens, cols = first.shape[1:]
    rows = total.shape[0]
    return pl.pallas_call(
        finish_kernel,
        out_shape=(jax.ShapeDtypeStruct((tokens, 4 * cols), BF16),) * 2
        + (jax.ShapeDtypeStruct((rows, BLOCK), F32),) * 2,
        in_specs=[SCALAR] + [WHOLE] * 4,
        out_specs=(WHOLE,) * 4,
        compiler_params=params(),
        name="finish",
    )(at, first, second, total, moved)


def stats_kernel(acts_ref, block_ref, after_ref, *outs):
    width = outs[0].shape[0]
    for j, out in enumerate(outs):
        out[...] = lax.dot_general(
            acts_ref[:, 2 * j * width : (2 * j + 1) * width],
            block_ref[...],
            (((0,), (0,)), ((), ())),
            preferred_element_type=F32,
        ).astype(out.dtype)


def stats(acts, block, after):
    width = 2 * BLOCK
    return pl.pallas_call(
        stats_kernel,
        out_shape=(jax.ShapeDtypeStruct((width, width), F32),)
        + (jax.ShapeDtypeStruct((width, width), BF16),) * 3,
        in_specs=[WHOLE, WHOLE, LEFT],
        out_specs=(WHOLE,) * 4,
        compiler_params=params(),
        name="stats",
    )(acts, block, after)


def swap(a, axis):
    return lax.ppermute(a, axis, [(0, 1), (1, 0)])


def shards(attn_float, attn_quant, proj_weight, weight_codes, group_scales):
    tokens, d_in = attn_float.shape
    features, d_out = proj_weight.shape
    groups = group_scales.shape[0]
    half, quarter = d_out // 2, d_out // 4
    inverse = 1.0 / (tokens * 128)
    yh, core, yl, z = (lax.axis_index(a) for a in ("yh", "core", "yl", "z"))

    def weight(kind, col):
        plain = lax.dynamic_slice_in_dim(proj_weight, col, quarter, 1)
        codes = lax.dynamic_slice_in_dim(weight_codes, col, quarter, 1)
        scales = lax.dynamic_slice_in_dim(group_scales, col, quarter, 1)
        values = (codes - 8).astype(F32).reshape(groups, features // groups, quarter)
        quant = (values * scales[:, None, :]).reshape(features, quarter).astype(BF16)
        return jnp.where(kind == 0, plain, quant)

    own = weight(yh, yl * half + core * quarter)
    send = weight(yh ^ core, (1 - yl) * half + core * quarter)
    pairs = []
    for a in range(2):
        for c in range(2):
            for b in range(2):
                pairs.append((a * 4 + c * 2 + b, (a ^ c) * 4 + c * 2 + (1 - b)))
    got = lax.ppermute(send, ("yh", "core", "yl"), pairs)

    payload, block_part = pack(z, attn_float, attn_quant)
    block_all = lax.all_to_all(block_part, PLANE, 0, 0, tiled=True)
    block_all = block_all.reshape(16 * tokens, 2 * BLOCK)

    rows = jnp.concatenate([own, got], axis=0)
    parts = [rows] + [
        lax.ppermute(rows, "z", [((i + j) % 4, i) for i in range(4)]) for j in (1, 2, 3)
    ]
    mine = jnp.concatenate(parts, axis=0)
    other = swap(mine, "core")

    acts = lax.all_to_all(payload, PLANE, 0, 0, tiled=True).reshape(16 * tokens, 8 * features)

    def output(p):
        return lax.all_to_all(p.reshape(16, tokens, quarter), PLANE, 0, 0, tiled=True)

    first = project(acts, mine)
    result1 = output(first)

    blocks = stats(acts, block_all, first)
    came = [
        lax.ppermute(blocks[j], "z", [(i, (i + j) % 4) for i in range(4)]) for j in (1, 2, 3)
    ]
    second = project(acts, other)
    second, *came = lax.optimization_barrier((second, *came))
    total = blocks[0]
    for block in came:
        total = total + block.astype(F32)
    total = (total + swap(total, "core")) * inverse
    moved = swap(total.astype(BF16), "yh")
    at = jnp.stack([core, yh])
    at, second, total, moved = lax.optimization_barrier((at, second, total, moved))
    result2 = output(second)
    return finish(at, result1, result2, total, moved)


def solution(mesh):
    fine = Mesh(mesh.devices.reshape(2, 2, 2, 4, 4), FINE)
    rows, tok = P(FINE, None), P(("yl", "z", "x"), None)
    return jax.shard_map(
        shards,
        mesh=fine,
        in_specs=(rows, rows, tok, tok, tok),
        out_specs=(rows, rows, tok, tok),
        check_vma=False,
    )
```

```python
import jax
import jax.numpy as jnp
from jax import lax
from jax.experimental import pallas as pl
from jax.experimental.pallas import tpu as pltpu
from jax.sharding import Mesh
from jax.sharding import PartitionSpec as P

BLOCK = 128
FINE = ("yh", "core", "yl", "z", "x")
PLANE = ("yh", "yl", "x")
F32 = jnp.float32
BF16 = jnp.bfloat16


WHOLE = pl.BlockSpec(memory_space=pltpu.VMEM)
LEFT = pl.BlockSpec(memory_space=pl.ANY)
SCALAR = pl.BlockSpec(memory_space=pltpu.SMEM)


def params():
    return pltpu.CompilerParams(vmem_limit_bytes=12 << 20)


def pack_kernel(z_ref, float_ref, quant_ref, out_ref):
    width = float_ref.shape[1] // 32
    z = z_ref[0]
    for kind, ref in enumerate((float_ref, quant_ref)):
        for j in range(4):
            zj = lax.rem(z + j, 4)
            for yl in range(2):
                for x in range(4):
                    start = pl.multiple_of(((yl * 4 + zj) * 4 + x) * width, width)
                    block = ref[:, pl.ds(start, width)]
                    for half in range(2):
                        at = (j * 2 + (yl ^ half)) * width
                        out_ref[kind * 8 + half * 4 + x, :, at : at + width] = block
    quant = quant_ref[:, :BLOCK]
    shift = (float_ref[:, :BLOCK].astype(F32) - quant.astype(F32)).astype(BF16)
    for d in range(16):
        out_ref[d, :, 8 * width :] = shift if d // 4 % 2 else quant


def pack(z, attn_float, attn_quant):
    tokens, d_in = attn_float.shape
    return pl.pallas_call(
        pack_kernel,
        out_shape=jax.ShapeDtypeStruct((16, tokens, d_in // 4 + BLOCK), BF16),
        in_specs=[SCALAR, WHOLE, WHOLE],
        out_specs=WHOLE,
        compiler_params=params(),
        name="pack",
    )(z.reshape(1), attn_float, attn_quant)


def project_kernel(acts_ref, *refs):
    weights, out_ref = refs[:4], refs[-1]
    depth, width = weights[0].shape
    tile = 512
    for col in range(0, width, tile):
        total = None
        for j, ref in enumerate(weights):
            term = jnp.dot(
                acts_ref[:, j * depth : (j + 1) * depth],
                ref[:, col : col + tile],
                preferred_element_type=F32,
            )
            total = term if total is None else total + term
        out_ref[:, col : col + tile] = total.astype(BF16)


def project(acts, weights, after):
    rows, cols = acts.shape[0], weights[0].shape[1]
    step = 256
    return pl.pallas_call(
        project_kernel,
        out_shape=jax.ShapeDtypeStruct((rows, cols), BF16),
        grid=(rows // step,),
        in_specs=[pl.BlockSpec((step, acts.shape[1]), lambda i: (i, 0))] + [WHOLE] * len(weights)
        + [LEFT] * len(after),
        out_specs=pl.BlockSpec((step, cols), lambda i: (i, 0)),
        compiler_params=params(),
        cost_estimate=pl.CostEstimate(
            flops=2 * rows * 2048 * cols, bytes_accessed=12 << 20, transcendentals=0
        ),
        name="project",
    )(acts, *weights, *after)


def finish_kernel(at_ref, first_ref, second_ref, total_ref, *refs):
    (side_ref, down_ref, cross_ref), outs = refs[:3], refs[3:]
    core, yh, yl = at_ref[0], at_ref[1], at_ref[2]
    width = first_ref.shape[2]
    for q, ref in enumerate((first_ref, second_ref)):
        quarter = core if q == 0 else 1 - core
        for kind, out in enumerate(outs[:2]):
            for half in range(2):
                at = kind * 8 + half * 4
                total = ref[at].astype(F32)
                for x in range(1, 4):
                    total += ref[at + x].astype(F32)
                start = pl.multiple_of((half * 2 + quarter) * width, width)
                out[:, pl.ds(start, width)] = total.astype(BF16)
    rows = outs[2].shape[0]
    own = jnp.where(yh == 1, total_ref[:rows], down_ref[...].astype(F32))
    other = jnp.where(yh == 1, side_ref[...].astype(F32), cross_ref[...].astype(F32))
    outs[2][...] = jnp.where(yl == 0, own, other)
    outs[3][...] = jnp.where(yl == 0, other, own)


def finish(at, first, second, total, moved):
    tokens, cols = first.shape[1:]
    rows = total.shape[0] // 2
    return pl.pallas_call(
        finish_kernel,
        out_shape=(jax.ShapeDtypeStruct((tokens, 4 * cols), BF16),) * 2
        + (jax.ShapeDtypeStruct((rows, BLOCK), F32),) * 2,
        in_specs=[SCALAR] + [WHOLE] * (3 + len(moved)),
        out_specs=(WHOLE,) * 4,
        compiler_params=params(),
        name="finish",
    )(at, first, second, total, *moved)


def stats_kernel(acts_ref, after_ref, *outs):
    width = outs[0].shape[0]
    for j, out in enumerate(outs):
        out[...] = lax.dot_general(
            acts_ref[:, j * width : (j + 1) * width],
            acts_ref[:, 4 * width :],
            (((0,), (0,)), ((), ())),
            preferred_element_type=F32,
        ).astype(out.dtype)


def stats(acts, after):
    width = (acts.shape[1] - BLOCK) // 4
    return pl.pallas_call(
        stats_kernel,
        out_shape=(jax.ShapeDtypeStruct((width, BLOCK), F32),)
        + (jax.ShapeDtypeStruct((width, BLOCK), BF16),) * 3,
        in_specs=[WHOLE, LEFT],
        out_specs=(WHOLE,) * 4,
        compiler_params=params(),
        name="stats",
    )(acts, after)


def tick_kernel(acts_ref, out_ref):
    out_ref[...] = jnp.zeros_like(out_ref)


def tick(acts):
    return pl.pallas_call(
        tick_kernel,
        out_shape=jax.ShapeDtypeStruct((8, 128), F32),
        in_specs=[LEFT],
        out_specs=WHOLE,
        compiler_params=params(),
        name="tick",
    )(acts)


def swap(a, axis):
    return lax.ppermute(a, axis, [(0, 1), (1, 0)])


def ahead(a, axis, j):
    return lax.ppermute(a, axis, [((i + j) % 4, i) for i in range(4)])


def shards(attn_float, attn_quant, proj_weight, weight_codes, group_scales):
    tokens, d_in = attn_float.shape
    features, d_out = proj_weight.shape
    groups = group_scales.shape[0]
    half, quarter = d_out // 2, d_out // 4
    inverse = 1.0 / (tokens * 128)
    yh, core, yl, z = (lax.axis_index(a) for a in ("yh", "core", "yl", "z"))

    def weight(kind, col):
        plain = lax.dynamic_slice_in_dim(proj_weight, col, quarter, 1)
        codes = lax.dynamic_slice_in_dim(weight_codes, col, quarter, 1)
        scales = lax.dynamic_slice_in_dim(group_scales, col, quarter, 1)
        values = (codes - 8).astype(F32).reshape(groups, features // groups, quarter)
        quant = (values * scales[:, None, :]).reshape(features, quarter).astype(BF16)
        return jnp.where(kind == 0, plain, quant)

    send = weight(yh ^ core, (1 - yl) * half + core * quarter)
    pairs = []
    for a in range(2):
        for c in range(2):
            for b in range(2):
                pairs.append((a * 4 + c * 2 + b, (a ^ c) * 4 + c * 2 + (1 - b)))
    got = lax.ppermute(send, ("yh", "core", "yl"), pairs)
    col, send = lax.optimization_barrier((yl * half + core * quarter, send))
    own = weight(yh, col)

    payload = pack(z, attn_float, attn_quant)
    rows = jnp.concatenate([own, got], axis=0)
    payload, rows = lax.optimization_barrier((payload, rows))
    parts = [rows] + [ahead(rows, "z", j) for j in (1, 2, 3)]

    acts = lax.all_to_all(payload, PLANE, 0, 0, tiled=True).reshape(16 * tokens, -1)
    there = tick(acts)
    there, *parts = lax.optimization_barrier((there, *parts))
    others = [swap(p, "core") for p in parts]

    def output(p):
        return lax.all_to_all(p.reshape(16, tokens, quarter), PLANE, 0, 0, tiled=True)

    first = project(acts, parts, ())
    result1 = output(first)

    blocks = stats(acts, first)
    total = blocks[0]
    for j in (1, 2, 3):
        total = total + ahead(blocks[j], "z", 4 - j).astype(F32)
    second = project(acts, others, (total,))
    total = (total + swap(total, "core")) * inverse
    here, there = total[:features].astype(BF16), total[features:].astype(BF16)
    moved = (
        swap(there, "yl"),
        swap(here, "yh"),
        lax.ppermute(there, ("yh", "yl"), [(i, 3 - i) for i in range(4)]),
    )
    at = jnp.stack([core, yh, yl])
    at, second, total, *moved = lax.optimization_barrier((at, second, total, *moved))
    result2 = output(second)
    return finish(at, result1, result2, total, moved)


def solution(mesh):
    fine = Mesh(mesh.devices.reshape(2, 2, 2, 4, 4), FINE)
    rows, tok = P(FINE, None), P(("yl", "z", "x"), None)
    return jax.shard_map(
        shards,
        mesh=fine,
        in_specs=(rows, rows, tok, tok, tok),
        out_specs=(rows, rows, tok, tok),
        check_vma=False,
    )
```

```python
import jax
import jax.numpy as jnp
from jax import lax
from jax.experimental import pallas as pl
from jax.experimental.pallas import tpu as pltpu
from jax.sharding import Mesh
from jax.sharding import PartitionSpec as P

BLOCK = 128
FINE = ("yh", "core", "yl", "z", "x")
PLANE = ("yh", "yl", "x")
F32 = jnp.float32
BF16 = jnp.bfloat16


WHOLE = pl.BlockSpec(memory_space=pltpu.VMEM)
LEFT = pl.BlockSpec(memory_space=pl.ANY)
SCALAR = pl.BlockSpec(memory_space=pltpu.SMEM)


def params():
    return pltpu.CompilerParams(vmem_limit_bytes=12 << 20)


def pack_kernel(z_ref, float_ref, quant_ref, out_ref):
    width = float_ref.shape[1] // 32
    z = z_ref[0]
    for kind, ref in enumerate((float_ref, quant_ref)):
        for j in range(4):
            zj = lax.rem(z + j, 4)
            for yl in range(2):
                for x in range(4):
                    start = pl.multiple_of(((yl * 4 + zj) * 4 + x) * width, width)
                    block = ref[:, pl.ds(start, width)]
                    for half in range(2):
                        at = (j * 2 + (yl ^ half)) * width
                        out_ref[kind * 8 + half * 4 + x, :, at : at + width] = block
    quant = quant_ref[:, :BLOCK]
    shift = (float_ref[:, :BLOCK].astype(F32) - quant.astype(F32)).astype(BF16)
    for d in range(16):
        out_ref[d, :, 8 * width :] = shift if d // 4 % 2 else quant


def pack(z, attn_float, attn_quant):
    tokens, d_in = attn_float.shape
    return pl.pallas_call(
        pack_kernel,
        out_shape=jax.ShapeDtypeStruct((16, tokens, d_in // 4 + BLOCK), BF16),
        in_specs=[SCALAR, WHOLE, WHOLE],
        out_specs=WHOLE,
        compiler_params=params(),
        name="pack",
    )(z.reshape(1), attn_float, attn_quant)


def project_kernel(acts_ref, *refs):
    weights, out_ref = refs[:4], refs[-1]
    depth, width = weights[0].shape
    tile = 512
    for col in range(0, width, tile):
        total = None
        for j, ref in enumerate(weights):
            term = jnp.dot(
                acts_ref[:, j * depth : (j + 1) * depth],
                ref[:, col : col + tile],
                preferred_element_type=F32,
            )
            total = term if total is None else total + term
        out_ref[:, col : col + tile] = total.astype(BF16)


def project(acts, weights, after):
    rows, cols = acts.shape[0], weights[0].shape[1]
    step = 256
    return pl.pallas_call(
        project_kernel,
        out_shape=jax.ShapeDtypeStruct((rows, cols), BF16),
        grid=(rows // step,),
        in_specs=[pl.BlockSpec((step, acts.shape[1]), lambda i: (i, 0))] + [WHOLE] * len(weights)
        + [LEFT] * len(after),
        out_specs=pl.BlockSpec((step, cols), lambda i: (i, 0)),
        compiler_params=params(),
        cost_estimate=pl.CostEstimate(
            flops=2 * rows * 2048 * cols, bytes_accessed=12 << 20, transcendentals=0
        ),
        name="project",
    )(acts, *weights, *after)


def finish_kernel(at_ref, first_ref, second_ref, total_ref, *refs):
    (side_ref, down_ref, cross_ref), outs = refs[:3], refs[3:]
    core, yh, yl = at_ref[0], at_ref[1], at_ref[2]
    width = first_ref.shape[2]
    for q, ref in enumerate((first_ref, second_ref)):
        quarter = core if q == 0 else 1 - core
        for kind, out in enumerate(outs[:2]):
            for half in range(2):
                at = kind * 8 + half * 4
                total = ref[at].astype(F32)
                for x in range(1, 4):
                    total += ref[at + x].astype(F32)
                start = pl.multiple_of((half * 2 + quarter) * width, width)
                out[:, pl.ds(start, width)] = total.astype(BF16)
    rows = outs[2].shape[0]
    own = jnp.where(yh == 1, total_ref[:rows], down_ref[...].astype(F32))
    other = jnp.where(yh == 1, side_ref[...].astype(F32), cross_ref[...].astype(F32))
    outs[2][...] = jnp.where(yl == 0, own, other)
    outs[3][...] = jnp.where(yl == 0, other, own)


def finish(at, first, second, total, moved):
    tokens, cols = first.shape[1:]
    rows = total.shape[0] // 2
    return pl.pallas_call(
        finish_kernel,
        out_shape=(jax.ShapeDtypeStruct((tokens, 4 * cols), BF16),) * 2
        + (jax.ShapeDtypeStruct((rows, BLOCK), F32),) * 2,
        in_specs=[SCALAR] + [WHOLE] * (3 + len(moved)),
        out_specs=(WHOLE,) * 4,
        compiler_params=params(),
        name="finish",
    )(at, first, second, total, *moved)


def stats_kernel(acts_ref, after_ref, *outs):
    width = outs[0].shape[0]
    for j, out in enumerate(outs):
        out[...] = lax.dot_general(
            acts_ref[:, j * width : (j + 1) * width],
            acts_ref[:, 4 * width :],
            (((0,), (0,)), ((), ())),
            preferred_element_type=F32,
        ).astype(out.dtype)


def stats(acts, after):
    width = (acts.shape[1] - BLOCK) // 4
    return pl.pallas_call(
        stats_kernel,
        out_shape=(jax.ShapeDtypeStruct((width, BLOCK), F32),)
        + (jax.ShapeDtypeStruct((width, BLOCK), BF16),) * 3,
        in_specs=[WHOLE, LEFT],
        out_specs=(WHOLE,) * 4,
        compiler_params=params(),
        name="stats",
    )(acts, after)


def tick_kernel(acts_ref, out_ref):
    out_ref[...] = jnp.zeros_like(out_ref)


def tick(acts):
    return pl.pallas_call(
        tick_kernel,
        out_shape=jax.ShapeDtypeStruct((8, 128), F32),
        in_specs=[LEFT],
        out_specs=WHOLE,
        compiler_params=params(),
        name="tick",
    )(acts)


def swap(a, axis):
    return lax.ppermute(a, axis, [(0, 1), (1, 0)])


def ahead(a, axis, j):
    return lax.ppermute(a, axis, [((i + j) % 4, i) for i in range(4)])


def shards(attn_float, attn_quant, proj_weight, weight_codes, group_scales):
    tokens, d_in = attn_float.shape
    features, d_out = proj_weight.shape
    groups = group_scales.shape[0]
    half, quarter = d_out // 2, d_out // 4
    inverse = 1.0 / (tokens * 128)
    yh, core, yl, z = (lax.axis_index(a) for a in ("yh", "core", "yl", "z"))

    def weight(kind, col):
        plain = lax.dynamic_slice_in_dim(proj_weight, col, quarter, 1)
        codes = lax.dynamic_slice_in_dim(weight_codes, col, quarter, 1)
        scales = lax.dynamic_slice_in_dim(group_scales, col, quarter, 1)
        values = (codes - 8).astype(F32).reshape(groups, features // groups, quarter)
        quant = (values * scales[:, None, :]).reshape(features, quarter).astype(BF16)
        return jnp.where(kind == 0, plain, quant)

    send = weight(yh ^ core, (1 - yl) * half + core * quarter)
    pairs = []
    for a in range(2):
        for c in range(2):
            for b in range(2):
                pairs.append((a * 4 + c * 2 + b, (a ^ c) * 4 + c * 2 + (1 - b)))
    got = lax.ppermute(send, ("yh", "core", "yl"), pairs)
    col, send = lax.optimization_barrier((yl * half + core * quarter, send))
    own = weight(yh, col)

    payload = pack(z, attn_float, attn_quant)
    rows = jnp.concatenate([own, got], axis=0)
    payload, rows = lax.optimization_barrier((payload, rows))
    parts = [rows] + [ahead(rows, "z", j) for j in (1, 2, 3)]

    acts = lax.all_to_all(payload, PLANE, 0, 0, tiled=True).reshape(16 * tokens, -1)
    there = tick(acts)
    there, *parts = lax.optimization_barrier((there, *parts))
    others = [swap(p, "core") for p in parts]

    def output(p):
        return lax.all_to_all(p.reshape(16, tokens, quarter), PLANE, 0, 0, tiled=True)

    first = project(acts, parts, ())
    result1 = output(first)

    blocks = stats(acts, first)
    total = blocks[0]
    came = [ahead(blocks[j], "z", 4 - j) for j in (1, 2, 3)]
    second = project(acts, others, (blocks[0],))
    second, *came = lax.optimization_barrier((second, *came))
    for block in came:
        total = total + block.astype(F32)
    total = (total + swap(total, "core")) * inverse
    here, there = total[:features].astype(BF16), total[features:].astype(BF16)
    moved = (
        swap(there, "yl"),
        swap(here, "yh"),
        lax.ppermute(there, ("yh", "yl"), [(i, 3 - i) for i in range(4)]),
    )
    at = jnp.stack([core, yh, yl])
    at, second, total, *moved = lax.optimization_barrier((at, second, total, *moved))
    result2 = output(second)
    return finish(at, result1, result2, total, moved)


def solution(mesh):
    fine = Mesh(mesh.devices.reshape(2, 2, 2, 4, 4), FINE)
    rows, tok = P(FINE, None), P(("yl", "z", "x"), None)
    return jax.shard_map(
        shards,
        mesh=fine,
        in_specs=(rows, rows, tok, tok, tok),
        out_specs=(rows, rows, tok, tok),
        check_vma=False,
    )
```

```python
import jax
import jax.numpy as jnp
from jax import lax
from jax.experimental import pallas as pl
from jax.experimental.pallas import tpu as pltpu
from jax.sharding import Mesh
from jax.sharding import PartitionSpec as P

BLOCK = 128
FINE = ("yh", "core", "yl", "z", "x")
PLANE = ("yh", "yl", "x")
F32 = jnp.float32
BF16 = jnp.bfloat16


WHOLE = pl.BlockSpec(memory_space=pltpu.VMEM)
LEFT = pl.BlockSpec(memory_space=pl.ANY)
SCALAR = pl.BlockSpec(memory_space=pltpu.SMEM)


def params():
    return pltpu.CompilerParams(vmem_limit_bytes=16 << 20)


def pack_kernel(z_ref, float_ref, quant_ref, out_ref):
    width = float_ref.shape[1] // 32
    z = z_ref[0]
    for kind, ref in enumerate((float_ref, quant_ref)):
        for j in range(4):
            zj = lax.rem(z + j, 4)
            for yl in range(2):
                for x in range(4):
                    start = pl.multiple_of(((yl * 4 + zj) * 4 + x) * width, width)
                    block = ref[:, pl.ds(start, width)]
                    for half in range(2):
                        at = (j * 2 + (yl ^ half)) * width
                        out_ref[kind * 8 + half * 4 + x, :, at : at + width] = block
    quant = quant_ref[:, :BLOCK]
    shift = (float_ref[:, :BLOCK].astype(F32) - quant.astype(F32)).astype(BF16)
    for d in range(16):
        out_ref[d, :, 8 * width :] = shift if d // 4 % 2 else quant


def pack(z, attn_float, attn_quant):
    tokens, d_in = attn_float.shape
    return pl.pallas_call(
        pack_kernel,
        out_shape=jax.ShapeDtypeStruct((16, tokens, d_in // 4 + BLOCK), BF16),
        in_specs=[SCALAR, WHOLE, WHOLE],
        out_specs=WHOLE,
        compiler_params=params(),
        name="pack",
    )(z.reshape(1), attn_float, attn_quant)


def project_kernel(acts_ref, *refs):
    weights, out_ref = refs[:4], refs[-1]
    depth, width = weights[0].shape
    tile = 512
    for col in range(0, width, tile):
        total = None
        for j, ref in enumerate(weights):
            term = jnp.dot(
                acts_ref[:, j * depth : (j + 1) * depth],
                ref[:, col : col + tile],
                preferred_element_type=F32,
            )
            total = term if total is None else total + term
        out_ref[:, col : col + tile] = total.astype(BF16)


def project(acts, weights, after):
    rows, cols = acts.shape[0], weights[0].shape[1]
    step = 512
    return pl.pallas_call(
        project_kernel,
        out_shape=jax.ShapeDtypeStruct((rows, cols), BF16),
        grid=(rows // step,),
        in_specs=[pl.BlockSpec((step, acts.shape[1]), lambda i: (i, 0))] + [WHOLE] * len(weights)
        + [LEFT] * len(after),
        out_specs=pl.BlockSpec((step, cols), lambda i: (i, 0)),
        compiler_params=params(),
        cost_estimate=pl.CostEstimate(
            flops=2 * rows * 2048 * cols, bytes_accessed=12 << 20, transcendentals=0
        ),
        name="project",
    )(acts, *weights, *after)


def finish_kernel(at_ref, first_ref, second_ref, total_ref, *refs):
    (side_ref, down_ref, cross_ref), outs = refs[:3], refs[3:]
    core, yh, yl = at_ref[0], at_ref[1], at_ref[2]
    width = first_ref.shape[2]
    for q, ref in enumerate((first_ref, second_ref)):
        quarter = core if q == 0 else 1 - core
        for kind, out in enumerate(outs[:2]):
            for half in range(2):
                at = kind * 8 + half * 4
                total = ref[at].astype(F32)
                for x in range(1, 4):
                    total += ref[at + x].astype(F32)
                start = pl.multiple_of((half * 2 + quarter) * width, width)
                out[:, pl.ds(start, width)] = total.astype(BF16)
    rows = outs[2].shape[0]
    own = jnp.where(yh == 1, total_ref[:rows], down_ref[...].astype(F32))
    other = jnp.where(yh == 1, side_ref[...].astype(F32), cross_ref[...].astype(F32))
    outs[2][...] = jnp.where(yl == 0, own, other)
    outs[3][...] = jnp.where(yl == 0, other, own)


def finish(at, first, second, total, moved):
    tokens, cols = first.shape[1:]
    rows = total.shape[0] // 2
    return pl.pallas_call(
        finish_kernel,
        out_shape=(jax.ShapeDtypeStruct((tokens, 4 * cols), BF16),) * 2
        + (jax.ShapeDtypeStruct((rows, BLOCK), F32),) * 2,
        in_specs=[SCALAR] + [WHOLE] * (3 + len(moved)),
        out_specs=(WHOLE,) * 4,
        compiler_params=params(),
        name="finish",
    )(at, first, second, total, *moved)


def stats_kernel(acts_ref, after_ref, *outs):
    width = outs[0].shape[0]
    for j, out in enumerate(outs):
        out[...] = lax.dot_general(
            acts_ref[:, j * width : (j + 1) * width],
            acts_ref[:, 4 * width :],
            (((0,), (0,)), ((), ())),
            preferred_element_type=F32,
        ).astype(out.dtype)


def stats(acts, after):
    width = (acts.shape[1] - BLOCK) // 4
    return pl.pallas_call(
        stats_kernel,
        out_shape=(jax.ShapeDtypeStruct((width, BLOCK), F32),)
        + (jax.ShapeDtypeStruct((width, BLOCK), BF16),) * 3,
        in_specs=[WHOLE, LEFT],
        out_specs=(WHOLE,) * 4,
        compiler_params=params(),
        name="stats",
    )(acts, after)


def tick_kernel(acts_ref, out_ref):
    out_ref[...] = jnp.zeros_like(out_ref)


def tick(acts):
    return pl.pallas_call(
        tick_kernel,
        out_shape=jax.ShapeDtypeStruct((8, 128), F32),
        in_specs=[LEFT],
        out_specs=WHOLE,
        compiler_params=params(),
        name="tick",
    )(acts)


def swap(a, axis):
    return lax.ppermute(a, axis, [(0, 1), (1, 0)])


def ahead(a, axis, j):
    return lax.ppermute(a, axis, [((i + j) % 4, i) for i in range(4)])


def shards(attn_float, attn_quant, proj_weight, weight_codes, group_scales):
    tokens, d_in = attn_float.shape
    features, d_out = proj_weight.shape
    groups = group_scales.shape[0]
    half, quarter = d_out // 2, d_out // 4
    inverse = 1.0 / (tokens * 128)
    yh, core, yl, z = (lax.axis_index(a) for a in ("yh", "core", "yl", "z"))

    def weight(kind, col):
        plain = lax.dynamic_slice_in_dim(proj_weight, col, quarter, 1)
        codes = lax.dynamic_slice_in_dim(weight_codes, col, quarter, 1)
        scales = lax.dynamic_slice_in_dim(group_scales, col, quarter, 1)
        values = (codes - 8).astype(F32).reshape(groups, features // groups, quarter)
        quant = (values * scales[:, None, :]).reshape(features, quarter).astype(BF16)
        return jnp.where(kind == 0, plain, quant)

    send = weight(yh ^ core, (1 - yl) * half + core * quarter)
    pairs = []
    for a in range(2):
        for c in range(2):
            for b in range(2):
                pairs.append((a * 4 + c * 2 + b, (a ^ c) * 4 + c * 2 + (1 - b)))
    got = lax.ppermute(send, ("yh", "core", "yl"), pairs)
    col, send = lax.optimization_barrier((yl * half + core * quarter, send))
    own = weight(yh, col)

    payload = pack(z, attn_float, attn_quant)
    rows = jnp.concatenate([own, got], axis=0)
    payload, rows = lax.optimization_barrier((payload, rows))
    parts = [rows] + [ahead(rows, "z", j) for j in (1, 2, 3)]

    acts = lax.all_to_all(payload, PLANE, 0, 0, tiled=True).reshape(16 * tokens, -1)
    there = tick(acts)
    there, *parts = lax.optimization_barrier((there, *parts))
    others = [swap(p, "core") for p in parts]

    def output(p):
        return lax.all_to_all(p.reshape(16, tokens, quarter), PLANE, 0, 0, tiled=True)

    first = project(acts, parts, ())
    result1 = output(first)

    blocks = stats(acts, first)
    total = blocks[0]
    came = [ahead(blocks[j], "z", 4 - j) for j in (1, 2, 3)]
    second = project(acts, others, (blocks[0],))
    second, *came = lax.optimization_barrier((second, *came))
    for block in came:
        total = total + block.astype(F32)
    total = (total + swap(total, "core")) * inverse
    here, there = total[:features].astype(BF16), total[features:].astype(BF16)
    moved = (
        swap(there, "yl"),
        swap(here, "yh"),
        lax.ppermute(there, ("yh", "yl"), [(i, 3 - i) for i in range(4)]),
    )
    at = jnp.stack([core, yh, yl])
    at, second, total, *moved = lax.optimization_barrier((at, second, total, *moved))
    result2 = output(second)
    return finish(at, result1, result2, total, moved)


def solution(mesh):
    fine = Mesh(mesh.devices.reshape(2, 2, 2, 4, 4), FINE)
    rows, tok = P(FINE, None), P(("yl", "z", "x"), None)
    return jax.shard_map(
        shards,
        mesh=fine,
        in_specs=(rows, rows, tok, tok, tok),
        out_specs=(rows, rows, tok, tok),
        check_vma=False,
    )
```
